32 devices in a mesh: dp: 16 (over z, y, x), mp: 2 (over core).
Axes of the slice: x: 2, y: 2, z: 4, core: 2. Of those that a mesh axis runs over, the one named last changes fastest.
Arguments:
- items: int32 [2, 8, 1024], P(None, None, 'dp'), may hold values from 0 to 18815
- targets: int32 [2, 8, 1024], P(None, None, 'dp'), may hold values from 0 to 18815
- masks: int32 [2, 8, 1024], P(None, None, 'dp'), may hold values from 0 to 2, as said below
- plan: int32 [1, 1024], P(None, 'dp'), may hold values from 0 to 1023, as said below
- negatives: int32 [2, 2048], replicated, may hold values from 0 to 18815, as said below
- h_init: float32 [1024, 1000], P('dp', 'mp'), may hold values from -0.9 to 0.9
- emb: bfloat16 [18816, 1000], P('dp', 'mp'), may hold values from -6 to 6
- w_in: bfloat16 [1000, 3, 1000], P(None, None, 'mp'), may hold values from -0.1875 to 0.1875
- w_rec: bfloat16 [1000, 3, 1000], P(None, None, 'mp'), may hold values from -0.1875 to 0.1875
- b_in: float32 [3, 1000], P(None, 'mp'), may hold values from -4 to 7
- b_rec_n: float32 [1000], P('mp'), may hold values from -2.5 to 2.5
- out_table: bfloat16 [18816, 1000], P('dp', 'mp'), may hold values from -0.59765625 to 0.59765625
- out_bias: float32 [18816], P('dp'), may hold values from -3 to 3
Outputs:
- loss: float32 [], replicated
- rms_inputs: float32 [], replicated
- rms_hidden: float32 [], replicated
- rms_scores: float32 [], replicated
- final_state: float32 [1024, 1000], P('dp', 'mp')
- grad_init: float32 [1024, 1000], P('dp', 'mp')
- grad_emb: float32 [18816, 1000], P('dp', 'mp')
- grad_w_in: float32 [1000, 3, 1000], P(None, None, 'mp')
- grad_w_rec: float32 [1000, 3, 1000], P(None, None, 'mp')
- grad_b_in: float32 [3, 1000], P(None, 'mp')
- grad_b_rec_n: float32 [1000], P('mp')
- grad_out_table: float32 [18816, 1000], P('dp', 'mp')
- grad_out_bias: float32 [18816], P('dp')
The draws below stay inside these ranges and needn't reach their ends.
Inputs may be any that keep to these rules, and one draw needn't show every extreme that they name: `masks`: code 2 marks a session's first event, 1 an event continuing the slot's state, 0 an empty step; the last slot is never empty, and slots with higher numbers are empty less often. Each row plan[b] is a bijection of the 1024 slots. Slot k of every device goes to the device a common offset ahead (offsets of slots k and k + 16 agree), and into a local slot given by one permutation of the 64 local slots that all devices share, so one device hands at most 4 slots to any one device, and exactly 4 to some. The offsets 1 and 8 are always among those used. `negatives`: the ids of one row are distinct.
All inputs are finite; a program needn't handle non-finite values.
Results may differ from the reference program's by a relative error of at most 0.017.
Values may be sent and summed in bfloat16 or wider, within the bound.
No kernel may reach another device: no remote copies, remote signals or barrier semaphores. Data moves between devices by JAX's collectives and lax.ppermute only.
A program may use at most 320 MiB of HBM per device.

```python
import math
import jax
import jax.numpy as jnp
import numpy as np
from jax import lax

HIDDEN_SIZE = 1000
VOCAB = 18816
NEGS = 2048
STEPS = 8
BLOCKS = 2
SLOTS = 64
ALL_SLOTS = 1024
N_DP = 16


def draw_negatives(key, part):
    key = jax.random.fold_in(key, 11)
    keys = jax.random.split(key, BLOCKS)
    picked = jax.vmap(lambda single: jax.random.permutation(single, VOCAB)[:NEGS])(keys)
    return picked.astype(jnp.int32)


def draw_plan(key, part):
    key = jax.random.fold_in(key, 12)
    keys = jax.random.split(key, BLOCKS - 1)
    used = min(SLOTS, N_DP)

    def one_boundary(single):
        first_key, second_key, third_key = jax.random.split(single, 3)
        ranks = jax.random.permutation(first_key, N_DP).astype(jnp.int32)
        values = jnp.arange(N_DP, dtype=jnp.int32)
        ranks = jnp.where(values == 1, -2, ranks)
        ranks = jnp.where(values == N_DP // 2, -1, ranks)
        ordered = jnp.argsort(ranks, stable=True).astype(jnp.int32)
        head = ordered[:used][jax.random.permutation(third_key, used)]
        offsets = jnp.concatenate([head, ordered[used:]])
        places = jax.random.permutation(second_key, SLOTS)
        slot_index = jnp.arange(SLOTS)
        device_index = jnp.arange(N_DP)
        target = (device_index[:, None] + offsets[slot_index % N_DP][None, :]) % N_DP
        return (target * SLOTS + places[None, :]).reshape(N_DP * SLOTS).astype(jnp.int32)
    return jax.vmap(one_boundary)(keys)


def draw_masks(key, part):
    key = jax.random.fold_in(key, 13)
    first_key, second_key = jax.random.split(key)
    total = N_DP * SLOTS
    level = jax.random.randint(first_key, (BLOCKS, STEPS, total), 0, 1000)
    begins = jax.random.randint(second_key, (BLOCKS, STEPS, total), 0, 100)
    barrier = 700 + 300 * jnp.arange(total) // max(total - 1, 1)
    living = (level < barrier[None, None, :]).astype(jnp.int32)
    return (living * (1 + (begins < 4).astype(jnp.int32))).astype(jnp.int32)


def draw_b_in(key, part):
    key = jax.random.fold_in(key, 14)
    first_key, second_key = jax.random.split(key)
    base = jnp.clip(jax.random.normal(first_key, (3, HIDDEN_SIZE), jnp.float32), -4.0, 4.0)
    slow = jax.random.randint(second_key, (HIDDEN_SIZE,), 0, 2).astype(jnp.float32)
    lift = jnp.zeros((3, HIDDEN_SIZE), jnp.float32).at[0].set(3.0 * slow)
    return base + lift


def plant(array, rng, low, high):
    extent = array.shape
    place = [jax.random.randint(jax.random.fold_in(rng, axis), (), 0, extent[axis]) for axis in range(len(extent))]
    array = array.at[tuple(place)].set(low)
    longest = extent.index(max(extent))
    place[longest] = (place[longest] + 1) % extent[longest]
    return array.at[tuple(place)].set(high)


def block_levels(stream_key, dims, cuts, least, top_value):
    loudness, own = 1.0, jax.random.fold_in(stream_key, 6)
    for dim, blocks in cuts:
        draws = jnp.exp(jax.random.uniform(jax.random.fold_in(own, dim), (blocks,), jnp.float32, least / len(cuts), top_value / len(cuts)))
        loudness = loudness * jnp.repeat(draws, dims[dim] // blocks).reshape([-1 if axis == dim else 1 for axis in range(len(dims))])
    return loudness


def rank_table(amount, slope):
    portions = [(1 << 20) // math.isqrt(standing ** slope) + 1 for standing in range(1, amount + 1)]
    deviation = 1 + sum(portions) // (1 << 30)
    return np.cumsum(np.array([max(1, weight // deviation) for weight in portions]))


def ranked(key, dims, count, lean):
    grid = rank_table(count, lean)
    pick = jax.random.randint(jax.random.fold_in(key, 1), dims, 0, int(grid[count - 1]))
    grade = jnp.searchsorted(jnp.asarray(grid, jnp.int32), pick, side="right")
    return jax.random.permutation(jax.random.fold_in(key, 2), count)[grade].astype(jnp.int32)


def centred(rng, extent, deviation, bound, cuts=(), kind=jnp.bfloat16):
    drawn = deviation * jax.random.normal(rng, extent, jnp.float32)
    if cuts:
        drawn = drawn * block_levels(rng, extent, cuts, -0.22, 0.18)
    return jnp.clip(drawn, -bound, bound).astype(kind)


def setup_inputs(seed: int = 0) -> dict:
    key_of = jax.random.split(jax.random.key(seed), 14)
    items = plant(ranked(key_of[0], (BLOCKS, STEPS, ALL_SLOTS), VOCAB, 2), jax.random.fold_in(key_of[0], 3), 0, VOCAB - 1).astype(jnp.int32)
    targets = plant(ranked(key_of[1], (BLOCKS, STEPS, ALL_SLOTS), VOCAB, 2), jax.random.fold_in(key_of[1], 3), 0, VOCAB - 1).astype(jnp.int32)
    masks = draw_masks(jax.random.fold_in(key_of[13], 71), 0)
    plan = draw_plan(jax.random.fold_in(key_of[13], 71), 0)
    negatives = draw_negatives(jax.random.fold_in(key_of[13], 71), 0)
    h_init = jnp.clip(jax.random.uniform(key_of[5], (ALL_SLOTS, HIDDEN_SIZE), jnp.float32, -0.9, 0.9) * block_levels(key_of[5], (ALL_SLOTS, HIDDEN_SIZE), ((0, 16), (1, 2)), -0.4, 0.0), -0.9, 0.9)
    emb = centred(key_of[6], (VOCAB, HIDDEN_SIZE), 1.0, 6.0, ((0, 16), (1, 2)))
    w_in = centred(key_of[7], (HIDDEN_SIZE, 3, HIDDEN_SIZE), HIDDEN_SIZE ** -0.5, 0.1875, ((2, 2),))
    w_rec = centred(key_of[8], (HIDDEN_SIZE, 3, HIDDEN_SIZE), HIDDEN_SIZE ** -0.5, 0.1875, ((2, 2),))
    b_in = draw_b_in(jax.random.fold_in(key_of[13], 71), 0)
    b_rec_n = centred(key_of[10], (HIDDEN_SIZE,), 0.5, 2.5, ((0, 2),), jnp.float32)
    out_table = centred(key_of[11], (VOCAB, HIDDEN_SIZE), 0.1, 0.59765625, ((0, 16), (1, 2)))
    out_bias = centred(key_of[12], (VOCAB,), 0.5, 3.0, ((0, 16),), jnp.float32)
    return {"items": items, "targets": targets, "masks": masks, "plan": plan, "negatives": negatives, "h_init": h_init, "emb": emb, "w_in": w_in, "w_rec": w_rec, "b_in": b_in, "b_rec_n": b_rec_n, "out_table": out_table, "out_bias": out_bias}


REGULAR = 1.0
NEGATIVE_FLOOR = -1e+30

@jax.custom_vjp
def low(v):
    return lax.optimization_barrier(v.astype(jnp.bfloat16)).astype(jnp.float32)

@jax.custom_vjp
def low_back(v):
    return v

def low_keep(v):
    return (low(v), None)

def low_pass(kept, grad):
    return (grad,)

def back_keep(v):
    return (v, None)

def back_low(kept, grad):
    return (low(grad),)
low.defvjp(low_keep, low_pass)
low_back.defvjp(back_keep, back_low)

def bpr_rows(scores, wanted, chosen, usable):
    session_events = scores.shape[0]
    allowed = usable[None, :] & (chosen[None, :] != wanted[:, None])
    positive = jnp.diagonal(scores[:, :session_events])
    top_score = lax.optimization_barrier(jnp.max(jnp.where(allowed, scores, NEGATIVE_FLOOR), axis=1, keepdims=True))
    weights = jnp.exp(jnp.where(allowed, scores - top_score, NEGATIVE_FLOOR))
    normal = lax.optimization_barrier(jnp.sum(weights, axis=1, keepdims=True))
    joined = scores + jax.nn.log_sigmoid(positive[:, None] - scores)
    top_joined = lax.optimization_barrier(jnp.max(jnp.where(allowed, joined, NEGATIVE_FLOOR), axis=1, keepdims=True))
    joined_sum = lax.optimization_barrier(jnp.sum(jnp.exp(jnp.where(allowed, joined - top_joined, NEGATIVE_FLOOR)), axis=1, keepdims=True))
    ranking = top_score + jnp.log(normal) - top_joined - jnp.log(joined_sum)
    penalty = lax.optimization_barrier(jnp.sum(weights / normal * scores * scores, axis=1))
    return ranking[:, 0] + REGULAR * penalty

def gru_cell(gates_in, recurrent, prior, bias_cand, active_sessions):
    update = jax.nn.sigmoid(gates_in[:, 0] + recurrent[:, 0])
    reset = jax.nn.sigmoid(gates_in[:, 1] + recurrent[:, 1])
    candidate = jnp.tanh(gates_in[:, 2] + reset * (recurrent[:, 2] + bias_cand))
    return active_sessions * ((1.0 - update) * candidate + update * prior)

def reference(items, targets, masks, plan, negatives, h_init, emb, w_in, w_rec, b_in, b_rec_n, out_table, out_bias):
    highest = lax.Precision.HIGHEST
    session_events = STEPS * SLOTS
    active_all = (masks > 0).astype(jnp.float32)
    total_events = jnp.sum(active_all)

    def forward(emb_full, w_in_full, w_rec_full, b_in_full, b_cand_full, table_full, bias_full, state_init):
        embedded = low_back(emb_full[items])
        preacts = low_back(jnp.einsum('blgh,hkm->blgkm', embedded, w_in_full, precision=highest)) + b_in_full
        state = state_init
        state_low = low(state_init)
        outputs_all = []
        for event_block in range(BLOCKS):

            def advance(carry_pair, step_inputs):
                prior, prior_low = carry_pair
                gates_in, codes = step_inputs
                keeping = (codes == 1).astype(jnp.float32)[:, None]
                active_sessions = (codes > 0).astype(jnp.float32)[:, None]
                entering = prior_low * keeping
                recurrent = low_back(jnp.einsum('gh,hkm->gkm', entering, w_rec_full, precision=highest))
                fresh = gru_cell(gates_in, recurrent, prior * keeping, b_cand_full, active_sessions)
                fresh_low = low(fresh)
                return ((fresh, fresh_low), fresh_low)
            (state, state_low), outputs = lax.scan(advance, (state, state_low), (preacts[event_block], masks[event_block]))
            outputs_all.append(outputs)
            if event_block + 1 < BLOCKS:
                state = jnp.zeros_like(state).at[plan[event_block]].set(state)
                state_low = jnp.zeros_like(state_low).at[plan[event_block]].set(state_low)
        loss_total_sum = jnp.zeros((), jnp.float32)
        score_squared = jnp.zeros((), jnp.float32)
        hidden_squared = jnp.zeros((), jnp.float32)
        for event_block in range(BLOCKS):
            outputs = outputs_all[event_block]
            hidden_squared = hidden_squared + jnp.sum(active_all[event_block][:, :, None] * outputs * outputs)
            per_device = outputs.reshape(STEPS, N_DP, SLOTS, HIDDEN_SIZE).transpose(1, 0, 2, 3).reshape(N_DP, session_events, HIDDEN_SIZE)
            wanted_all = targets[event_block].reshape(STEPS, N_DP, SLOTS).transpose(1, 0, 2).reshape(N_DP, session_events)
            active_dev = active_all[event_block].reshape(STEPS, N_DP, SLOTS).transpose(1, 0, 2).reshape(N_DP, session_events)
            shared = negatives[event_block]

            def device_scores(packed):
                rows_low, wanted, active_sessions = packed
                chosen = jnp.concatenate([wanted, shared]).astype(jnp.int32)
                product = jnp.dot(rows_low, table_full[chosen].T, precision=highest, preferred_element_type=jnp.float32)
                scores = low_back(product) + bias_full[chosen]
                usable = jnp.concatenate([active_sessions > 0, jnp.ones((NEGS,), dtype=bool)])
                losses = bpr_rows(scores, wanted, chosen, usable)
                return (jnp.sum(active_sessions * losses), jnp.sum(active_sessions * lax.optimization_barrier(jnp.sum(scores * scores, axis=1))))
            losses, squares = lax.map(jax.checkpoint(device_scores), (per_device, wanted_all, active_dev))
            loss_total_sum = loss_total_sum + jnp.sum(losses)
            score_squared = score_squared + jnp.sum(squares)
        input_squared = jnp.sum(active_all[:, :, :, None] * embedded * embedded)
        return (loss_total_sum / total_events, (input_squared, hidden_squared, score_squared, state))
    arguments = (emb.astype(jnp.float32), w_in.astype(jnp.float32), w_rec.astype(jnp.float32), b_in, b_rec_n, out_table.astype(jnp.float32), out_bias, h_init)
    loss, pullback, extras = jax.vjp(forward, *arguments, has_aux=True)
    grads = pullback(jnp.ones((), jnp.float32))
    input_squared, hidden_squared, score_squared, final_state = extras
    rms_inputs = jnp.sqrt(input_squared / (total_events * HIDDEN_SIZE))
    rms_hidden = jnp.sqrt(hidden_squared / (total_events * HIDDEN_SIZE))
    rms_scores = jnp.sqrt(score_squared / (total_events * (session_events + NEGS)))
    return (loss, rms_inputs, rms_hidden, rms_scores, final_state, grads[7], grads[0], grads[1], grads[2], grads[3], grads[4], grads[5], grads[6])
```

```python
import functools
import math

import jax
import jax.numpy as jnp
from jax import lax
from jax.experimental import pallas as pl
from jax.experimental.pallas import tpu as pltpu
from jax.sharding import PartitionSpec as P

REGULAR = 1.0
NEGATIVE_FLOOR = -1e30
VMEM_LIMIT = 56 * 1024 * 1024


def bpr_rows(scores, wanted, chosen, usable):
    session_events = scores.shape[0]
    allowed = usable[None, :] & (chosen[None, :] != wanted[:, None])
    positive = jnp.diagonal(scores[:, :session_events])
    top_score = jnp.max(jnp.where(allowed, scores, NEGATIVE_FLOOR), axis=1, keepdims=True)
    weights = jnp.exp(jnp.where(allowed, scores - top_score, NEGATIVE_FLOOR))
    normal = jnp.sum(weights, axis=1, keepdims=True)
    joined = scores + jax.nn.log_sigmoid(positive[:, None] - scores)
    top_joined = jnp.max(jnp.where(allowed, joined, NEGATIVE_FLOOR), axis=1, keepdims=True)
    joined_sum = jnp.sum(
        jnp.exp(jnp.where(allowed, joined - top_joined, NEGATIVE_FLOOR)), axis=1, keepdims=True
    )
    ranking = top_score + jnp.log(normal) - top_joined - jnp.log(joined_sum)
    penalty = jnp.sum(weights / normal * scores * scores, axis=1)
    return ranking[:, 0] + REGULAR * penalty


def gru_cell(gates_in, recurrent, prior, bias_cand, active_sessions):
    update = jax.nn.sigmoid(gates_in[:, 0] + recurrent[:, 0])
    reset = jax.nn.sigmoid(gates_in[:, 1] + recurrent[:, 1])
    candidate = jnp.tanh(gates_in[:, 2] + reset * (recurrent[:, 2] + bias_cand))
    return active_sessions * ((1.0 - update) * candidate + update * prior)


def block_rows(total, row_count):
    return math.gcd(total, 2 ** max(8, 22 - row_count.bit_length()))


def lookup_rows(index, table, row_count):
    total = index.shape[0]
    size = block_rows(total, row_count)

    def one_block(index_block):
        indicator = index_block[:, None] == jnp.arange(row_count, dtype=jnp.int32)[None, :]
        return jnp.dot(indicator.astype(jnp.bfloat16), table, preferred_element_type=jnp.float32)

    picked = lax.map(one_block, index.reshape(total // size, size))
    return picked.reshape(total, table.shape[1])


def sum_rows(index, values, row_count):
    total = index.shape[0]
    breadth = values.shape[1]
    size = block_rows(total, row_count)

    def add_block(accum, pair):
        index_block, value_block = pair
        indicator = index_block[:, None] == jnp.arange(row_count, dtype=jnp.int32)[None, :]
        term = lax.dot_general(
            indicator.astype(jnp.bfloat16),
            value_block,
            (((0,), (0,)), ((), ())),
            preferred_element_type=jnp.float32,
        )
        return (accum + term, None)

    accum, _ = lax.scan(
        add_block,
        jnp.zeros((row_count, breadth), jnp.float32),
        (index.reshape(total // size, size), values.reshape(total // size, size, breadth)),
    )
    return accum


def spread(own_low):
    return lax.all_gather(own_low, "mp", axis=1, tiled=True)


def move_state(state, destination, devices, slots):
    capacity = (slots + devices - 1) // devices
    target_device = destination // slots
    target_slot = destination % slots
    order = jnp.arange(slots)
    earlier = (target_device[:, None] == target_device[None, :]) & (order[:, None] > order[None, :])
    position = target_device * capacity + jnp.sum(earlier.astype(jnp.int32), axis=1)
    outgoing = jnp.zeros((devices * capacity, state.shape[1]), jnp.float32).at[position].set(state)
    labels = jnp.full((devices * capacity,), slots, jnp.int32).at[position].set(target_slot)
    arrived, arrived_labels = (
        lax.all_to_all(
            outgoing.astype(jnp.bfloat16), "dp", split_axis=0, concat_axis=0, tiled=True
        ).astype(outgoing.dtype),
        lax.all_to_all(labels, "dp", split_axis=0, concat_axis=0, tiled=True),
    )
    moved = jnp.zeros_like(state).at[arrived_labels].set(arrived, mode="drop")
    return (moved, arrived_labels, position)


def return_state(grad_start, labels, position, slots):
    inside = labels < slots
    spot = jnp.where(inside, labels, 0)
    returning = jnp.where(inside[:, None], jnp.take(grad_start, spot, axis=0), 0.0)
    back = lax.all_to_all(
        returning.astype(jnp.bfloat16), "dp", split_axis=0, concat_axis=0, tiled=True
    ).astype(returning.dtype)
    return jnp.take(back, position, axis=0)


def general(
    items,
    targets,
    masks,
    plan,
    negatives,
    h_init,
    emb,
    w_in,
    w_rec,
    b_in,
    b_rec_n,
    out_table,
    out_bias,
):
    blocks, steps, slots = items.shape
    halfwidth = h_init.shape[1]
    breadth = w_in.shape[0]
    vocab_rows = emb.shape[0]
    devices = lax.axis_size("dp")
    negs = negatives.shape[1]
    session_events = steps * slots
    columns = session_events + negs
    token_ids = blocks * session_events
    item_ids = items.reshape(token_ids)
    cand_ids = jnp.concatenate([targets.reshape(blocks, session_events), negatives], axis=1)
    flat_cands = cand_ids.reshape(blocks * columns)
    alive_flags = (masks > 0).astype(jnp.float32)
    w_in_flat = w_in.reshape(breadth, 3 * halfwidth)
    w_rec_flat = w_rec.reshape(breadth, 3 * halfwidth)
    cand_rows = jnp.zeros((blocks * columns, halfwidth), jnp.bfloat16)
    cand_bias = jnp.zeros((blocks * columns,), jnp.float32)
    emb_piece = lax.all_gather(emb, "dp", axis=0, tiled=True)
    out_piece = lax.all_gather(out_table, "dp", axis=0, tiled=True)
    bias_piece = lax.all_gather(out_bias.astype(jnp.bfloat16), "dp", axis=0, tiled=True).astype(
        jnp.float32
    )
    row_count = emb_piece.shape[0]
    embedded = lookup_rows(item_ids, emb_piece, row_count)
    shifted = flat_cands
    inside = (shifted >= 0) & (shifted < row_count)
    take_position = jnp.clip(shifted, 0, row_count - 1)
    cand_rows = jnp.where(inside[:, None], jnp.take(out_piece, take_position, axis=0), cand_rows)
    cand_bias = jnp.where(inside, jnp.take(bias_piece, take_position), cand_bias)
    embedded, cand_rows, cand_bias = (embedded, cand_rows, cand_bias)
    inputs_full, cand_full = (
        lax.all_gather(embedded.astype(jnp.bfloat16), "mp", axis=1, tiled=True),
        lax.all_gather(cand_rows, "mp", axis=1, tiled=True),
    )
    preacts = jnp.dot(inputs_full, w_in_flat, preferred_element_type=jnp.float32)
    preacts = preacts.reshape(blocks, steps, slots, 3, halfwidth) + b_in

    def advance(carry_pair, step_inputs):
        prior, prior_low = carry_pair
        gates_in, codes = step_inputs
        keeping = (codes == 1).astype(jnp.float32)[:, None]
        active_sessions = (codes > 0).astype(jnp.float32)[:, None]
        entering = prior_low * keeping.astype(jnp.bfloat16)
        recurrent = jnp.dot(entering, w_rec_flat, preferred_element_type=jnp.float32).reshape(
            slots, 3, halfwidth
        )
        fresh = gru_cell(gates_in, recurrent, prior * keeping, b_rec_n, active_sessions)
        fresh_own = fresh.astype(jnp.bfloat16)
        fresh_low = spread(fresh_own)
        return ((fresh, fresh_low), (prior, prior_low, recurrent, fresh_low, fresh_own))

    state = h_init
    state_low = spread(h_init.astype(jnp.bfloat16))
    records = []
    routes = []
    for event_block in range(blocks):
        (state, state_low), record = lax.scan(
            advance, (state, state_low), (preacts[event_block], masks[event_block])
        )
        records.append(record)
        if event_block + 1 < blocks:
            state, labels, position = move_state(state, plan[event_block], devices, slots)
            routes.append((labels, position))
            state_low = spread(state.astype(jnp.bfloat16))
    loss_total_sum = jnp.zeros((), jnp.float32)
    score_squared = jnp.zeros((), jnp.float32)
    hidden_squared = jnp.zeros((), jnp.float32)
    score_list = []
    for event_block in range(blocks):
        outputs = records[event_block][3].reshape(session_events, breadth)
        candidates = cand_full[event_block * columns : (event_block + 1) * columns]
        scores = lax.dot_general(
            outputs, candidates, (((1,), (1,)), ((), ())), preferred_element_type=jnp.float32
        )
        scores = scores + cand_bias[event_block * columns : (event_block + 1) * columns]
        active_sessions = alive_flags[event_block].reshape(session_events)
        usable = jnp.concatenate([active_sessions > 0, jnp.ones((negs,), dtype=bool)])
        losses = bpr_rows(
            scores, targets[event_block].reshape(session_events), cand_ids[event_block], usable
        )
        loss_total_sum = loss_total_sum + jnp.sum(active_sessions * losses)
        score_squared = score_squared + jnp.sum(active_sessions * jnp.sum(scores * scores, axis=1))
        output_values = outputs.astype(jnp.float32)
        hidden_squared = hidden_squared + jnp.sum(
            active_sessions[:, None] * output_values * output_values
        )
        score_list.append(scores)
    input_entries = inputs_full.astype(jnp.float32)
    input_squared = jnp.sum(alive_flags.reshape(token_ids)[:, None] * input_entries * input_entries)
    count_all, loss_all, input_all, hidden_all, score_all = lax.psum(
        (jnp.sum(alive_flags), loss_total_sum, input_squared, hidden_squared, score_squared), "dp"
    )
    loss = loss_all / count_all
    rms_inputs = jnp.sqrt(input_all / (count_all * breadth))
    rms_hidden = jnp.sqrt(hidden_all / (count_all * breadth))
    rms_scores = jnp.sqrt(score_all / (count_all * columns))
    from_scores = []
    row_grads = []
    bias_grads = []
    for event_block in range(blocks):
        active_sessions = alive_flags[event_block].reshape(session_events)
        usable = jnp.concatenate([active_sessions > 0, jnp.ones((negs,), dtype=bool)])
        wanted = targets[event_block].reshape(session_events)
        chosen = cand_ids[event_block]

        def block_loss(scores_arg):
            return jnp.sum(active_sessions * bpr_rows(scores_arg, wanted, chosen, usable))

        _, pullback = jax.vjp(block_loss, score_list[event_block])
        (grad_scores,) = pullback(jnp.ones((), jnp.float32) / count_all)
        bias_grads.append(jnp.sum(grad_scores, axis=0))
        scores_low = grad_scores.astype(jnp.bfloat16)
        own_rows = cand_rows[event_block * columns : (event_block + 1) * columns]
        to_outputs = jnp.dot(scores_low, own_rows, preferred_element_type=jnp.float32)
        from_scores.append(to_outputs.reshape(steps, slots, halfwidth))
        own_outputs = records[event_block][4].reshape(session_events, halfwidth)
        row_grads.append(
            lax.dot_general(
                scores_low,
                own_outputs,
                (((0,), (0,)), ((), ())),
                preferred_element_type=jnp.float32,
            )
        )
    cand_row_grads = jnp.concatenate(row_grads, axis=0)
    cand_bias_grads = jnp.concatenate(bias_grads, axis=0)

    def retreat(carry_triple, saved):
        grad_state, grad_rec_w, grad_bias_cand = carry_triple
        prior, prior_low, recurrent, gates_in, codes, from_output = saved
        grad_state = grad_state + from_output
        keeping = (codes == 1).astype(jnp.float32)[:, None]
        active_sessions = (codes > 0).astype(jnp.float32)[:, None]
        _, cell_pull = jax.vjp(
            lambda gate_arg, rec_arg, prior_arg, bias_arg: gru_cell(
                gate_arg, rec_arg, prior_arg, bias_arg, active_sessions
            ),
            gates_in,
            recurrent,
            prior * keeping,
            b_rec_n,
        )
        grad_gates, grad_rec, grad_prior, grad_bias = cell_pull(grad_state)
        rec_low = grad_rec.reshape(slots, 3 * halfwidth).astype(jnp.bfloat16)
        partial_sum = lax.dot_general(
            rec_low, w_rec_flat, (((1,), (1,)), ((), ())), preferred_element_type=jnp.float32
        )
        through_rec = lax.psum_scatter(
            partial_sum.astype(jnp.bfloat16), "mp", scatter_dimension=1, tiled=True
        ).astype(jnp.float32)
        entering = prior_low * keeping.astype(jnp.bfloat16)
        grad_rec_w = grad_rec_w + lax.dot_general(
            entering, rec_low, (((0,), (0,)), ((), ())), preferred_element_type=jnp.float32
        )
        previous = keeping * (grad_prior + through_rec)
        return ((previous, grad_rec_w, grad_bias_cand + grad_bias), grad_gates)

    grad_state = jnp.zeros((slots, halfwidth), jnp.float32)
    grad_rec_w = jnp.zeros((breadth, 3 * halfwidth), jnp.float32)
    grad_bias_cand = jnp.zeros((halfwidth,), jnp.float32)
    pre_grads = [None] * blocks
    for event_block in reversed(range(blocks)):
        prior_all, prior_low_all, recurrent_all, _, _ = records[event_block]
        (grad_state, grad_rec_w, grad_bias_cand), grad_pre = lax.scan(
            retreat,
            (grad_state, grad_rec_w, grad_bias_cand),
            (
                prior_all,
                prior_low_all,
                recurrent_all,
                preacts[event_block],
                masks[event_block],
                from_scores[event_block],
            ),
            reverse=True,
        )
        pre_grads[event_block] = grad_pre
        if event_block > 0:
            grad_state = return_state(
                grad_state, routes[event_block - 1][0], routes[event_block - 1][1], slots
            )
    pre_all = jnp.stack(pre_grads)
    grad_bias_in = jnp.sum(pre_all, axis=(0, 1, 2))
    pre_low = pre_all.reshape(token_ids, 3 * halfwidth).astype(jnp.bfloat16)
    grad_w_in = lax.dot_general(
        inputs_full, pre_low, (((0,), (0,)), ((), ())), preferred_element_type=jnp.float32
    )
    input_part = lax.dot_general(
        pre_low, w_in_flat, (((1,), (1,)), ((), ())), preferred_element_type=jnp.float32
    )
    grad_inputs = lax.psum_scatter(
        input_part.astype(jnp.bfloat16), "mp", scatter_dimension=1, tiled=True
    )
    bias_term = jnp.zeros((vocab_rows * devices,), jnp.float32).at[flat_cands].add(cand_bias_grads)
    weight_count = breadth * 3 * halfwidth
    packed_grads = jnp.concatenate(
        [
            grad_w_in.reshape(weight_count),
            grad_rec_w.reshape(weight_count),
            grad_bias_in.reshape(3 * halfwidth),
            grad_bias_cand,
        ]
    )
    packed_length = packed_grads.shape[0]
    padded_length = -(-packed_length // devices) * devices
    packed_grads = jnp.pad(packed_grads, (0, padded_length - packed_length))
    own_share, grad_out_bias = (
        lax.psum_scatter(packed_grads, "dp", scatter_dimension=0, tiled=True),
        lax.psum_scatter(bias_term, "dp", scatter_dimension=0, tiled=True),
    )
    summed_all = lax.all_gather(own_share.astype(jnp.bfloat16), "dp", axis=0, tiled=True).astype(
        own_share.dtype
    )
    summed_w_in = summed_all[:weight_count]
    summed_w_rec = summed_all[weight_count : 2 * weight_count]
    summed_b_in = summed_all[2 * weight_count : 2 * weight_count + 3 * halfwidth].reshape(
        3, halfwidth
    )
    summed_b_cand = summed_all[2 * weight_count + 3 * halfwidth : 2 * weight_count + 4 * halfwidth]
    shifted = flat_cands
    inside = (shifted >= 0) & (shifted < lax.axis_size("dp") * vocab_rows)
    position = jnp.where(inside, shifted, lax.axis_size("dp") * vocab_rows)
    both = lax.psum_scatter(
        jnp.concatenate(
            [
                sum_rows(item_ids, grad_inputs, lax.axis_size("dp") * vocab_rows),
                jnp.zeros((lax.axis_size("dp") * vocab_rows, halfwidth), jnp.float32)
                .at[position]
                .add(cand_row_grads, mode="drop"),
            ],
            axis=1,
        ),
        "dp",
        scatter_dimension=0,
        tiled=True,
    )
    grad_emb = both[:, :halfwidth]
    grad_out_table = both[:, halfwidth:]
    return (
        loss,
        rms_inputs,
        rms_hidden,
        rms_scores,
        state,
        grad_state,
        grad_emb,
        summed_w_in.reshape(breadth, 3, halfwidth),
        summed_w_rec.reshape(breadth, 3, halfwidth),
        summed_b_in,
        summed_b_cand,
        grad_out_table,
        grad_out_bias,
    )


def roundup(value, unit):
    return -(-value // unit) * unit


def bf16_parts(values):
    first = lax.reduce_precision(values, 8, 7)
    second = lax.reduce_precision(values - first, 8, 7)
    third = lax.reduce_precision(values - first - second, 8, 7)
    return first, second, third


def one_hot(index, size):
    return (index[:, None] == jnp.arange(size, dtype=index.dtype)[None, :]).astype(jnp.bfloat16)


def dot_f32(left, right):
    return jnp.dot(left, right, preferred_element_type=jnp.float32)


def dot_first(left, right):
    return lax.dot_general(
        left, right, (((0,), (0,)), ((), ())), preferred_element_type=jnp.float32
    )


def dot_last(left, right):
    return lax.dot_general(
        left, right, (((1,), (1,)), ((), ())), preferred_element_type=jnp.float32
    )


def swap_cores(values):
    return lax.ppermute(values, "mp", [(0, 1), (1, 0)])


def exchange(values):
    return lax.all_to_all(values, "dp", split_axis=0, concat_axis=0, tiled=True)


def plan_requests(ids, devices, rows, capacity):
    owner = ids // rows
    owners = one_hot(owner, devices)
    local = one_hot(ids % rows, rows)
    wanted = dot_first(owners, local) > 0.5
    order = jnp.arange(rows)
    before = (order[:, None] < order[None, :]).astype(jnp.bfloat16)
    position = dot_f32(wanted.astype(jnp.bfloat16), before)
    longest = jnp.max(jnp.sum(wanted.astype(jnp.float32), axis=1))
    spots = jnp.sum(
        owners.astype(jnp.float32) * dot_last(local, position.astype(jnp.bfloat16)), axis=1
    )
    slot = owner * capacity + spots.astype(jnp.int32)
    keyed = jnp.where(wanted, position, -1.0)
    match = keyed[:, None, :] == jnp.arange(capacity, dtype=jnp.float32)[None, :, None]
    listed = jnp.sum(jnp.where(match, order.astype(jnp.float32) + 1.0, 0.0), axis=2) - 1.0
    return listed.astype(jnp.int32), slot, longest


def plan_negatives(negatives, devices, rows, capacity, device):
    blocks, negs = negatives.shape
    chunk = math.gcd(negs, 128)
    owner = negatives // rows
    counts = jnp.sum(
        (owner[:, None, :] == jnp.arange(devices)[None, :, None]).astype(jnp.float32), axis=2
    )
    mine = (owner == device).astype(jnp.float32)
    grouped = mine.reshape(blocks * (negs // chunk), chunk)
    order = jnp.arange(chunk)
    before = (order[:, None] < order[None, :]).astype(jnp.bfloat16)
    inner = dot_f32(grouped.astype(jnp.bfloat16), before).reshape(blocks, negs // chunk, chunk)
    totals = jnp.sum(grouped, axis=1).reshape(blocks, negs // chunk)
    group = jnp.arange(negs // chunk)
    outer = jnp.sum(
        jnp.where(group[None, :, None] > group[None, None, :], totals[:, None, :], 0.0), axis=2
    )
    position = (inner + outer[:, :, None]).reshape(blocks, negs)
    keyed = jnp.where(mine > 0.5, position, -1.0)
    match = keyed[:, None, :] == jnp.arange(capacity, dtype=jnp.float32)[None, :, None]
    local = (negatives % rows).astype(jnp.float32) + 1.0
    listed = jnp.sum(jnp.where(match, local[:, None, :], 0.0), axis=2) - 1.0
    return listed.astype(jnp.int32), jnp.max(counts)


def widen(code, width):
    return jnp.concatenate([code] * (width // code.shape[1]), axis=1)


def forward_kernel(half, mp_ref, own_ref, oth_ref, code_ref, start_ref, wi_own, wi_oth, wr_own,
                   wr_oth, out_ref, ent_ref, upd_ref, rst_ref, cand_ref, rec_ref, pri_ref, end_ref,
                   sq_ref, wi, wr, pre, state, sems):
    me = mp_ref[0]
    other = 1 - me
    copies = [
        pltpu.make_async_copy(wi_own, wi.at[me], sems.at[0]),
        pltpu.make_async_copy(wi_oth, wi.at[other], sems.at[1]),
        pltpu.make_async_copy(wr_own, wr.at[me], sems.at[2]),
        pltpu.make_async_copy(wr_oth, wr.at[other], sems.at[3]),
    ]
    for copy in copies:
        copy.start()
    steps, slots, _ = code_ref.shape
    width = own_ref.shape[1]
    lane = lax.broadcasted_iota(jnp.int32, (slots, width), 1)
    real = lane < half
    ones = (lane >= half) & (lane < half + 3)
    own = own_ref[...]
    oth = oth_ref[...]
    state[...] = start_ref[...]
    copies[0].wait()
    copies[1].wait()
    for side in range(2):
        for gate in range(3):
            value = dot_f32(own, wi[side, gate, me]) + dot_f32(oth, wi[side, gate, other])
            pre[side, gate] = value.reshape(steps, slots, width)
    copies[2].wait()
    copies[3].wait()

    def step(t, sums):
        in_sum, out_sum = sums
        code = code_ref[t]
        keep = widen((code == 1.0).astype(jnp.float32), width)
        live = widen((code > 0.0).astype(jnp.float32), width)
        rows = pl.ds(pl.multiple_of(t * slots, slots), slots)
        for ref in (own_ref, oth_ref):
            entry = jnp.where(real, ref[rows, :].astype(jnp.float32), 0.0)
            in_sum = in_sum + live * entry * entry
        entering = []
        for side in range(2):
            value = keep * state[side].astype(jnp.bfloat16).astype(jnp.float32)
            if side == 0:
                value = jnp.where(ones, 1.0, value)
            value = value.astype(jnp.bfloat16)
            ent_ref[side, t] = value
            entering.append(value)
        for side in range(2):
            recurrent = [
                dot_f32(entering[0], wr[side, gate, 0]) + dot_f32(entering[1], wr[side, gate, 1])
                for gate in range(3)
            ]
            update = jax.nn.sigmoid(pre[side, 0, t] + recurrent[0])
            reset = jax.nn.sigmoid(pre[side, 1, t] + recurrent[1])
            candidate = jnp.tanh(pre[side, 2, t] + reset * recurrent[2])
            prior = keep * state[side]
            fresh = live * ((1.0 - update) * candidate + update * prior)
            fresh = jnp.where(real, fresh, 0.0)
            upd_ref[side, t] = update
            rst_ref[side, t] = reset
            cand_ref[side, t] = candidate
            rec_ref[side, t] = recurrent[2]
            pri_ref[side, t] = prior
            state[side] = fresh
            low = fresh.astype(jnp.bfloat16)
            out_sum = out_sum + low.astype(jnp.float32) * low.astype(jnp.float32)
            if side == 0:
                low = jnp.where(ones, 1.0, low.astype(jnp.float32)).astype(jnp.bfloat16)
            out_ref[side, t] = low
        return in_sum, out_sum

    zero = jnp.zeros((slots, width), jnp.float32)
    in_sum, out_sum = lax.fori_loop(0, steps, step, (zero, zero))
    end_ref[...] = state[...]
    sq_ref[0] = in_sum
    sq_ref[1] = out_sum


def run_forward(half, block, me, own, oth, codes, start, weights):
    _, blocks, events, width = own.shape
    _, steps, slots, lanes = codes.shape
    f32, low = jnp.float32, jnp.bfloat16
    whole = lambda shape: pl.BlockSpec(shape, lambda i, s: (0,) * len(shape))
    saved = (2, steps, slots, width)
    hidden = (2, slots, width)
    return pl.pallas_call(
        functools.partial(forward_kernel, half),
        grid_spec=pltpu.PrefetchScalarGridSpec(
            num_scalar_prefetch=1,
            grid=(1,),
            in_specs=[
                pl.BlockSpec((None, None, events, width), lambda i, s: (s[0], block, 0, 0)),
                pl.BlockSpec((None, None, events, width), lambda i, s: (s[0], block, 0, 0)),
                pl.BlockSpec((None, steps, slots, lanes), lambda i, s: (block, 0, 0, 0)),
                whole(hidden),
            ]
            + [pl.BlockSpec(memory_space=pl.ANY)] * 4,
            out_specs=[whole(saved)] * 7 + [whole(hidden)] * 2,
            scratch_shapes=[
                pltpu.VMEM((2, 3, 2, width, width), low),
                pltpu.VMEM((2, 3, 2, width, width), low),
                pltpu.VMEM((2, 3, steps, slots, width), f32),
                pltpu.VMEM(hidden, f32),
                pltpu.SemaphoreType.DMA((4,)),
            ],
        ),
        out_shape=[jax.ShapeDtypeStruct(saved, low)] * 2
        + [jax.ShapeDtypeStruct(saved, f32)] * 5
        + [jax.ShapeDtypeStruct(hidden, f32)] * 2,
        compiler_params=pltpu.CompilerParams(vmem_limit_bytes=VMEM_LIMIT),
        name="forward",
    )(me, own, oth, codes, start, *weights)


def backward_kernel(half, mp_ref, code_ref, from_ref, upd_ref, rst_ref, cand_ref, rec_ref, pri_ref,
                    last_ref, wi_own, wi_oth, wr_own, wr_oth, gate_ref, emb_ref, first_ref, wi, wr,
                    state, sems):
    me = mp_ref[0]
    other = 1 - me
    copies = [
        pltpu.make_async_copy(wr_own, wr.at[me], sems.at[0]),
        pltpu.make_async_copy(wr_oth, wr.at[other], sems.at[1]),
        pltpu.make_async_copy(wi_own, wi.at[me], sems.at[2]),
        pltpu.make_async_copy(wi_oth, wi.at[other], sems.at[3]),
    ]
    for copy in copies:
        copy.start()
    steps, slots, _ = code_ref.shape
    width = from_ref.shape[-1]
    real = lax.broadcasted_iota(jnp.int32, (slots, width), 1) < half
    state[...] = last_ref[...]
    copies[0].wait()
    copies[1].wait()

    def step(i, carry):
        t = steps - 1 - i
        code = code_ref[t]
        keep = widen((code == 1.0).astype(jnp.float32), width)
        live = widen((code > 0.0).astype(jnp.float32), width)
        gates = []
        direct = []
        for side in range(2):
            grad = live * (state[side] + from_ref[side, t])
            update, reset = upd_ref[side, t], rst_ref[side, t]
            candidate = cand_ref[side, t]
            grad_update = grad * (pri_ref[side, t] - candidate)
            grad_cand = grad * (1.0 - update) * (1.0 - candidate * candidate)
            grad_reset = grad_cand * rec_ref[side, t]
            values = [
                grad_update * update * (1.0 - update),
                grad_reset * reset * (1.0 - reset),
                grad_cand * reset,
                grad_cand,
            ]
            values = [value.astype(jnp.bfloat16) for value in values]
            for gate in range(4):
                gate_ref[gate, side, t] = values[gate]
            gates.append(values)
            direct.append(grad * update)
        for into in range(2):
            total = direct[into]
            for side in range(2):
                for gate in range(3):
                    total = total + dot_last(gates[side][gate], wr[side, gate, into])
            state[into] = jnp.where(real, keep * total, 0.0)
        return carry

    lax.fori_loop(0, steps, step, 0)
    first_ref[...] = state[...]
    copies[2].wait()
    copies[3].wait()
    events = steps * slots
    for into in range(2):
        total = jnp.zeros((events, width), jnp.float32)
        for side in range(2):
            for gate in range(3):
                grads = gate_ref[3 if gate == 2 else gate, side].reshape(events, width)
                total = total + dot_last(grads, wi[side, gate, into])
        emb_ref[into] = total.astype(jnp.bfloat16)


def run_backward(half, block, me, codes, from_scores, saved_values, last, weights):
    _, steps, slots, lanes = codes.shape
    width = last.shape[-1]
    f32, low = jnp.float32, jnp.bfloat16
    whole = lambda shape: pl.BlockSpec(shape, lambda i, s: (0,) * len(shape))
    saved = (2, steps, slots, width)
    hidden = (2, slots, width)
    return pl.pallas_call(
        functools.partial(backward_kernel, half),
        grid_spec=pltpu.PrefetchScalarGridSpec(
            num_scalar_prefetch=1,
            grid=(1,),
            in_specs=[pl.BlockSpec((None, steps, slots, lanes), lambda i, s: (block, 0, 0, 0))]
            + [whole(saved)] * 6
            + [whole(hidden)]
            + [pl.BlockSpec(memory_space=pl.ANY)] * 4,
            out_specs=[
                whole((4,) + saved),
                whole((2, steps * slots, width)),
                whole(hidden),
            ],
            scratch_shapes=[
                pltpu.VMEM((2, 3, 2, width, width), low),
                pltpu.VMEM((2, 3, 2, width, width), low),
                pltpu.VMEM(hidden, f32),
                pltpu.SemaphoreType.DMA((4,)),
            ],
        ),
        out_shape=[
            jax.ShapeDtypeStruct((4,) + saved, low),
            jax.ShapeDtypeStruct((2, steps * slots, width), low),
            jax.ShapeDtypeStruct(hidden, f32),
        ],
        compiler_params=pltpu.CompilerParams(vmem_limit_bytes=VMEM_LIMIT),
        name="backward",
    )(me, codes, from_scores, *saved_values, last, *weights)


def score_kernel(half, mp_ref, inv_ref, out_ref, want_ref, live_ref, use_ref, tgt_own, tgt_oth,
                 neg_own, neg_oth, grad_ref, to_ref, stat_ref, scores):
    me = mp_ref[0]
    other = 1 - me
    _, events, width = out_ref.shape
    batch = tgt_own.shape[0]
    devices, capacity, _ = neg_own.shape
    negs = devices * capacity
    cols = batch + negs
    lane = lax.broadcasted_iota(jnp.int32, (16, width), 1)
    row = lax.broadcasted_iota(jnp.int32, (16, width), 0)
    pick = jnp.where(
        row == 0,
        jnp.where(lane == half + 3, 256.0, jnp.where(lane == half + 4, 1.0, 0.0)),
        jnp.where((row == 1) & (lane == half + 5), 1.0, 0.0),
    ).astype(jnp.bfloat16)
    left_own = jnp.concatenate([out_ref[me], pick], axis=0)
    left_oth = jnp.concatenate([out_ref[other], pick], axis=0)
    nown = neg_own[...].reshape(negs, width)
    noth = neg_oth[...].reshape(negs, width)
    scores[:, :batch] = dot_last(left_own, tgt_own[...]) + dot_last(left_oth, tgt_oth[...])
    scores[:, batch:] = dot_last(left_own, nown) + dot_last(left_oth, noth)
    ids = scores[events : events + 1, :]
    usable = jnp.concatenate([use_ref[:1, :], scores[events + 1 : events + 2, batch:]], axis=1)
    ids = jnp.where(usable > 0.5, ids, -1.0)
    group = 16
    inv = inv_ref[0]
    base = me * events

    def rows_step(i, stats):
        loss_sum, square_sum = stats
        rows = pl.ds(pl.multiple_of(i * group, group), group)
        s = scores[rows, :]
        want = want_ref[rows, :1]
        live = live_ref[rows, :1]
        allowed = (ids != want) & (usable > 0.5)
        head = s[:, :batch]
        column = lax.broadcasted_iota(jnp.int32, (group, batch), 1)
        place = lax.broadcasted_iota(jnp.int32, (group, batch), 0) + (base + i * group)
        diagonal = column == place
        positive = jnp.sum(jnp.where(diagonal, head, 0.0), axis=1, keepdims=True)
        masked = jnp.where(allowed, s, NEGATIVE_FLOOR)
        top = jnp.max(masked, axis=1, keepdims=True)
        weight = jnp.exp(masked - top)
        normal = jnp.sum(weight, axis=1, keepdims=True)
        gap = positive - s
        tail = jnp.exp(-jnp.abs(gap))
        lift = 1.0 + tail
        joined = jnp.where(allowed, jnp.minimum(s, positive) - jnp.log(lift), NEGATIVE_FLOOR)
        top_joined = jnp.max(joined, axis=1, keepdims=True)
        mass = jnp.exp(joined - top_joined)
        joined_sum = jnp.sum(mass, axis=1, keepdims=True)
        shared = mass / lift
        below = gap >= 0.0
        to_score = shared * jnp.where(below, 1.0, tail)
        to_positive = jnp.sum(shared * jnp.where(below, tail, 1.0), axis=1, keepdims=True)
        square = s * s
        penalty = jnp.sum(weight * square, axis=1, keepdims=True) / normal
        loss = top + jnp.log(normal) - top_joined - jnp.log(joined_sum) + REGULAR * penalty
        scale = live * inv
        grad = (scale / normal) * weight * (
            1.0 + REGULAR * (square + 2.0 * s - penalty)
        ) - (scale / joined_sum) * to_score
        drop = jnp.where(diagonal, scale * to_positive / joined_sum, 0.0)
        grad_ref[rows, :batch] = (grad[:, :batch] - drop).astype(jnp.bfloat16)
        grad_ref[rows, batch:] = grad[:, batch:].astype(jnp.bfloat16)
        loss_sum = loss_sum + live * loss
        square_sum = square_sum + live * jnp.sum(square, axis=1, keepdims=True)
        return loss_sum, square_sum

    zero = jnp.zeros((group, 1), jnp.float32)
    loss_sum, square_sum = lax.fori_loop(0, events // group, rows_step, (zero, zero))
    stat_ref[0] = jnp.broadcast_to(loss_sum[:8] + loss_sum[8:], (8, 128))
    stat_ref[1] = jnp.broadcast_to(square_sum[:8] + square_sum[8:], (8, 128))
    grad_tgt = grad_ref[:, :batch]
    grad_neg = grad_ref[:, batch:]
    real = lax.broadcasted_iota(jnp.int32, (events, width), 1) < half
    to_own = dot_f32(grad_tgt, tgt_own[...]) + dot_f32(grad_neg, nown)
    to_oth = dot_f32(grad_tgt, tgt_oth[...]) + dot_f32(grad_neg, noth)
    to_ref[me] = jnp.where(real, to_own, 0.0)
    to_ref[other] = jnp.where(real, to_oth, 0.0)


def run_scores(half, block, me, inv, outputs, want, live, use, tgt_own, tgt_oth, neg_own, neg_oth):
    _, events, width = outputs.shape
    batch = tgt_own.shape[1]
    devices, _, capacity, _ = neg_own.shape
    cols = batch + devices * capacity
    low, f32 = jnp.bfloat16, jnp.float32
    whole = lambda shape: pl.BlockSpec(shape, lambda i, s: (0,) * len(shape))
    ofblock = lambda shape: pl.BlockSpec((None,) + shape, lambda i, s: (block,) + (0,) * len(shape))
    once = pl.Buffered(1)
    neg = pl.BlockSpec(
        (devices, None, capacity, width), lambda i, s: (0, block, 0, 0), pipeline_mode=once
    )
    return pl.pallas_call(
        functools.partial(score_kernel, half),
        grid_spec=pltpu.PrefetchScalarGridSpec(
            num_scalar_prefetch=1,
            grid=(1,),
            in_specs=[
                pl.BlockSpec(memory_space=pltpu.SMEM),
                whole((2, events, width)),
                ofblock((events, 128)),
                ofblock((events, 128)),
                ofblock((8, batch)),
                ofblock((batch, width)),
                ofblock((batch, width)),
                neg,
                neg,
            ],
            out_specs=[whole((events, cols)), whole((2, events, width)), whole((2, 8, 128))],
            scratch_shapes=[pltpu.VMEM((events + 16, cols), f32)],
        ),
        out_shape=[
            jax.ShapeDtypeStruct((events, cols), low),
            jax.ShapeDtypeStruct((2, events, width), f32),
            jax.ShapeDtypeStruct((2, 8, 128), f32),
        ],
        compiler_params=pltpu.CompilerParams(vmem_limit_bytes=VMEM_LIMIT),
        name="scores",
    )(me, inv, outputs, want, live, use, tgt_own, tgt_oth, neg_own, neg_oth)


def weight_grads_kernel(count, *refs):
    lefts, rights, out_ref = refs[:count], refs[count : 2 * count], refs[2 * count]
    for side in range(2):
        total = dot_first(lefts[0][side], rights[0][...])
        for left, right in zip(lefts[1:], rights[1:]):
            total = total + dot_first(left[side], right[...])
        out_ref[side] = total.astype(jnp.bfloat16)


def weight_grads(lefts, rights):
    _, _, width = lefts[0].shape
    return pl.pallas_call(
        functools.partial(weight_grads_kernel, len(lefts)),
        out_shape=jax.ShapeDtypeStruct((2, width, width), jnp.bfloat16),
        compiler_params=pltpu.CompilerParams(vmem_limit_bytes=VMEM_LIMIT),
        name="weights",
    )(*lefts, *rights)


def pair(index, own, oth):
    return jnp.where(index == 0, jnp.stack([own, oth]), jnp.stack([oth, own]))


def sum_devices(chunk):
    return lax.psum(chunk, "dp")


def routed(items, targets, masks, plan, negatives, h_init, emb, w_in, w_rec, b_in, b_rec_n,
           out_table, out_bias, wanted_rows, item_slot, target_slot, own_negatives, count):
    f32, low = jnp.float32, jnp.bfloat16
    blocks, steps, all_slots = items.shape
    slots = all_slots // 2
    events = steps * slots
    batch = 2 * events
    half = h_init.shape[1]
    width = roundup(half + 6, 128)
    rows = emb.shape[0]
    devices = lax.axis_size("dp")
    device = lax.axis_index("dp")
    core = lax.axis_index("mp")
    me = core.astype(jnp.int32).reshape(1)
    first_half = (core == 0).astype(f32)
    capacity = wanted_rows.shape[1] // 2
    neg_capacity = own_negatives.shape[1]
    breadth = 2 * half
    spare = width - half

    def mine(values):
        return lax.dynamic_index_in_dim(values, core, 0, keepdims=False)

    def core_major(values):
        return values.reshape(blocks, steps, 2, slots).transpose(2, 0, 1, 3)

    row_lanes = jnp.concatenate(
        [jnp.ones((rows, 3), f32), jnp.zeros((rows, spare - 3), f32)], axis=1
    )
    emb_wide = jnp.concatenate([emb, (row_lanes * first_half).astype(low)], axis=1)
    ids = device * rows + jnp.arange(rows)
    parts = bf16_parts(out_bias)
    out_lanes = jnp.stack(
        [*parts, (ids // 256).astype(f32), (ids % 256).astype(f32), jnp.ones((rows,), f32)]
        + [jnp.zeros((rows,), f32)] * (spare - 6),
        axis=1,
    )
    out_wide = jnp.concatenate([out_table, (out_lanes * first_half).astype(low)], axis=1)

    item_pick = one_hot(wanted_rows[:, :capacity].reshape(devices * capacity), rows)
    target_pick = one_hot(wanted_rows[:, capacity:].reshape(devices * capacity), rows)
    negative_pick = one_hot(own_negatives.reshape(blocks * neg_capacity), rows)
    item_rows = exchange(
        dot_f32(item_pick, emb_wide).astype(low).reshape(devices, capacity, width)
    ).reshape(devices * capacity, width)
    neg_own = lax.all_gather(
        dot_f32(negative_pick, out_wide).astype(low), "dp", axis=0, tiled=True
    )
    target_rows = exchange(
        dot_f32(target_pick, out_wide).astype(low).reshape(devices, capacity, width)
    ).reshape(devices * capacity, width)

    def widened(weight, bias, gate):
        matrix = weight[:, gate, :].reshape(2, half, half)
        matrix = jnp.pad(matrix, ((0, 0), (0, 0), (0, spare)))
        if bias is None:
            extra = jnp.zeros((2, spare, width), low)
        else:
            line = jnp.stack([*bf16_parts(bias)]).astype(low)
            extra = jnp.pad(line[None], ((0, 1), (0, spare - 3), (0, spare)))
        return jnp.concatenate([matrix, extra], axis=1)

    wi_own = jnp.stack([widened(w_in, b_in[gate], gate) for gate in range(3)])
    wr_own = jnp.stack([widened(w_rec, b_rec_n if gate == 2 else None, gate) for gate in range(3)])
    weights = (wi_own, swap_cores(wi_own), wr_own, swap_cores(wr_own))

    start_all = jnp.pad(h_init, ((0, 0), (0, spare))).reshape(2, slots, width)
    start_own = mine(start_all)
    start_oth = swap_cores(lax.dynamic_index_in_dim(start_all, 1 - core, 0, keepdims=False))
    state = pair(core, start_own, start_oth)

    codes_all = core_major(masks)
    codes = mine(codes_all).astype(f32)
    codes_wide = jnp.broadcast_to(codes[..., None], (blocks, steps, slots, 128))
    target_all = core_major(targets).reshape(2, blocks, events)
    want = jnp.broadcast_to(mine(target_all).astype(f32)[..., None], (blocks, events, 128))
    live = (codes_wide > 0.0).astype(f32).reshape(blocks, events, 128)
    use = (codes_all > 0).astype(f32).reshape(2, blocks, events).transpose(1, 0, 2)
    use = jnp.broadcast_to(use.reshape(blocks, 1, batch), (blocks, 8, batch))

    emb_own = dot_f32(one_hot(item_slot, devices * capacity), item_rows).astype(low)
    emb_oth = swap_cores(emb_own).reshape(2, blocks, events, width)
    emb_own = emb_own.reshape(2, blocks, events, width)

    hop = -(-slots // devices)
    saves = []
    outs = []
    entries = []
    routes = []
    in_square = jnp.zeros((), f32)
    out_square = jnp.zeros((), f32)
    lane_real = (jnp.arange(2 * width) % width < half).astype(f32)
    for block in range(blocks):
        result = run_forward(half, block, me, emb_own, emb_oth, codes_wide, state, weights)
        outs.append(result[0].reshape(2, events, width))
        entries.append(result[1].reshape(2, events, width))
        saves.append(result[2:7])
        state = result[7]
        in_square = in_square + jnp.sum(result[8][0])
        out_square = out_square + jnp.sum(result[8][1])
        if block + 1 < blocks:
            going = lax.dynamic_slice_in_dim(plan[block], core * slots, slots, 0)
            aim = going // all_slots
            place = going % all_slots
            order = jnp.arange(slots)
            earlier = (aim[:, None] == aim[None, :]) & (order[:, None] > order[None, :])
            position = aim * hop + jnp.sum(earlier.astype(jnp.int32), axis=1)
            lanes = jnp.arange(2 * width)[None, :]
            flat = state.transpose(1, 0, 2).reshape(slots, 2 * width)
            flat = jnp.where(lanes == half, place.astype(f32)[:, None], flat)
            flat = jnp.where(lanes == half + 1, 1.0, flat).astype(low)
            put = (jnp.arange(devices * hop)[:, None] == position[None, :]).astype(low)
            sent = dot_f32(put, flat).astype(low).reshape(devices, hop, 2 * width)
            came = exchange(sent).reshape(devices * hop, 2 * width)
            both = jnp.concatenate([came, swap_cores(came)], axis=0)
            label = jnp.where(both[:, half + 1] > 0.5, both[:, half].astype(f32), -1.0)
            here = (core * slots + order).astype(f32)
            take = (here[:, None] == label[None, :]).astype(low)
            moved = dot_f32(take, both) * lane_real
            state = moved.reshape(slots, 2, width).transpose(1, 0, 2)
            routes.append((label[: devices * hop], put))

    neg_oth = swap_cores(neg_own).reshape(devices, blocks, neg_capacity, width)
    neg_own = neg_own.reshape(devices, blocks, neg_capacity, width)
    target_slot_blocks = target_slot.reshape(2, blocks, events).transpose(1, 0, 2)
    target_hot = one_hot(target_slot_blocks.reshape(blocks * batch), devices * capacity)
    tgt_own = dot_f32(target_hot, target_rows).astype(low)
    tgt_oth = swap_cores(tgt_own).reshape(blocks, batch, width)
    tgt_own = tgt_own.reshape(blocks, batch, width)
    inv = (1.0 / count).reshape(1)
    from_scores = [None] * blocks
    loss_sum = jnp.zeros((), f32)
    score_square = jnp.zeros((), f32)
    row_grads = [None] * blocks
    for block in reversed(range(blocks)):
        grad_own, toward, stat = run_scores(
            half, block, me, inv, outs[block], want, live, use, tgt_own, tgt_oth, neg_own, neg_oth
        )
        from_scores[block] = toward.reshape(2, steps, slots, width)
        loss_sum = loss_sum + jnp.sum(stat[0, :, 0])
        score_square = score_square + jnp.sum(stat[1, :, 0])
        grad_oth = swap_cores(grad_own)
        outs_oth = swap_cores(
            lax.dynamic_index_in_dim(outs[block], 1 - core, 0, keepdims=False)
        )
        row_grads[block] = (
            dot_first(grad_own, mine(outs[block])) + dot_first(grad_oth, outs_oth)
        ).astype(low)
    target_grads = jnp.concatenate([value[:batch] for value in row_grads], axis=0)
    negative_grads = jnp.stack(
        [value[batch:].reshape(devices, neg_capacity, width) for value in row_grads], axis=1
    ).reshape(devices, blocks * neg_capacity, width)
    negative_came = exchange(negative_grads)
    target_came = exchange(
        dot_first(target_hot, target_grads).astype(low).reshape(devices, capacity, width)
    )

    own_stats = jnp.stack([loss_sum, in_square, out_square, score_square])
    own_stats = jnp.pad(own_stats, (0, 124)).reshape(1, 1, 128)
    own_stats = own_stats + swap_cores(own_stats)
    all_stats = jnp.sum(exchange(jnp.broadcast_to(own_stats, (devices, 1, 128))), axis=(0, 1))

    grad_state = jnp.zeros((2, slots, width), f32)
    gate_own = [None] * blocks
    gate_oth = [None] * blocks
    emb_grads = [None] * blocks
    for block in reversed(range(blocks)):
        gates, grad_emb_rows, grad_state = run_backward(
            half, block, me, codes_wide, from_scores[block], saves[block], grad_state, weights
        )
        gates = gates.reshape(4, 2, events, width).transpose(1, 0, 2, 3)
        gate_own[block] = mine(gates)
        gate_oth[block] = swap_cores(
            lax.dynamic_index_in_dim(gates, 1 - core, 0, keepdims=False)
        )
        emb_own_grad = mine(grad_emb_rows)
        emb_oth_grad = swap_cores(
            lax.dynamic_index_in_dim(grad_emb_rows, 1 - core, 0, keepdims=False)
        )
        emb_grads[block] = pair(core, emb_own_grad, emb_oth_grad)
        if block > 0:
            label, put = routes[block - 1]
            flat = grad_state.transpose(1, 0, 2).reshape(slots, 2 * width).astype(low)
            both = jnp.concatenate([flat, swap_cores(flat)], axis=0)
            order = jnp.arange(slots)
            names = jnp.concatenate([core * slots + order, (1 - core) * slots + order]).astype(f32)
            fetch = (label[:, None] == names[None, :]).astype(low)
            back = exchange(dot_f32(fetch, both).astype(low).reshape(devices, hop, 2 * width))
            flat = dot_first(put, back.reshape(devices * hop, 2 * width)) * lane_real
            grad_state = flat.reshape(slots, 2, width).transpose(1, 0, 2)

    entry_oth = [swap_cores(value) for value in entries]
    emb_full = [
        [pair(core, mine(emb_own)[block], mine(emb_oth)[block]) for block in range(blocks)],
        [
            pair(
                core,
                lax.dynamic_index_in_dim(emb_own, 1 - core, 0, keepdims=False)[block],
                lax.dynamic_index_in_dim(emb_oth, 1 - core, 0, keepdims=False)[block],
            )
            for block in range(blocks)
        ],
    ]
    summed = []
    for lefts, last in (
        ([*entries, *entry_oth], 2),
        ([*emb_full[0], *emb_full[1]], 3),
    ):
        for gate in (0, 1, last):
            rights = [value[gate] for value in gate_own] + [value[gate] for value in gate_oth]
            summed.append(weight_grads(lefts, rights))
    summed = sum_devices(jnp.stack(summed)).astype(f32)
    rec_sum, in_sum = summed[:3], summed[3:]

    def unpadded(values):
        return values[:, :, :half, :half].reshape(3, breadth, half).transpose(1, 0, 2)

    grad_b_in = in_sum[:, 0, half, :half]
    grad_b_rec = rec_sum[2, 0, half, :half]

    item_slot_blocks = item_slot.reshape(2, blocks, events).transpose(1, 0, 2)
    item_hot = one_hot(item_slot_blocks.reshape(blocks * batch), devices * capacity)
    item_grads = jnp.stack(emb_grads).reshape(blocks * batch, width)
    item_came = exchange(
        dot_first(item_hot, item_grads).astype(low).reshape(devices, capacity, width)
    )
    grad_emb = dot_first(item_pick, item_came.reshape(devices * capacity, width))[:, :half]
    negative_sum = jnp.sum(negative_came.astype(f32), axis=0).astype(low)
    grad_out = dot_first(
        target_pick, target_came.reshape(devices * capacity, width)
    ) + dot_first(negative_pick, negative_sum)
    bias_own = grad_out[:, half]
    grad_out_bias = jnp.where(core == 0, bias_own, swap_cores(bias_own))

    def slots_of(values):
        own = mine(values)
        oth = swap_cores(lax.dynamic_index_in_dim(values, 1 - core, 0, keepdims=False))
        return pair(core, own, oth).reshape(all_slots, width)[:, :half]

    columns = batch + negatives.shape[1]
    return (
        all_stats[0] / count,
        jnp.sqrt(all_stats[1] / (count * breadth)),
        jnp.sqrt(all_stats[2] / (count * breadth)),
        jnp.sqrt(all_stats[3] / (count * columns)),
        slots_of(state),
        slots_of(grad_state),
        grad_emb,
        unpadded(in_sum),
        unpadded(rec_sum),
        grad_b_in,
        grad_b_rec,
        grad_out[:, :half],
        grad_out_bias,
    )


def shards(items, targets, masks, plan, negatives, h_init, emb, w_in, w_rec, b_in, b_rec_n,
           out_table, out_bias):
    blocks, steps, all_slots = items.shape
    devices = lax.axis_size("dp")
    rows = emb.shape[0]
    requests = blocks * steps * all_slots
    capacity = max(32, roundup(-(-requests // devices), 16))
    mean = -(-negatives.shape[1] // devices)
    neg_capacity = min(roundup(mean + 4 * math.isqrt(mean), 16), roundup(rows, 16))

    def core_major(values):
        split = values.reshape(blocks, steps, 2, all_slots // 2)
        return split.transpose(2, 0, 1, 3).reshape(requests)

    item_rows, item_slot, item_most = plan_requests(core_major(items), devices, rows, capacity)
    target_rows, target_slot, target_most = plan_requests(
        core_major(targets), devices, rows, capacity
    )
    own_negatives, negative_most = plan_negatives(
        negatives, devices, rows, neg_capacity, lax.axis_index("dp")
    )
    wanted_rows = exchange(jnp.concatenate([item_rows, target_rows], axis=1))
    over = (
        (item_most > capacity) | (target_most > capacity) | (negative_most > neg_capacity)
    ).astype(jnp.int32)
    alive = jnp.sum((masks > 0).astype(jnp.int32))
    lane = jnp.arange(128)[None, :]
    tally = jnp.where(lane == 0, alive, jnp.where(lane == 1, over, 0))
    tally = lax.psum(jnp.broadcast_to(tally, (8, 128)), "dp")
    count = tally[0, 0].astype(jnp.float32)
    given = (items, targets, masks, plan, negatives, h_init, emb, w_in, w_rec, b_in, b_rec_n,
             out_table, out_bias)
    return lax.cond(
        tally[0, 1] == 0,
        lambda: routed(*given, wanted_rows, item_slot, target_slot, own_negatives, count),
        lambda: general(*given),
    )


def solution(mesh):
    return jax.shard_map(
        shards,
        mesh=mesh,
        in_specs=(
            P(None, None, "dp"),
            P(None, None, "dp"),
            P(None, None, "dp"),
            P(None, "dp"),
            P(),
            P("dp", "mp"),
            P("dp", "mp"),
            P(None, None, "mp"),
            P(None, None, "mp"),
            P(None, "mp"),
            P("mp"),
            P("dp", "mp"),
            P("dp"),
        ),
        out_specs=(
            P(),
            P(),
            P(),
            P(),
            P("dp", "mp"),
            P("dp", "mp"),
            P("dp", "mp"),
            P(None, None, "mp"),
            P(None, None, "mp"),
            P(None, "mp"),
            P("mp"),
            P("dp", "mp"),
            P("dp"),
        ),
        check_vma=False,
    )
```

```python
import functools
import math

import jax
import jax.numpy as jnp
from jax import lax
from jax.experimental import pallas as pl
from jax.experimental.pallas import tpu as pltpu
from jax.sharding import PartitionSpec as P

REGULAR = 1.0
NEGATIVE_FLOOR = -1e30
VMEM_LIMIT = 56 * 1024 * 1024


def bpr_rows(scores, wanted, chosen, usable):
    session_events = scores.shape[0]
    allowed = usable[None, :] & (chosen[None, :] != wanted[:, None])
    positive = jnp.diagonal(scores[:, :session_events])
    top_score = jnp.max(jnp.where(allowed, scores, NEGATIVE_FLOOR), axis=1, keepdims=True)
    weights = jnp.exp(jnp.where(allowed, scores - top_score, NEGATIVE_FLOOR))
    normal = jnp.sum(weights, axis=1, keepdims=True)
    joined = scores + jax.nn.log_sigmoid(positive[:, None] - scores)
    top_joined = jnp.max(jnp.where(allowed, joined, NEGATIVE_FLOOR), axis=1, keepdims=True)
    joined_sum = jnp.sum(
        jnp.exp(jnp.where(allowed, joined - top_joined, NEGATIVE_FLOOR)), axis=1, keepdims=True
    )
    ranking = top_score + jnp.log(normal) - top_joined - jnp.log(joined_sum)
    penalty = jnp.sum(weights / normal * scores * scores, axis=1)
    return ranking[:, 0] + REGULAR * penalty


def gru_cell(gates_in, recurrent, prior, bias_cand, active_sessions):
    update = jax.nn.sigmoid(gates_in[:, 0] + recurrent[:, 0])
    reset = jax.nn.sigmoid(gates_in[:, 1] + recurrent[:, 1])
    candidate = jnp.tanh(gates_in[:, 2] + reset * (recurrent[:, 2] + bias_cand))
    return active_sessions * ((1.0 - update) * candidate + update * prior)


def block_rows(total, row_count):
    return math.gcd(total, 2 ** max(8, 22 - row_count.bit_length()))


def lookup_rows(index, table, row_count):
    total = index.shape[0]
    size = block_rows(total, row_count)

    def one_block(index_block):
        indicator = index_block[:, None] == jnp.arange(row_count, dtype=jnp.int32)[None, :]
        return jnp.dot(indicator.astype(jnp.bfloat16), table, preferred_element_type=jnp.float32)

    picked = lax.map(one_block, index.reshape(total // size, size))
    return picked.reshape(total, table.shape[1])


def sum_rows(index, values, row_count):
    total = index.shape[0]
    breadth = values.shape[1]
    size = block_rows(total, row_count)

    def add_block(accum, pair):
        index_block, value_block = pair
        indicator = index_block[:, None] == jnp.arange(row_count, dtype=jnp.int32)[None, :]
        term = lax.dot_general(
            indicator.astype(jnp.bfloat16),
            value_block,
            (((0,), (0,)), ((), ())),
            preferred_element_type=jnp.float32,
        )
        return (accum + term, None)

    accum, _ = lax.scan(
        add_block,
        jnp.zeros((row_count, breadth), jnp.float32),
        (index.reshape(total // size, size), values.reshape(total // size, size, breadth)),
    )
    return accum


def spread(own_low):
    return lax.all_gather(own_low, "mp", axis=1, tiled=True)


def move_state(state, destination, devices, slots):
    capacity = (slots + devices - 1) // devices
    target_device = destination // slots
    target_slot = destination % slots
    order = jnp.arange(slots)
    earlier = (target_device[:, None] == target_device[None, :]) & (order[:, None] > order[None, :])
    position = target_device * capacity + jnp.sum(earlier.astype(jnp.int32), axis=1)
    outgoing = jnp.zeros((devices * capacity, state.shape[1]), jnp.float32).at[position].set(state)
    labels = jnp.full((devices * capacity,), slots, jnp.int32).at[position].set(target_slot)
    arrived, arrived_labels = (
        lax.all_to_all(
            outgoing.astype(jnp.bfloat16), "dp", split_axis=0, concat_axis=0, tiled=True
        ).astype(outgoing.dtype),
        lax.all_to_all(labels, "dp", split_axis=0, concat_axis=0, tiled=True),
    )
    moved = jnp.zeros_like(state).at[arrived_labels].set(arrived, mode="drop")
    return (moved, arrived_labels, position)


def return_state(grad_start, labels, position, slots):
    inside = labels < slots
    spot = jnp.where(inside, labels, 0)
    returning = jnp.where(inside[:, None], jnp.take(grad_start, spot, axis=0), 0.0)
    back = lax.all_to_all(
        returning.astype(jnp.bfloat16), "dp", split_axis=0, concat_axis=0, tiled=True
    ).astype(returning.dtype)
    return jnp.take(back, position, axis=0)


def general(
    items,
    targets,
    masks,
    plan,
    negatives,
    h_init,
    emb,
    w_in,
    w_rec,
    b_in,
    b_rec_n,
    out_table,
    out_bias,
):
    blocks, steps, slots = items.shape
    halfwidth = h_init.shape[1]
    breadth = w_in.shape[0]
    vocab_rows = emb.shape[0]
    devices = lax.axis_size("dp")
    negs = negatives.shape[1]
    session_events = steps * slots
    columns = session_events + negs
    token_ids = blocks * session_events
    item_ids = items.reshape(token_ids)
    cand_ids = jnp.concatenate([targets.reshape(blocks, session_events), negatives], axis=1)
    flat_cands = cand_ids.reshape(blocks * columns)
    alive_flags = (masks > 0).astype(jnp.float32)
    w_in_flat = w_in.reshape(breadth, 3 * halfwidth)
    w_rec_flat = w_rec.reshape(breadth, 3 * halfwidth)
    cand_rows = jnp.zeros((blocks * columns, halfwidth), jnp.bfloat16)
    cand_bias = jnp.zeros((blocks * columns,), jnp.float32)
    emb_piece = lax.all_gather(emb, "dp", axis=0, tiled=True)
    out_piece = lax.all_gather(out_table, "dp", axis=0, tiled=True)
    bias_piece = lax.all_gather(out_bias.astype(jnp.bfloat16), "dp", axis=0, tiled=True).astype(
        jnp.float32
    )
    row_count = emb_piece.shape[0]
    embedded = lookup_rows(item_ids, emb_piece, row_count)
    shifted = flat_cands
    inside = (shifted >= 0) & (shifted < row_count)
    take_position = jnp.clip(shifted, 0, row_count - 1)
    cand_rows = jnp.where(inside[:, None], jnp.take(out_piece, take_position, axis=0), cand_rows)
    cand_bias = jnp.where(inside, jnp.take(bias_piece, take_position), cand_bias)
    embedded, cand_rows, cand_bias = (embedded, cand_rows, cand_bias)
    inputs_full, cand_full = (
        lax.all_gather(embedded.astype(jnp.bfloat16), "mp", axis=1, tiled=True),
        lax.all_gather(cand_rows, "mp", axis=1, tiled=True),
    )
    preacts = jnp.dot(inputs_full, w_in_flat, preferred_element_type=jnp.float32)
    preacts = preacts.reshape(blocks, steps, slots, 3, halfwidth) + b_in

    def advance(carry_pair, step_inputs):
        prior, prior_low = carry_pair
        gates_in, codes = step_inputs
        keeping = (codes == 1).astype(jnp.float32)[:, None]
        active_sessions = (codes > 0).astype(jnp.float32)[:, None]
        entering = prior_low * keeping.astype(jnp.bfloat16)
        recurrent = jnp.dot(entering, w_rec_flat, preferred_element_type=jnp.float32).reshape(
            slots, 3, halfwidth
        )
        fresh = gru_cell(gates_in, recurrent, prior * keeping, b_rec_n, active_sessions)
        fresh_own = fresh.astype(jnp.bfloat16)
        fresh_low = spread(fresh_own)
        return ((fresh, fresh_low), (prior, prior_low, recurrent, fresh_low, fresh_own))

    state = h_init
    state_low = spread(h_init.astype(jnp.bfloat16))
    records = []
    routes = []
    for event_block in range(blocks):
        (state, state_low), record = lax.scan(
            advance, (state, state_low), (preacts[event_block], masks[event_block])
        )
        records.append(record)
        if event_block + 1 < blocks:
            state, labels, position = move_state(state, plan[event_block], devices, slots)
            routes.append((labels, position))
            state_low = spread(state.astype(jnp.bfloat16))
    loss_total_sum = jnp.zeros((), jnp.float32)
    score_squared = jnp.zeros((), jnp.float32)
    hidden_squared = jnp.zeros((), jnp.float32)
    score_list = []
    for event_block in range(blocks):
        outputs = records[event_block][3].reshape(session_events, breadth)
        candidates = cand_full[event_block * columns : (event_block + 1) * columns]
        scores = lax.dot_general(
            outputs, candidates, (((1,), (1,)), ((), ())), preferred_element_type=jnp.float32
        )
        scores = scores + cand_bias[event_block * columns : (event_block + 1) * columns]
        active_sessions = alive_flags[event_block].reshape(session_events)
        usable = jnp.concatenate([active_sessions > 0, jnp.ones((negs,), dtype=bool)])
        losses = bpr_rows(
            scores, targets[event_block].reshape(session_events), cand_ids[event_block], usable
        )
        loss_total_sum = loss_total_sum + jnp.sum(active_sessions * losses)
        score_squared = score_squared + jnp.sum(active_sessions * jnp.sum(scores * scores, axis=1))
        output_values = outputs.astype(jnp.float32)
        hidden_squared = hidden_squared + jnp.sum(
            active_sessions[:, None] * output_values * output_values
        )
        score_list.append(scores)
    input_entries = inputs_full.astype(jnp.float32)
    input_squared = jnp.sum(alive_flags.reshape(token_ids)[:, None] * input_entries * input_entries)
    count_all, loss_all, input_all, hidden_all, score_all = lax.psum(
        (jnp.sum(alive_flags), loss_total_sum, input_squared, hidden_squared, score_squared), "dp"
    )
    loss = loss_all / count_all
    rms_inputs = jnp.sqrt(input_all / (count_all * breadth))
    rms_hidden = jnp.sqrt(hidden_all / (count_all * breadth))
    rms_scores = jnp.sqrt(score_all / (count_all * columns))
    from_scores = []
    row_grads = []
    bias_grads = []
    for event_block in range(blocks):
        active_sessions = alive_flags[event_block].reshape(session_events)
        usable = jnp.concatenate([active_sessions > 0, jnp.ones((negs,), dtype=bool)])
        wanted = targets[event_block].reshape(session_events)
        chosen = cand_ids[event_block]

        def block_loss(scores_arg):
            return jnp.sum(active_sessions * bpr_rows(scores_arg, wanted, chosen, usable))

        _, pullback = jax.vjp(block_loss, score_list[event_block])
        (grad_scores,) = pullback(jnp.ones((), jnp.float32) / count_all)
        bias_grads.append(jnp.sum(grad_scores, axis=0))
        scores_low = grad_scores.astype(jnp.bfloat16)
        own_rows = cand_rows[event_block * columns : (event_block + 1) * columns]
        to_outputs = jnp.dot(scores_low, own_rows, preferred_element_type=jnp.float32)
        from_scores.append(to_outputs.reshape(steps, slots, halfwidth))
        own_outputs = records[event_block][4].reshape(session_events, halfwidth)
        row_grads.append(
            lax.dot_general(
                scores_low,
                own_outputs,
                (((0,), (0,)), ((), ())),
                preferred_element_type=jnp.float32,
            )
        )
    cand_row_grads = jnp.concatenate(row_grads, axis=0)
    cand_bias_grads = jnp.concatenate(bias_grads, axis=0)

    def retreat(carry_triple, saved):
        grad_state, grad_rec_w, grad_bias_cand = carry_triple
        prior, prior_low, recurrent, gates_in, codes, from_output = saved
        grad_state = grad_state + from_output
        keeping = (codes == 1).astype(jnp.float32)[:, None]
        active_sessions = (codes > 0).astype(jnp.float32)[:, None]
        _, cell_pull = jax.vjp(
            lambda gate_arg, rec_arg, prior_arg, bias_arg: gru_cell(
                gate_arg, rec_arg, prior_arg, bias_arg, active_sessions
            ),
            gates_in,
            recurrent,
            prior * keeping,
            b_rec_n,
        )
        grad_gates, grad_rec, grad_prior, grad_bias = cell_pull(grad_state)
        rec_low = grad_rec.reshape(slots, 3 * halfwidth).astype(jnp.bfloat16)
        partial_sum = lax.dot_general(
            rec_low, w_rec_flat, (((1,), (1,)), ((), ())), preferred_element_type=jnp.float32
        )
        through_rec = lax.psum_scatter(
            partial_sum.astype(jnp.bfloat16), "mp", scatter_dimension=1, tiled=True
        ).astype(jnp.float32)
        entering = prior_low * keeping.astype(jnp.bfloat16)
        grad_rec_w = grad_rec_w + lax.dot_general(
            entering, rec_low, (((0,), (0,)), ((), ())), preferred_element_type=jnp.float32
        )
        previous = keeping * (grad_prior + through_rec)
        return ((previous, grad_rec_w, grad_bias_cand + grad_bias), grad_gates)

    grad_state = jnp.zeros((slots, halfwidth), jnp.float32)
    grad_rec_w = jnp.zeros((breadth, 3 * halfwidth), jnp.float32)
    grad_bias_cand = jnp.zeros((halfwidth,), jnp.float32)
    pre_grads = [None] * blocks
    for event_block in reversed(range(blocks)):
        prior_all, prior_low_all, recurrent_all, _, _ = records[event_block]
        (grad_state, grad_rec_w, grad_bias_cand), grad_pre = lax.scan(
            retreat,
            (grad_state, grad_rec_w, grad_bias_cand),
            (
                prior_all,
                prior_low_all,
                recurrent_all,
                preacts[event_block],
                masks[event_block],
                from_scores[event_block],
            ),
            reverse=True,
        )
        pre_grads[event_block] = grad_pre
        if event_block > 0:
            grad_state = return_state(
                grad_state, routes[event_block - 1][0], routes[event_block - 1][1], slots
            )
    pre_all = jnp.stack(pre_grads)
    grad_bias_in = jnp.sum(pre_all, axis=(0, 1, 2))
    pre_low = pre_all.reshape(token_ids, 3 * halfwidth).astype(jnp.bfloat16)
    grad_w_in = lax.dot_general(
        inputs_full, pre_low, (((0,), (0,)), ((), ())), preferred_element_type=jnp.float32
    )
    input_part = lax.dot_general(
        pre_low, w_in_flat, (((1,), (1,)), ((), ())), preferred_element_type=jnp.float32
    )
    grad_inputs = lax.psum_scatter(
        input_part.astype(jnp.bfloat16), "mp", scatter_dimension=1, tiled=True
    )
    bias_term = jnp.zeros((vocab_rows * devices,), jnp.float32).at[flat_cands].add(cand_bias_grads)
    weight_count = breadth * 3 * halfwidth
    packed_grads = jnp.concatenate(
        [
            grad_w_in.reshape(weight_count),
            grad_rec_w.reshape(weight_count),
            grad_bias_in.reshape(3 * halfwidth),
            grad_bias_cand,
        ]
    )
    packed_length = packed_grads.shape[0]
    padded_length = -(-packed_length // devices) * devices
    packed_grads = jnp.pad(packed_grads, (0, padded_length - packed_length))
    own_share, grad_out_bias = (
        lax.psum_scatter(packed_grads, "dp", scatter_dimension=0, tiled=True),
        lax.psum_scatter(bias_term, "dp", scatter_dimension=0, tiled=True),
    )
    summed_all = lax.all_gather(own_share.astype(jnp.bfloat16), "dp", axis=0, tiled=True).astype(
        own_share.dtype
    )
    summed_w_in = summed_all[:weight_count]
    summed_w_rec = summed_all[weight_count : 2 * weight_count]
    summed_b_in = summed_all[2 * weight_count : 2 * weight_count + 3 * halfwidth].reshape(
        3, halfwidth
    )
    summed_b_cand = summed_all[2 * weight_count + 3 * halfwidth : 2 * weight_count + 4 * halfwidth]
    shifted = flat_cands
    inside = (shifted >= 0) & (shifted < lax.axis_size("dp") * vocab_rows)
    position = jnp.where(inside, shifted, lax.axis_size("dp") * vocab_rows)
    both = lax.psum_scatter(
        jnp.concatenate(
            [
                sum_rows(item_ids, grad_inputs, lax.axis_size("dp") * vocab_rows),
                jnp.zeros((lax.axis_size("dp") * vocab_rows, halfwidth), jnp.float32)
                .at[position]
                .add(cand_row_grads, mode="drop"),
            ],
            axis=1,
        ),
        "dp",
        scatter_dimension=0,
        tiled=True,
    )
    grad_emb = both[:, :halfwidth]
    grad_out_table = both[:, halfwidth:]
    return (
        loss,
        rms_inputs,
        rms_hidden,
        rms_scores,
        state,
        grad_state,
        grad_emb,
        summed_w_in.reshape(breadth, 3, halfwidth),
        summed_w_rec.reshape(breadth, 3, halfwidth),
        summed_b_in,
        summed_b_cand,
        grad_out_table,
        grad_out_bias,
    )


def roundup(value, unit):
    return -(-value // unit) * unit


def bf16_parts(values):
    first = lax.reduce_precision(values, 8, 7)
    second = lax.reduce_precision(values - first, 8, 7)
    third = lax.reduce_precision(values - first - second, 8, 7)
    return first, second, third


def one_hot(index, size):
    return (index[:, None] == jnp.arange(size, dtype=index.dtype)[None, :]).astype(jnp.bfloat16)


def dot_f32(left, right):
    return jnp.dot(left, right, preferred_element_type=jnp.float32)


def dot_first(left, right):
    return lax.dot_general(
        left, right, (((0,), (0,)), ((), ())), preferred_element_type=jnp.float32
    )


def dot_last(left, right):
    return lax.dot_general(
        left, right, (((1,), (1,)), ((), ())), preferred_element_type=jnp.float32
    )


def swap_cores(values):
    return lax.ppermute(values, "mp", [(0, 1), (1, 0)])


def exchange(values):
    return lax.all_to_all(values, "dp", split_axis=0, concat_axis=0, tiled=True)


def plan_requests(ids, devices, rows, capacity):
    owner = ids // rows
    owners = one_hot(owner, devices)
    local = one_hot(ids % rows, rows)
    wanted = dot_first(owners, local) > 0.5
    order = jnp.arange(rows)
    before = (order[:, None] < order[None, :]).astype(jnp.bfloat16)
    position = dot_f32(wanted.astype(jnp.bfloat16), before)
    longest = jnp.max(jnp.sum(wanted.astype(jnp.float32), axis=1))
    spots = jnp.sum(
        owners.astype(jnp.float32) * dot_last(local, position.astype(jnp.bfloat16)), axis=1
    )
    slot = owner * capacity + spots.astype(jnp.int32)
    keyed = jnp.where(wanted, position, -1.0)
    match = keyed[:, None, :] == jnp.arange(capacity, dtype=jnp.float32)[None, :, None]
    listed = jnp.sum(jnp.where(match, order.astype(jnp.float32) + 1.0, 0.0), axis=2) - 1.0
    return listed.astype(jnp.int32), slot, longest


def plan_negatives(negatives, devices, rows, capacity, device):
    blocks, negs = negatives.shape
    chunk = math.gcd(negs, 128)
    owner = negatives // rows
    mine = (owner == device).astype(jnp.float32)
    grouped = mine.reshape(blocks * (negs // chunk), chunk)
    order = jnp.arange(chunk)
    before = (order[:, None] < order[None, :]).astype(jnp.bfloat16)
    inner = dot_f32(grouped.astype(jnp.bfloat16), before).reshape(blocks, negs // chunk, chunk)
    totals = jnp.sum(grouped, axis=1).reshape(blocks, negs // chunk)
    group = jnp.arange(negs // chunk)
    outer = jnp.sum(
        jnp.where(group[None, :, None] > group[None, None, :], totals[:, None, :], 0.0), axis=2
    )
    position = (inner + outer[:, :, None]).reshape(blocks, negs)
    keyed = jnp.where(mine > 0.5, position, -1.0)
    match = keyed[:, None, :] == jnp.arange(capacity, dtype=jnp.float32)[None, :, None]
    local = (negatives % rows).astype(jnp.float32) + 1.0
    listed = jnp.sum(jnp.where(match, local[:, None, :], 0.0), axis=2) - 1.0
    return listed.astype(jnp.int32)


def most_negatives(negatives, devices, rows):
    owner = negatives // rows
    counts = jnp.sum(
        (owner[:, None, :] == jnp.arange(devices)[None, :, None]).astype(jnp.float32), axis=2
    )
    return jnp.max(counts)


def cost(microseconds):
    return pl.CostEstimate(
        flops=0, bytes_accessed=int(microseconds * 3.6e6), transcendentals=0
    )


def widen(code, width):
    return jnp.concatenate([code] * (width // code.shape[1]), axis=1)


def forward_kernel(half, mp_ref, own_ref, oth_ref, code_ref, start_ref, wi_own, wi_oth, wr_own,
                   wr_oth, outs_ref, outo_ref, ent_ref, upd_ref, rst_ref, cand_ref, rec_ref, pri_ref, end_ref,
                   sq_ref, wi, wr, pre, state, sems):
    me = mp_ref[0]
    other = 1 - me
    copies = [
        pltpu.make_async_copy(wi_own, wi.at[me], sems.at[0]),
        pltpu.make_async_copy(wi_oth, wi.at[other], sems.at[1]),
        pltpu.make_async_copy(wr_own, wr.at[me], sems.at[2]),
        pltpu.make_async_copy(wr_oth, wr.at[other], sems.at[3]),
    ]
    for copy in copies:
        copy.start()
    steps, slots, _ = code_ref.shape
    width = own_ref.shape[1]
    lane = lax.broadcasted_iota(jnp.int32, (slots, width), 1)
    real = lane < half
    ones = (lane >= half) & (lane < half + 3)
    own = own_ref[...]
    oth = oth_ref[...]
    state[...] = start_ref[...]
    copies[0].wait()
    copies[1].wait()
    for side in range(2):
        for gate in range(3):
            value = dot_f32(own, wi[side, gate, me]) + dot_f32(oth, wi[side, gate, other])
            pre[side, gate] = value.reshape(steps, slots, width)
    copies[2].wait()
    copies[3].wait()

    def step(t, sums):
        in_sum, out_sum = sums
        code = code_ref[t]
        keep = widen((code == 1.0).astype(jnp.float32), width)
        live = widen((code > 0.0).astype(jnp.float32), width)
        rows = pl.ds(pl.multiple_of(t * slots, slots), slots)
        for ref in (own_ref, oth_ref):
            entry = jnp.where(real, ref[rows, :].astype(jnp.float32), 0.0)
            in_sum = in_sum + live * entry * entry
        entering = []
        for side in range(2):
            value = keep * state[side].astype(jnp.bfloat16).astype(jnp.float32)
            if side == 0:
                value = jnp.where(ones, 1.0, value)
            value = value.astype(jnp.bfloat16)
            ent_ref[t, :, side * width : (side + 1) * width] = value
            entering.append(value)
        lows = []
        for side in range(2):
            recurrent = [
                dot_f32(entering[0], wr[side, gate, 0]) + dot_f32(entering[1], wr[side, gate, 1])
                for gate in range(3)
            ]
            update = jax.nn.sigmoid(pre[side, 0, t] + recurrent[0])
            reset = jax.nn.sigmoid(pre[side, 1, t] + recurrent[1])
            candidate = jnp.tanh(pre[side, 2, t] + reset * recurrent[2])
            prior = keep * state[side]
            fresh = live * ((1.0 - update) * candidate + update * prior)
            fresh = jnp.where(real, fresh, 0.0)
            upd_ref[side, t] = update
            rst_ref[side, t] = reset
            cand_ref[side, t] = candidate
            rec_ref[side, t] = recurrent[2]
            pri_ref[side, t] = prior
            state[side] = fresh
            low = fresh.astype(jnp.bfloat16)
            out_sum = out_sum + low.astype(jnp.float32) * low.astype(jnp.float32)
            if side == 0:
                low = jnp.where(ones, 1.0, low.astype(jnp.float32)).astype(jnp.bfloat16)
            lows.append(low)
        outs_ref[t] = jnp.where(me == 0, lows[0], lows[1])
        outo_ref[t] = jnp.where(me == 0, lows[1], lows[0])
        return in_sum, out_sum

    zero = jnp.zeros((slots, width), jnp.float32)
    in_sum, out_sum = lax.fori_loop(0, steps, step, (zero, zero))
    end_ref[...] = state[...]
    sq_ref[0] = in_sum
    sq_ref[1] = out_sum


def run_forward(half, block, me, own, oth, codes, start, weights):
    _, blocks, events, width = own.shape
    _, steps, slots, lanes = codes.shape
    f32, low = jnp.float32, jnp.bfloat16
    whole = lambda shape: pl.BlockSpec(shape, lambda i, s: (0,) * len(shape))
    saved = (2, steps, slots, width)
    hidden = (2, slots, width)
    return pl.pallas_call(
        functools.partial(forward_kernel, half),
        grid_spec=pltpu.PrefetchScalarGridSpec(
            num_scalar_prefetch=1,
            grid=(1,),
            in_specs=[
                pl.BlockSpec((None, None, events, width), lambda i, s: (0, block, 0, 0)),
                pl.BlockSpec((None, None, events, width), lambda i, s: (1, block, 0, 0)),
                pl.BlockSpec((None, steps, slots, lanes), lambda i, s: (block, 0, 0, 0)),
                whole(hidden),
            ]
            + [pl.BlockSpec(memory_space=pl.ANY)] * 4,
            out_specs=[whole(saved[1:])] * 2
            + [whole((steps, slots, 2 * width))]
            + [whole(saved)] * 5
            + [whole(hidden)] * 2,
            scratch_shapes=[
                pltpu.VMEM((2, 3, 2, width, width), low),
                pltpu.VMEM((2, 3, 2, width, width), low),
                pltpu.VMEM((2, 3, steps, slots, width), f32),
                pltpu.VMEM(hidden, f32),
                pltpu.SemaphoreType.DMA((4,)),
            ],
        ),
        out_shape=[jax.ShapeDtypeStruct(saved[1:], low)] * 2
        + [jax.ShapeDtypeStruct((steps, slots, 2 * width), low)]
        + [jax.ShapeDtypeStruct(saved, f32)] * 5
        + [jax.ShapeDtypeStruct(hidden, f32)] * 2,
        compiler_params=pltpu.CompilerParams(vmem_limit_bytes=VMEM_LIMIT),
        cost_estimate=cost(18),
        name="forward",
    )(me, own, oth, codes, start, *weights)


def backward_kernel(half, mp_ref, code_ref, from_own, from_oth, upd_ref, rst_ref, cand_ref, rec_ref, pri_ref,
                    last_ref, wi_own, wi_oth, wr_own, wr_oth, gate_own, gate_oth, emb_own, emb_oth,
                    first_ref, wi, wr, gate_ref, state, sems):
    me = mp_ref[0]
    other = 1 - me
    copies = [
        pltpu.make_async_copy(wr_own, wr.at[me], sems.at[0]),
        pltpu.make_async_copy(wr_oth, wr.at[other], sems.at[1]),
        pltpu.make_async_copy(wi_own, wi.at[me], sems.at[2]),
        pltpu.make_async_copy(wi_oth, wi.at[other], sems.at[3]),
    ]
    for copy in copies:
        copy.start()
    steps, slots, _ = code_ref.shape
    width = from_own.shape[-1]
    real = lax.broadcasted_iota(jnp.int32, (slots, width), 1) < half
    state[...] = last_ref[...]
    copies[0].wait()
    copies[1].wait()

    def step(i, carry):
        t = steps - 1 - i
        code = code_ref[t]
        keep = widen((code == 1.0).astype(jnp.float32), width)
        live = widen((code > 0.0).astype(jnp.float32), width)
        gates = []
        direct = []
        for side in range(2):
            toward = jnp.where(me == side, from_own[t], from_oth[t])
            grad = live * (state[side] + toward)
            update, reset = upd_ref[side, t], rst_ref[side, t]
            candidate = cand_ref[side, t]
            grad_update = grad * (pri_ref[side, t] - candidate)
            grad_cand = grad * (1.0 - update) * (1.0 - candidate * candidate)
            grad_reset = grad_cand * rec_ref[side, t]
            values = [
                grad_update * update * (1.0 - update),
                grad_reset * reset * (1.0 - reset),
                grad_cand * reset,
                grad_cand,
            ]
            values = [value.astype(jnp.bfloat16) for value in values]
            for gate in range(4):
                gate_ref[gate, side, t] = values[gate]
            gates.append(values)
            direct.append(grad * update)
        for gate in range(4):
            gate_own[gate, t] = jnp.where(me == 0, gates[0][gate], gates[1][gate])
            gate_oth[gate, t] = jnp.where(me == 0, gates[1][gate], gates[0][gate])
        for into in range(2):
            total = direct[into]
            for side in range(2):
                for gate in range(3):
                    total = total + dot_last(gates[side][gate], wr[side, gate, into])
            state[into] = jnp.where(real, keep * total, 0.0)
        return carry

    lax.fori_loop(0, steps, step, 0)
    first_ref[...] = state[...]
    copies[2].wait()
    copies[3].wait()
    events = steps * slots
    results = []
    for into in range(2):
        total = jnp.zeros((events, width), jnp.float32)
        for side in range(2):
            for gate in range(3):
                grads = gate_ref[3 if gate == 2 else gate, side].reshape(events, width)
                total = total + dot_last(grads, wi[side, gate, into])
        results.append(total.astype(jnp.bfloat16))
    emb_own[...] = jnp.where(me == 0, results[0], results[1])
    emb_oth[...] = jnp.where(me == 0, results[1], results[0])


def run_backward(half, block, me, codes, from_own, from_oth, saved_values, last, weights):
    _, steps, slots, lanes = codes.shape
    width = last.shape[-1]
    f32, low = jnp.float32, jnp.bfloat16
    whole = lambda shape: pl.BlockSpec(shape, lambda i, s: (0,) * len(shape))
    saved = (2, steps, slots, width)
    hidden = (2, slots, width)
    return pl.pallas_call(
        functools.partial(backward_kernel, half),
        grid_spec=pltpu.PrefetchScalarGridSpec(
            num_scalar_prefetch=1,
            grid=(1,),
            in_specs=[pl.BlockSpec((None, steps, slots, lanes), lambda i, s: (block, 0, 0, 0))]
            + [whole(saved[1:])] * 2
            + [whole(saved)] * 5
            + [whole(hidden)]
            + [pl.BlockSpec(memory_space=pl.ANY)] * 4,
            out_specs=[
                whole((4,) + saved[1:]),
                whole((4,) + saved[1:]),
                whole((steps * slots, width)),
                whole((steps * slots, width)),
                whole(hidden),
            ],
            scratch_shapes=[
                pltpu.VMEM((2, 3, 2, width, width), low),
                pltpu.VMEM((2, 3, 2, width, width), low),
                pltpu.VMEM((4,) + saved, low),
                pltpu.VMEM(hidden, f32),
                pltpu.SemaphoreType.DMA((4,)),
            ],
        ),
        out_shape=[
            jax.ShapeDtypeStruct((4,) + saved[1:], low),
            jax.ShapeDtypeStruct((4,) + saved[1:], low),
            jax.ShapeDtypeStruct((steps * slots, width), low),
            jax.ShapeDtypeStruct((steps * slots, width), low),
            jax.ShapeDtypeStruct(hidden, f32),
        ],
        compiler_params=pltpu.CompilerParams(vmem_limit_bytes=VMEM_LIMIT),
        cost_estimate=cost(23),
        name="backward",
    )(me, codes, from_own, from_oth, *saved_values, last, *weights)


def score_kernel(half, mp_ref, inv_ref, out_own, out_oth, want_ref, live_ref, use_ref, tgt_own, tgt_oth,
                 neg_own, neg_oth, grad_ref, to_own, to_oth, stat_ref, scores):
    me = mp_ref[0]
    events, width = out_own.shape
    batch = tgt_own.shape[0]
    devices, capacity, _ = neg_own.shape
    negs = devices * capacity
    cols = batch + negs
    lane = lax.broadcasted_iota(jnp.int32, (16, width), 1)
    row = lax.broadcasted_iota(jnp.int32, (16, width), 0)
    pick = jnp.where(
        row == 0,
        jnp.where(lane == half + 3, 256.0, jnp.where(lane == half + 4, 1.0, 0.0)),
        jnp.where((row == 1) & (lane == half + 5), 1.0, 0.0),
    ).astype(jnp.bfloat16)
    left_own = jnp.concatenate([out_own[...], pick], axis=0)
    left_oth = jnp.concatenate([out_oth[...], pick], axis=0)
    nown = neg_own[...].reshape(negs, width)
    noth = neg_oth[...].reshape(negs, width)
    scores[:, :batch] = dot_last(left_own, tgt_own[...]) + dot_last(left_oth, tgt_oth[...])
    scores[:, batch:] = dot_last(left_own, nown) + dot_last(left_oth, noth)
    ids = scores[events : events + 1, :]
    usable = jnp.concatenate([use_ref[:1, :], scores[events + 1 : events + 2, batch:]], axis=1)
    ids = jnp.where(usable > 0.5, ids, -1.0)
    group = 16
    inv = inv_ref[0]
    base = me * events

    def rows_step(i, stats):
        loss_sum, square_sum = stats
        rows = pl.ds(pl.multiple_of(i * group, group), group)
        s = scores[rows, :]
        want = want_ref[rows, :1]
        live = live_ref[rows, :1]
        allowed = (ids != want) & (usable > 0.5)
        head = s[:, :batch]
        column = lax.broadcasted_iota(jnp.int32, (group, batch), 1)
        place = lax.broadcasted_iota(jnp.int32, (group, batch), 0) + (base + i * group)
        diagonal = column == place
        positive = jnp.sum(jnp.where(diagonal, head, 0.0), axis=1, keepdims=True)
        masked = jnp.where(allowed, s, NEGATIVE_FLOOR)
        top = jnp.max(masked, axis=1, keepdims=True)
        weight = jnp.exp(masked - top)
        normal = jnp.sum(weight, axis=1, keepdims=True)
        gap = positive - s
        tail = jnp.exp(-jnp.abs(gap))
        lift = 1.0 + tail
        joined = jnp.where(allowed, jnp.minimum(s, positive) - jnp.log(lift), NEGATIVE_FLOOR)
        top_joined = jnp.max(joined, axis=1, keepdims=True)
        mass = jnp.exp(joined - top_joined)
        joined_sum = jnp.sum(mass, axis=1, keepdims=True)
        shared = mass / lift
        below = gap >= 0.0
        to_score = shared * jnp.where(below, 1.0, tail)
        to_positive = jnp.sum(shared * jnp.where(below, tail, 1.0), axis=1, keepdims=True)
        square = s * s
        penalty = jnp.sum(weight * square, axis=1, keepdims=True) / normal
        loss = top + jnp.log(normal) - top_joined - jnp.log(joined_sum) + REGULAR * penalty
        scale = live * inv
        grad = (scale / normal) * weight * (
            1.0 + REGULAR * (square + 2.0 * s - penalty)
        ) - (scale / joined_sum) * to_score
        drop = jnp.where(diagonal, scale * to_positive / joined_sum, 0.0)
        grad_ref[rows, :batch] = (grad[:, :batch] - drop).astype(jnp.bfloat16)
        grad_ref[rows, batch:] = grad[:, batch:].astype(jnp.bfloat16)
        loss_sum = loss_sum + live * loss
        square_sum = square_sum + live * jnp.sum(square, axis=1, keepdims=True)
        return loss_sum, square_sum

    zero = jnp.zeros((group, 1), jnp.float32)
    loss_sum, square_sum = lax.fori_loop(0, events // group, rows_step, (zero, zero))
    stat_ref[0] = jnp.broadcast_to(loss_sum[:8] + loss_sum[8:], (8, 128))
    stat_ref[1] = jnp.broadcast_to(square_sum[:8] + square_sum[8:], (8, 128))
    grad_tgt = grad_ref[:, :batch]
    grad_neg = grad_ref[:, batch:]
    real = lax.broadcasted_iota(jnp.int32, (events, width), 1) < half
    total = dot_f32(grad_tgt, tgt_own[...]) + dot_f32(grad_neg, nown)
    to_own[...] = jnp.where(real, total, 0.0)
    total = dot_f32(grad_tgt, tgt_oth[...]) + dot_f32(grad_neg, noth)
    to_oth[...] = jnp.where(real, total, 0.0)


def run_scores(half, block, me, inv, out_own, out_oth, want, live, use, tgt_own, tgt_oth, neg_own,
               neg_oth):
    events, width = out_own.shape
    batch = tgt_own.shape[1]
    devices, _, capacity, _ = neg_own.shape
    cols = batch + devices * capacity
    low, f32 = jnp.bfloat16, jnp.float32
    whole = lambda shape: pl.BlockSpec(shape, lambda i, s: (0,) * len(shape))
    ofblock = lambda shape: pl.BlockSpec((None,) + shape, lambda i, s: (block,) + (0,) * len(shape))
    once = pl.Buffered(1)
    neg = pl.BlockSpec(
        (devices, None, capacity, width), lambda i, s: (0, block, 0, 0), pipeline_mode=once
    )
    return pl.pallas_call(
        functools.partial(score_kernel, half),
        grid_spec=pltpu.PrefetchScalarGridSpec(
            num_scalar_prefetch=1,
            grid=(1,),
            in_specs=[
                pl.BlockSpec(memory_space=pltpu.SMEM),
                whole((events, width)),
                whole((events, width)),
                ofblock((events, 128)),
                ofblock((events, 128)),
                ofblock((8, batch)),
                ofblock((batch, width)),
                ofblock((batch, width)),
                neg,
                neg,
            ],
            out_specs=[
                whole((events, cols)),
                whole((events, width)),
                whole((events, width)),
                whole((2, 8, 128)),
            ],
            scratch_shapes=[pltpu.VMEM((events + 16, cols), f32)],
        ),
        out_shape=[
            jax.ShapeDtypeStruct((events, cols), low),
            jax.ShapeDtypeStruct((events, width), f32),
            jax.ShapeDtypeStruct((events, width), f32),
            jax.ShapeDtypeStruct((2, 8, 128), f32),
        ],
        compiler_params=pltpu.CompilerParams(vmem_limit_bytes=VMEM_LIMIT),
        cost_estimate=cost(22),
        name="scores",
    )(me, inv, out_own, out_oth, want, live, use, tgt_own, tgt_oth, neg_own, neg_oth)


def after(values, *others):
    return lax.optimization_barrier((values, others))[0]


AR_GROUPS = ((0, 2), (1, 3), (4,), (5,))


def unpad_kernel(half, sides_ref, *refs):
    halves, outs = refs[:-2], refs[-2:]
    width = halves[0].shape[0]

    def one_chunk(i, k, chunk):
        kept, came = halves[2 * i], halves[2 * i + 1]
        lanes = slice(k * width, (k + 1) * width)
        for side in range(2):
            value = jnp.where(sides_ref[chunk] == side, kept[:, lanes], came[:, lanes])
            rows = slice(side * half, (side + 1) * half)
            outs[chunk // 3][rows, :] = value.astype(jnp.float32)[:half, :half]

    for i, group in enumerate(AR_GROUPS):
        for k, chunk in enumerate(group):
            pl.when(pl.program_id(0) == chunk % 3)(functools.partial(one_chunk, i, k, chunk))


def unpad(half, sides, halves):
    shape = jax.ShapeDtypeStruct((3, 2 * half, half), jnp.float32)
    vmem = pl.BlockSpec(memory_space=pltpu.VMEM)
    out = pl.BlockSpec((None, 2 * half, half), lambda gate: (gate, 0, 0))
    return pl.pallas_call(
        functools.partial(unpad_kernel, half),
        grid=(3,),
        in_specs=[pl.BlockSpec(memory_space=pltpu.SMEM)] + [vmem] * len(halves),
        out_specs=[out, out],
        out_shape=[shape, shape],
        compiler_params=pltpu.CompilerParams(vmem_limit_bytes=VMEM_LIMIT),
        cost_estimate=cost(8),
        name="unpad",
    )(sides, *halves)


def pair(index, own, oth):
    return jnp.where(index == 0, jnp.stack([own, oth]), jnp.stack([oth, own]))


def reduce_orders(devices):
    bits = devices.bit_length() - 1
    if devices != 1 << bits or bits < 3:
        return None
    rest = list(range(3, bits))
    along, across = [0, 1, 2, *rest], [1, 0, 2, *rest]
    return [along, across] * 3


def flip(values, bit):
    devices = lax.axis_size("dp")
    return lax.ppermute(values, "dp", [(i, i ^ (1 << bit)) for i in range(devices)])


def halve(values, bit):
    place = (lax.axis_index("dp") >> bit) & 1
    size = values.shape[0] // 2
    send = lax.dynamic_slice_in_dim(values, (1 - place) * size, size)
    keep = lax.dynamic_slice_in_dim(values, place * size, size)
    return send, keep


def add_low(left, right):
    return (left.astype(jnp.float32) + right.astype(jnp.float32)).astype(left.dtype)


def scatter_sum(chunks, orders, owner_sums):
    parts = list(chunks)
    for level in range(len(orders[0])):
        if level >= 2:
            arrived = [value.came for value in owner_sums]
            parts = [after(part, arrived) for part in parts]
        sends = []
        for i, order in enumerate(orders):
            send, keep = halve(parts[i], order[level])
            parts[i] = add_low(keep, flip(send, order[level]))
            sends.append(send)
        if level != 1:
            for value in owner_sums:
                value.finish(sends)
                if value.order:
                    value.start()
    while owner_sums and owner_sums[0].order:
        for value in owner_sums:
            value.start()
            value.finish()
    return parts


def gather_sum(parts, orders, sent):
    device = lax.axis_index("dp")
    parts = [jnp.concatenate([parts[i] for i in group], axis=1) for group in AR_GROUPS]
    orders = [orders[group[0]] for group in AR_GROUPS]
    halves = []
    for level in reversed(range(len(orders[0]))):
        if level == 1:
            came_rows = exchange(after(sent, parts))
        for i, order in enumerate(orders):
            bit = (device >> order[level]) & 1
            came = flip(parts[i], order[level])
            if level == 0:
                halves += [parts[i], came]
            else:
                parts[i] = jnp.where(
                    bit == 0,
                    jnp.concatenate([parts[i], came]),
                    jnp.concatenate([came, parts[i]]),
                )
    return halves, came_rows


class OwnerSum:
    def __init__(self, values, order):
        bits = len(order)
        self.order = list(order)
        self.axes = list(reversed(range(bits)))
        self.values = values.reshape((2,) * bits + values.shape[1:])

    def start(self):
        bit = self.order.pop(0)
        axis = self.axes.index(bit)
        place = (lax.axis_index("dp") >> bit) & 1
        send = lax.dynamic_index_in_dim(self.values, 1 - place, axis, keepdims=False)
        self.keep = lax.dynamic_index_in_dim(self.values, place, axis, keepdims=False)
        self.axes.remove(bit)
        self.came = flip(send, bit)
        return send

    def finish(self, *others):
        self.values = add_low(self.keep, after(self.came, *others) if others else self.came)

    def join(self, other):
        self.values = jnp.concatenate([self.values, other.values], axis=-2)


def routed(items, targets, masks, plan, negatives, h_init, emb, w_in, w_rec, b_in, b_rec_n,
           out_table, out_bias, item_list, target_list, item_slot, target_slot, neg_capacity, over):
    f32, low = jnp.float32, jnp.bfloat16
    blocks, steps, all_slots = items.shape
    slots = all_slots // 2
    events = steps * slots
    batch = 2 * events
    half = h_init.shape[1]
    width = roundup(half + 6, 128)
    rows = emb.shape[0]
    devices = lax.axis_size("dp")
    device = lax.axis_index("dp")
    core = lax.axis_index("mp")
    me = core.astype(jnp.int32).reshape(1)
    first_half = (core == 0).astype(f32)
    capacity = item_list.shape[1]
    breadth = 2 * half
    spare = width - half

    def mine(values):
        return lax.dynamic_index_in_dim(values, core, 0, keepdims=False)

    def theirs(values):
        return lax.dynamic_index_in_dim(values, 1 - core, 0, keepdims=False)

    def core_major(values):
        return values.reshape(blocks, steps, 2, slots).transpose(2, 0, 1, 3)

    row_lanes = jnp.concatenate(
        [jnp.ones((rows, 3), f32), jnp.zeros((rows, spare - 3), f32)], axis=1
    )
    emb_wide = jnp.concatenate([emb, (row_lanes * first_half).astype(low)], axis=1)
    ids = device * rows + jnp.arange(rows)
    parts = bf16_parts(out_bias)
    out_lanes = jnp.stack(
        [*parts, (ids // 256).astype(f32), (ids % 256).astype(f32), jnp.ones((rows,), f32)]
        + [jnp.zeros((rows,), f32)] * (spare - 6),
        axis=1,
    )
    out_wide = jnp.concatenate([out_table, (out_lanes * first_half).astype(low)], axis=1)

    own_negatives = plan_negatives(negatives, devices, rows, neg_capacity, device)
    negative_pick = one_hot(own_negatives.reshape(blocks * neg_capacity), rows)
    neg_own = lax.all_gather(
        dot_f32(negative_pick, out_wide).astype(low), "dp", axis=0, tiled=True
    )
    alive = jnp.sum((masks > 0).astype(jnp.int32))
    told = jnp.broadcast_to(jnp.stack([alive, over])[None, :], (devices, 2))
    asking = jnp.concatenate([item_list, target_list, told], axis=1)
    asked = exchange(asking)
    wanted_rows = asked[:, : 2 * capacity]
    count = jnp.sum(asked[:, 2 * capacity]).astype(f32)
    overs = jnp.sum(asked[:, 2 * capacity + 1])
    item_pick = one_hot(wanted_rows[:, :capacity].reshape(devices * capacity), rows)
    target_pick = one_hot(wanted_rows[:, capacity:].reshape(devices * capacity), rows)
    item_send = dot_f32(item_pick, emb_wide).astype(low).reshape(devices, capacity, width)
    w_in, w_rec = after((w_in, w_rec), item_send)
    item_rows = exchange(item_send).reshape(devices * capacity, width)
    target_send = dot_f32(target_pick, out_wide).astype(low).reshape(devices, capacity, width)

    def widened(weight, bias, gate):
        matrix = weight[:, gate, :].reshape(2, half, half)
        matrix = jnp.pad(matrix, ((0, 0), (0, 0), (0, spare)))
        if bias is None:
            extra = jnp.zeros((2, spare, width), low)
        else:
            line = jnp.stack([*bf16_parts(bias)]).astype(low)
            extra = jnp.pad(line[None], ((0, 1), (0, spare - 3), (0, spare)))
        return jnp.concatenate([matrix, extra], axis=1)

    wi_own = jnp.stack([widened(w_in, b_in[gate], gate) for gate in range(3)])
    wr_own = jnp.stack([widened(w_rec, b_rec_n if gate == 2 else None, gate) for gate in range(3)])
    weights = (wi_own, swap_cores(wi_own), wr_own, swap_cores(wr_own))

    start_all = jnp.pad(h_init, ((0, 0), (0, spare))).reshape(2, slots, width)
    start_own = mine(start_all)
    start_oth = swap_cores(lax.dynamic_index_in_dim(start_all, 1 - core, 0, keepdims=False))
    state = pair(core, start_own, start_oth)

    codes_all = core_major(masks)
    codes = mine(codes_all).astype(f32)
    codes_wide = jnp.broadcast_to(codes[..., None], (blocks, steps, slots, 128))
    target_all = core_major(targets).reshape(2, blocks, events)
    want = jnp.broadcast_to(mine(target_all).astype(f32)[..., None], (blocks, events, 128))
    live = (codes_wide > 0.0).astype(f32).reshape(blocks, events, 128)
    use = (codes_all > 0).astype(f32).reshape(2, blocks, events).transpose(1, 0, 2)
    use = jnp.broadcast_to(use.reshape(blocks, 1, batch), (blocks, 8, batch))

    slots_first = item_slot.reshape(2, blocks * events)
    slots_first = jnp.concatenate([mine(slots_first), theirs(slots_first)])
    item_hot = one_hot(slots_first, devices * capacity)
    emb_own = dot_f32(item_hot, item_rows).astype(low)
    emb_oth = swap_cores(emb_own)
    target_rows = exchange(after(target_send, emb_own)).reshape(devices * capacity, width)
    emb_own = emb_own.reshape(2, blocks, events, width)
    emb_oth = emb_oth.reshape(2, blocks, events, width)
    inputs = jnp.concatenate(
        [
            emb_own.reshape(blocks * batch, width),
            jnp.concatenate([emb_oth[1], emb_oth[0]]).reshape(blocks * batch, width),
        ],
        axis=1,
    )

    target_slot_blocks = target_slot.reshape(2, blocks, events).transpose(1, 0, 2)
    target_hot = one_hot(target_slot_blocks.reshape(blocks * batch), devices * capacity)
    tgt_own = dot_f32(target_hot, target_rows).astype(low)
    hop = -(-slots // devices)
    saves = []
    outs = []
    entries = []
    routes = []
    squares = []
    lane_real = (jnp.arange(2 * width) % width < half).astype(f32)
    for block in range(blocks):
        result = run_forward(half, block, me, emb_own, emb_oth, codes_wide, state, weights)
        outs.append([value.reshape(events, width) for value in result[:2]])
        entries.append(result[2].reshape(events, 2 * width))
        saves.append(result[3:8])
        state = result[8]
        squares.append(result[9])
        if block + 1 < blocks:
            going = lax.dynamic_slice_in_dim(plan[block], core * slots, slots, 0)
            aim = going // all_slots
            place = going % all_slots
            order = jnp.arange(slots)
            earlier = (aim[:, None] == aim[None, :]) & (order[:, None] > order[None, :])
            position = aim * hop + jnp.sum(earlier.astype(jnp.int32), axis=1)
            lanes = jnp.arange(2 * width)[None, :]
            flat = state.transpose(1, 0, 2).reshape(slots, 2 * width)
            flat = jnp.where(lanes == half, place.astype(f32)[:, None], flat)
            flat = jnp.where(lanes == half + 1, 1.0, flat).astype(low)
            put = (jnp.arange(devices * hop)[:, None] == position[None, :]).astype(low)
            sent = dot_f32(put, flat).astype(low).reshape(devices, hop, 2 * width)
            sent = after(sent, target_rows)
            came = exchange(sent).reshape(devices * hop, 2 * width)
            both = jnp.concatenate([came, swap_cores(came)], axis=0)
            label = jnp.where(both[:, half + 1] > 0.5, both[:, half].astype(f32), -1.0)
            here = (core * slots + order).astype(f32)
            take = (here[:, None] == label[None, :]).astype(low)
            moved = dot_f32(take, both) * lane_real
            state = moved.reshape(slots, 2, width).transpose(1, 0, 2)
            state = after(state, tgt_own)
            neg_own = after(neg_own, sent)
            outs[block] = after(outs[block], state)
            routes.append((label[: devices * hop], put))

    neg_oth = swap_cores(neg_own)
    tgt_oth = swap_cores(tgt_own).reshape(blocks, batch, width)
    outs[-1] = after(outs[-1], neg_oth, tgt_oth)
    neg_oth = neg_oth.reshape(devices, blocks, neg_capacity, width)
    neg_own = neg_own.reshape(devices, blocks, neg_capacity, width)
    tgt_own = tgt_own.reshape(blocks, batch, width)
    inv = (1.0 / count).reshape(1)
    from_scores = [None] * blocks
    orders = reduce_orders(devices)
    stats = []
    row_grads = [None] * blocks
    gate_own = [None] * blocks
    gate_oth = [None] * blocks
    emb_grads = [None] * blocks
    emb_grads_oth = [None] * blocks
    grad_state = jnp.zeros((2, slots, width), f32)
    grad_pairs = []
    for block in reversed(range(blocks)):
        grad_own, *from_scores[block], stat = run_scores(
            half, block, me, inv, *outs[block], want, live, use, tgt_own, tgt_oth, neg_own, neg_oth
        )
        stats.append(stat)
        grad_pairs.insert(0, (grad_own, swap_cores(grad_own), swap_cores(outs[block][1])))
    negative_grads = [None] * blocks

    for block in range(blocks):
        grad_own, grad_oth, outs_oth = grad_pairs[block]
        value = dot_first(grad_own, outs[block][0]) + dot_first(grad_oth, outs_oth)
        row_grads[block] = value.astype(low)
    negative_grads = jnp.stack(
        [value[batch:].reshape(devices, neg_capacity, width) for value in row_grads], axis=1
    )
    cut = roundup(neg_capacity // 2, 16)
    owner_sums = []
    if orders is not None:
        owner_sums = [
            OwnerSum(negative_grads[:, :, :cut], orders[0]),
            OwnerSum(negative_grads[:, :, cut:], orders[1]),
        ]
        from_scores[-1] = after(from_scores[-1], [value.start() for value in owner_sums])
    target_grads = jnp.concatenate([value[:batch] for value in row_grads], axis=0)
    target_send = dot_first(target_hot, target_grads).astype(low)
    target_came = exchange(target_send.reshape(devices, capacity, width))
    entering = jnp.concatenate(entries, axis=0)
    entering = jnp.concatenate([entering, swap_cores(entering)], axis=0)
    for block in reversed(range(blocks)):
        own, oth, emb_grads[block], emb_oth_grad, grad_state = run_backward(
            half,
            block,
            me,
            codes_wide,
            *[value.reshape(steps, slots, width) for value in from_scores[block]],
            saves[block],
            grad_state,
            weights,
        )
        gate_own[block] = own.reshape(4, events, width)
        gate_oth[block] = swap_cores(oth).reshape(4, events, width)
        emb_grads_oth[block] = swap_cores(emb_oth_grad)
        if block > 0:
            label, put = routes[block - 1]
            flat = grad_state.transpose(1, 0, 2).reshape(slots, 2 * width).astype(low)
            both = jnp.concatenate([flat, swap_cores(flat)], axis=0)
            order = jnp.arange(slots)
            names = jnp.concatenate([core * slots + order, (1 - core) * slots + order]).astype(f32)
            fetch = (label[:, None] == names[None, :]).astype(low)
            home = dot_f32(fetch, both).astype(low).reshape(devices, hop, 2 * width)
            back = exchange(home)
            flat = dot_first(put, back.reshape(devices * hop, 2 * width)) * lane_real
            grad_state = flat.reshape(slots, 2, width).transpose(1, 0, 2)
            if block == 1 and orders is not None:
                for value in owner_sums:
                    value.finish(home)
                grad_state = after(grad_state, [value.start() for value in owner_sums], target_send)

    gates = jnp.concatenate([*gate_own, *gate_oth], axis=1)
    gates = after(gates, target_came)
    chunks = [dot_first(entering, gates[gate]).astype(low) for gate in (0, 1, 2)]
    chunks += [dot_first(inputs, gates[gate]).astype(low) for gate in (0, 1, 3)]
    marker = chunks[-1]
    target_came = after(target_came, marker)
    own_stats = [
        sum(jnp.sum(value[0, :, 0]) for value in stats),
        sum(jnp.sum(value[0]) for value in squares),
        sum(jnp.sum(value[1]) for value in squares),
        sum(jnp.sum(value[1, :, 0]) for value in stats),
    ]
    own_stats = jnp.stack(bf16_parts(jnp.stack(own_stats)))
    own_stats = jnp.pad(own_stats, ((0, capacity - 3), (width - 4, 0)))

    def row_sums():
        item_grads = jnp.concatenate([*emb_grads, *emb_grads_oth], axis=0)
        item_sums = dot_first(item_hot, after(item_grads, marker))
        item_sums = item_sums.reshape(devices, capacity, width) + own_stats
        return item_sums.astype(low)

    if orders is None:
        item_came = exchange(row_sums())
        sums = [lax.psum(chunk, "dp") for chunk in chunks]
        sums = [jnp.concatenate([sums[i] for i in group], axis=1) for group in AR_GROUPS]
        halves = [value for chunk in sums for value in (chunk[:width], chunk[width:])]
        sides = [jnp.zeros((), jnp.int32)] * 6
        negative_sum = lax.psum_scatter(
            negative_grads, "dp", scatter_dimension=0, tiled=True
        ).reshape(blocks * neg_capacity, width)
    else:

        parts = scatter_sum(chunks, orders, owner_sums)
        first, second = [value.values for value in owner_sums]
        negative_sum = jnp.concatenate(
            [first.reshape(blocks, cut, width), second.reshape(blocks, neg_capacity - cut, width)],
            axis=1,
        ).reshape(blocks * neg_capacity, width)
        halves, item_came = gather_sum(parts, orders, row_sums())
        sides = [(device >> order[0]) & 1 for order in orders]
    all_stats = jnp.sum(item_came[:, :3, width - 4 :].astype(f32), axis=(0, 1))
    all_stats = all_stats + swap_cores(all_stats)
    sides = [side.astype(jnp.int32) for side in sides]
    sides = jnp.stack(sides[:3] + [side ^ core.astype(jnp.int32) for side in sides[3:]])

    def first_row(chunk):
        for i, group in enumerate(AR_GROUPS):
            if chunk in group:
                lanes = slice(group.index(chunk) * width, group.index(chunk) * width + half)
                kept, came = halves[2 * i][half, lanes], halves[2 * i + 1][half, lanes]
        return jnp.where(sides[chunk] == 0, kept, came).astype(f32)

    grad_b_in = jnp.stack([first_row(chunk) for chunk in (3, 4, 5)])
    grad_b_rec = first_row(2)
    grad_emb = dot_first(item_pick, item_came.reshape(devices * capacity, width))[:, :half]
    grad_out = dot_first(
        target_pick, target_came.reshape(devices * capacity, width)
    ) + dot_first(negative_pick, negative_sum)
    bias_own = grad_out[:, half]
    grad_out_bias = jnp.where(core == 0, bias_own, swap_cores(bias_own))

    def slots_of(values):
        own = mine(values)
        oth = swap_cores(theirs(values))
        return pair(core, own, oth).reshape(all_slots, width)[:, :half]

    columns = batch + negatives.shape[1]
    return overs, halves, sides, (
        all_stats[0] / count,
        jnp.sqrt(all_stats[1] / (count * breadth)),
        jnp.sqrt(all_stats[2] / (count * breadth)),
        jnp.sqrt(all_stats[3] / (count * columns)),
        slots_of(after(state, marker)),
        slots_of(after(grad_state, marker)),
        grad_emb,
        grad_b_in,
        grad_b_rec,
        grad_out[:, :half],
        grad_out_bias,
    )


def shards(items, targets, masks, plan, negatives, h_init, emb, w_in, w_rec, b_in, b_rec_n,
           out_table, out_bias):
    blocks, steps, all_slots = items.shape
    devices = lax.axis_size("dp")
    rows = emb.shape[0]
    requests = blocks * steps * all_slots
    capacity = max(32, roundup(-(-requests // devices), 16))
    mean = -(-negatives.shape[1] // devices)
    neg_capacity = min(roundup(mean + 4 * math.isqrt(mean), 16), roundup(rows, 16))

    def core_major(values):
        split = values.reshape(blocks, steps, 2, all_slots // 2)
        return split.transpose(2, 0, 1, 3).reshape(requests)

    item_rows, item_slot, item_most = plan_requests(core_major(items), devices, rows, capacity)
    target_rows, target_slot, target_most = plan_requests(
        core_major(targets), devices, rows, capacity
    )
    negative_most = most_negatives(negatives, devices, rows)
    over = (
        (item_most > capacity) | (target_most > capacity) | (negative_most > neg_capacity)
    ).astype(jnp.int32)
    given = (items, targets, masks, plan, negatives, h_init, emb, w_in, w_rec, b_in, b_rec_n,
             out_table, out_bias)
    overs, halves, sides, ready = routed(
        *given, item_rows, target_rows, item_slot, target_slot, neg_capacity, over
    )

    halves, sides, ready = lax.optimization_barrier((halves, sides, ready))

    def finish(halves, sides, ready):
        grad_w_rec, grad_w_in = unpad(h_init.shape[1], sides, halves)
        return (
            *ready[:7],
            grad_w_in.transpose(1, 0, 2),
            grad_w_rec.transpose(1, 0, 2),
            *ready[7:],
        )

    return lax.cond(overs == 0, finish, lambda *unused: general(*given), halves, sides, ready)


def solution(mesh):
    return jax.shard_map(
        shards,
        mesh=mesh,
        in_specs=(
            P(None, None, "dp"),
            P(None, None, "dp"),
            P(None, None, "dp"),
            P(None, "dp"),
            P(),
            P("dp", "mp"),
            P("dp", "mp"),
            P(None, None, "mp"),
            P(None, None, "mp"),
            P(None, "mp"),
            P("mp"),
            P("dp", "mp"),
            P("dp"),
        ),
        out_specs=(
            P(),
            P(),
            P(),
            P(),
            P("dp", "mp"),
            P("dp", "mp"),
            P("dp", "mp"),
            P(None, None, "mp"),
            P(None, None, "mp"),
            P(None, "mp"),
            P("mp"),
            P("dp", "mp"),
            P("dp"),
        ),
        check_vma=False,
    )
```

```python
import functools
import math

import jax
import jax.numpy as jnp
from jax import lax
from jax.experimental import pallas as pl
from jax.experimental.pallas import tpu as pltpu
from jax.sharding import PartitionSpec as P

REGULAR = 1.0
NEGATIVE_FLOOR = -1e30
VMEM_LIMIT = 56 * 1024 * 1024


def bpr_rows(scores, wanted, chosen, usable):
    session_events = scores.shape[0]
    allowed = usable[None, :] & (chosen[None, :] != wanted[:, None])
    positive = jnp.diagonal(scores[:, :session_events])
    top_score = jnp.max(jnp.where(allowed, scores, NEGATIVE_FLOOR), axis=1, keepdims=True)
    weights = jnp.exp(jnp.where(allowed, scores - top_score, NEGATIVE_FLOOR))
    normal = jnp.sum(weights, axis=1, keepdims=True)
    joined = scores + jax.nn.log_sigmoid(positive[:, None] - scores)
    top_joined = jnp.max(jnp.where(allowed, joined, NEGATIVE_FLOOR), axis=1, keepdims=True)
    joined_sum = jnp.sum(
        jnp.exp(jnp.where(allowed, joined - top_joined, NEGATIVE_FLOOR)), axis=1, keepdims=True
    )
    ranking = top_score + jnp.log(normal) - top_joined - jnp.log(joined_sum)
    penalty = jnp.sum(weights / normal * scores * scores, axis=1)
    return ranking[:, 0] + REGULAR * penalty


def gru_cell(gates_in, recurrent, prior, bias_cand, active_sessions):
    update = jax.nn.sigmoid(gates_in[:, 0] + recurrent[:, 0])
    reset = jax.nn.sigmoid(gates_in[:, 1] + recurrent[:, 1])
    candidate = jnp.tanh(gates_in[:, 2] + reset * (recurrent[:, 2] + bias_cand))
    return active_sessions * ((1.0 - update) * candidate + update * prior)


def block_rows(total, row_count):
    return math.gcd(total, 2 ** max(8, 22 - row_count.bit_length()))


def lookup_rows(index, table, row_count):
    total = index.shape[0]
    size = block_rows(total, row_count)

    def one_block(index_block):
        indicator = index_block[:, None] == jnp.arange(row_count, dtype=jnp.int32)[None, :]
        return jnp.dot(indicator.astype(jnp.bfloat16), table, preferred_element_type=jnp.float32)

    picked = lax.map(one_block, index.reshape(total // size, size))
    return picked.reshape(total, table.shape[1])


def sum_rows(index, values, row_count):
    total = index.shape[0]
    breadth = values.shape[1]
    size = block_rows(total, row_count)

    def add_block(accum, pair):
        index_block, value_block = pair
        indicator = index_block[:, None] == jnp.arange(row_count, dtype=jnp.int32)[None, :]
        term = lax.dot_general(
            indicator.astype(jnp.bfloat16),
            value_block,
            (((0,), (0,)), ((), ())),
            preferred_element_type=jnp.float32,
        )
        return (accum + term, None)

    accum, _ = lax.scan(
        add_block,
        jnp.zeros((row_count, breadth), jnp.float32),
        (index.reshape(total // size, size), values.reshape(total // size, size, breadth)),
    )
    return accum


def spread(own_low):
    return lax.all_gather(own_low, "mp", axis=1, tiled=True)


def move_state(state, destination, devices, slots):
    capacity = (slots + devices - 1) // devices
    target_device = destination // slots
    target_slot = destination % slots
    order = jnp.arange(slots)
    earlier = (target_device[:, None] == target_device[None, :]) & (order[:, None] > order[None, :])
    position = target_device * capacity + jnp.sum(earlier.astype(jnp.int32), axis=1)
    outgoing = jnp.zeros((devices * capacity, state.shape[1]), jnp.float32).at[position].set(state)
    labels = jnp.full((devices * capacity,), slots, jnp.int32).at[position].set(target_slot)
    arrived, arrived_labels = (
        lax.all_to_all(
            outgoing.astype(jnp.bfloat16), "dp", split_axis=0, concat_axis=0, tiled=True
        ).astype(outgoing.dtype),
        lax.all_to_all(labels, "dp", split_axis=0, concat_axis=0, tiled=True),
    )
    moved = jnp.zeros_like(state).at[arrived_labels].set(arrived, mode="drop")
    return (moved, arrived_labels, position)


def return_state(grad_start, labels, position, slots):
    inside = labels < slots
    spot = jnp.where(inside, labels, 0)
    returning = jnp.where(inside[:, None], jnp.take(grad_start, spot, axis=0), 0.0)
    back = lax.all_to_all(
        returning.astype(jnp.bfloat16), "dp", split_axis=0, concat_axis=0, tiled=True
    ).astype(returning.dtype)
    return jnp.take(back, position, axis=0)


def general(
    items,
    targets,
    masks,
    plan,
    negatives,
    h_init,
    emb,
    w_in,
    w_rec,
    b_in,
    b_rec_n,
    out_table,
    out_bias,
):
    blocks, steps, slots = items.shape
    halfwidth = h_init.shape[1]
    breadth = w_in.shape[0]
    vocab_rows = emb.shape[0]
    devices = lax.axis_size("dp")
    negs = negatives.shape[1]
    session_events = steps * slots
    columns = session_events + negs
    token_ids = blocks * session_events
    item_ids = items.reshape(token_ids)
    cand_ids = jnp.concatenate([targets.reshape(blocks, session_events), negatives], axis=1)
    flat_cands = cand_ids.reshape(blocks * columns)
    alive_flags = (masks > 0).astype(jnp.float32)
    w_in_flat = w_in.reshape(breadth, 3 * halfwidth)
    w_rec_flat = w_rec.reshape(breadth, 3 * halfwidth)
    cand_rows = jnp.zeros((blocks * columns, halfwidth), jnp.bfloat16)
    cand_bias = jnp.zeros((blocks * columns,), jnp.float32)
    emb_piece = lax.all_gather(emb, "dp", axis=0, tiled=True)
    out_piece = lax.all_gather(out_table, "dp", axis=0, tiled=True)
    bias_piece = lax.all_gather(out_bias.astype(jnp.bfloat16), "dp", axis=0, tiled=True).astype(
        jnp.float32
    )
    row_count = emb_piece.shape[0]
    embedded = lookup_rows(item_ids, emb_piece, row_count)
    shifted = flat_cands
    inside = (shifted >= 0) & (shifted < row_count)
    take_position = jnp.clip(shifted, 0, row_count - 1)
    cand_rows = jnp.where(inside[:, None], jnp.take(out_piece, take_position, axis=0), cand_rows)
    cand_bias = jnp.where(inside, jnp.take(bias_piece, take_position), cand_bias)
    embedded, cand_rows, cand_bias = (embedded, cand_rows, cand_bias)
    inputs_full, cand_full = (
        lax.all_gather(embedded.astype(jnp.bfloat16), "mp", axis=1, tiled=True),
        lax.all_gather(cand_rows, "mp", axis=1, tiled=True),
    )
    preacts = jnp.dot(inputs_full, w_in_flat, preferred_element_type=jnp.float32)
    preacts = preacts.reshape(blocks, steps, slots, 3, halfwidth) + b_in

    def advance(carry_pair, step_inputs):
        prior, prior_low = carry_pair
        gates_in, codes = step_inputs
        keeping = (codes == 1).astype(jnp.float32)[:, None]
        active_sessions = (codes > 0).astype(jnp.float32)[:, None]
        entering = prior_low * keeping.astype(jnp.bfloat16)
        recurrent = jnp.dot(entering, w_rec_flat, preferred_element_type=jnp.float32).reshape(
            slots, 3, halfwidth
        )
        fresh = gru_cell(gates_in, recurrent, prior * keeping, b_rec_n, active_sessions)
        fresh_own = fresh.astype(jnp.bfloat16)
        fresh_low = spread(fresh_own)
        return ((fresh, fresh_low), (prior, prior_low, recurrent, fresh_low, fresh_own))

    state = h_init
    state_low = spread(h_init.astype(jnp.bfloat16))
    records = []
    routes = []
    for event_block in range(blocks):
        (state, state_low), record = lax.scan(
            advance, (state, state_low), (preacts[event_block], masks[event_block])
        )
        records.append(record)
        if event_block + 1 < blocks:
            state, labels, position = move_state(state, plan[event_block], devices, slots)
            routes.append((labels, position))
            state_low = spread(state.astype(jnp.bfloat16))
    loss_total_sum = jnp.zeros((), jnp.float32)
    score_squared = jnp.zeros((), jnp.float32)
    hidden_squared = jnp.zeros((), jnp.float32)
    score_list = []
    for event_block in range(blocks):
        outputs = records[event_block][3].reshape(session_events, breadth)
        candidates = cand_full[event_block * columns : (event_block + 1) * columns]
        scores = lax.dot_general(
            outputs, candidates, (((1,), (1,)), ((), ())), preferred_element_type=jnp.float32
        )
        scores = scores + cand_bias[event_block * columns : (event_block + 1) * columns]
        active_sessions = alive_flags[event_block].reshape(session_events)
        usable = jnp.concatenate([active_sessions > 0, jnp.ones((negs,), dtype=bool)])
        losses = bpr_rows(
            scores, targets[event_block].reshape(session_events), cand_ids[event_block], usable
        )
        loss_total_sum = loss_total_sum + jnp.sum(active_sessions * losses)
        score_squared = score_squared + jnp.sum(active_sessions * jnp.sum(scores * scores, axis=1))
        output_values = outputs.astype(jnp.float32)
        hidden_squared = hidden_squared + jnp.sum(
            active_sessions[:, None] * output_values * output_values
        )
        score_list.append(scores)
    input_entries = inputs_full.astype(jnp.float32)
    input_squared = jnp.sum(alive_flags.reshape(token_ids)[:, None] * input_entries * input_entries)
    count_all, loss_all, input_all, hidden_all, score_all = lax.psum(
        (jnp.sum(alive_flags), loss_total_sum, input_squared, hidden_squared, score_squared), "dp"
    )
    loss = loss_all / count_all
    rms_inputs = jnp.sqrt(input_all / (count_all * breadth))
    rms_hidden = jnp.sqrt(hidden_all / (count_all * breadth))
    rms_scores = jnp.sqrt(score_all / (count_all * columns))
    from_scores = []
    row_grads = []
    bias_grads = []
    for event_block in range(blocks):
        active_sessions = alive_flags[event_block].reshape(session_events)
        usable = jnp.concatenate([active_sessions > 0, jnp.ones((negs,), dtype=bool)])
        wanted = targets[event_block].reshape(session_events)
        chosen = cand_ids[event_block]

        def block_loss(scores_arg):
            return jnp.sum(active_sessions * bpr_rows(scores_arg, wanted, chosen, usable))

        _, pullback = jax.vjp(block_loss, score_list[event_block])
        (grad_scores,) = pullback(jnp.ones((), jnp.float32) / count_all)
        bias_grads.append(jnp.sum(grad_scores, axis=0))
        scores_low = grad_scores.astype(jnp.bfloat16)
        own_rows = cand_rows[event_block * columns : (event_block + 1) * columns]
        to_outputs = jnp.dot(scores_low, own_rows, preferred_element_type=jnp.float32)
        from_scores.append(to_outputs.reshape(steps, slots, halfwidth))
        own_outputs = records[event_block][4].reshape(session_events, halfwidth)
        row_grads.append(
            lax.dot_general(
                scores_low,
                own_outputs,
                (((0,), (0,)), ((), ())),
                preferred_element_type=jnp.float32,
            )
        )
    cand_row_grads = jnp.concatenate(row_grads, axis=0)
    cand_bias_grads = jnp.concatenate(bias_grads, axis=0)

    def retreat(carry_triple, saved):
        grad_state, grad_rec_w, grad_bias_cand = carry_triple
        prior, prior_low, recurrent, gates_in, codes, from_output = saved
        grad_state = grad_state + from_output
        keeping = (codes == 1).astype(jnp.float32)[:, None]
        active_sessions = (codes > 0).astype(jnp.float32)[:, None]
        _, cell_pull = jax.vjp(
            lambda gate_arg, rec_arg, prior_arg, bias_arg: gru_cell(
                gate_arg, rec_arg, prior_arg, bias_arg, active_sessions
            ),
            gates_in,
            recurrent,
            prior * keeping,
            b_rec_n,
        )
        grad_gates, grad_rec, grad_prior, grad_bias = cell_pull(grad_state)
        rec_low = grad_rec.reshape(slots, 3 * halfwidth).astype(jnp.bfloat16)
        partial_sum = lax.dot_general(
            rec_low, w_rec_flat, (((1,), (1,)), ((), ())), preferred_element_type=jnp.float32
        )
        through_rec = lax.psum_scatter(
            partial_sum.astype(jnp.bfloat16), "mp", scatter_dimension=1, tiled=True
        ).astype(jnp.float32)
        entering = prior_low * keeping.astype(jnp.bfloat16)
        grad_rec_w = grad_rec_w + lax.dot_general(
            entering, rec_low, (((0,), (0,)), ((), ())), preferred_element_type=jnp.float32
        )
        previous = keeping * (grad_prior + through_rec)
        return ((previous, grad_rec_w, grad_bias_cand + grad_bias), grad_gates)

    grad_state = jnp.zeros((slots, halfwidth), jnp.float32)
    grad_rec_w = jnp.zeros((breadth, 3 * halfwidth), jnp.float32)
    grad_bias_cand = jnp.zeros((halfwidth,), jnp.float32)
    pre_grads = [None] * blocks
    for event_block in reversed(range(blocks)):
        prior_all, prior_low_all, recurrent_all, _, _ = records[event_block]
        (grad_state, grad_rec_w, grad_bias_cand), grad_pre = lax.scan(
            retreat,
            (grad_state, grad_rec_w, grad_bias_cand),
            (
                prior_all,
                prior_low_all,
                recurrent_all,
                preacts[event_block],
                masks[event_block],
                from_scores[event_block],
            ),
            reverse=True,
        )
        pre_grads[event_block] = grad_pre
        if event_block > 0:
            grad_state = return_state(
                grad_state, routes[event_block - 1][0], routes[event_block - 1][1], slots
            )
    pre_all = jnp.stack(pre_grads)
    grad_bias_in = jnp.sum(pre_all, axis=(0, 1, 2))
    pre_low = pre_all.reshape(token_ids, 3 * halfwidth).astype(jnp.bfloat16)
    grad_w_in = lax.dot_general(
        inputs_full, pre_low, (((0,), (0,)), ((), ())), preferred_element_type=jnp.float32
    )
    input_part = lax.dot_general(
        pre_low, w_in_flat, (((1,), (1,)), ((), ())), preferred_element_type=jnp.float32
    )
    grad_inputs = lax.psum_scatter(
        input_part.astype(jnp.bfloat16), "mp", scatter_dimension=1, tiled=True
    )
    bias_term = jnp.zeros((vocab_rows * devices,), jnp.float32).at[flat_cands].add(cand_bias_grads)
    weight_count = breadth * 3 * halfwidth
    packed_grads = jnp.concatenate(
        [
            grad_w_in.reshape(weight_count),
            grad_rec_w.reshape(weight_count),
            grad_bias_in.reshape(3 * halfwidth),
            grad_bias_cand,
        ]
    )
    packed_length = packed_grads.shape[0]
    padded_length = -(-packed_length // devices) * devices
    packed_grads = jnp.pad(packed_grads, (0, padded_length - packed_length))
    own_share, grad_out_bias = (
        lax.psum_scatter(packed_grads, "dp", scatter_dimension=0, tiled=True),
        lax.psum_scatter(bias_term, "dp", scatter_dimension=0, tiled=True),
    )
    summed_all = lax.all_gather(own_share.astype(jnp.bfloat16), "dp", axis=0, tiled=True).astype(
        own_share.dtype
    )
    summed_w_in = summed_all[:weight_count]
    summed_w_rec = summed_all[weight_count : 2 * weight_count]
    summed_b_in = summed_all[2 * weight_count : 2 * weight_count + 3 * halfwidth].reshape(
        3, halfwidth
    )
    summed_b_cand = summed_all[2 * weight_count + 3 * halfwidth : 2 * weight_count + 4 * halfwidth]
    shifted = flat_cands
    inside = (shifted >= 0) & (shifted < lax.axis_size("dp") * vocab_rows)
    position = jnp.where(inside, shifted, lax.axis_size("dp") * vocab_rows)
    both = lax.psum_scatter(
        jnp.concatenate(
            [
                sum_rows(item_ids, grad_inputs, lax.axis_size("dp") * vocab_rows),
                jnp.zeros((lax.axis_size("dp") * vocab_rows, halfwidth), jnp.float32)
                .at[position]
                .add(cand_row_grads, mode="drop"),
            ],
            axis=1,
        ),
        "dp",
        scatter_dimension=0,
        tiled=True,
    )
    grad_emb = both[:, :halfwidth]
    grad_out_table = both[:, halfwidth:]
    return (
        loss,
        rms_inputs,
        rms_hidden,
        rms_scores,
        state,
        grad_state,
        grad_emb,
        summed_w_in.reshape(breadth, 3, halfwidth),
        summed_w_rec.reshape(breadth, 3, halfwidth),
        summed_b_in,
        summed_b_cand,
        grad_out_table,
        grad_out_bias,
    )


def roundup(value, unit):
    return -(-value // unit) * unit


def bf16_parts(values):
    first = lax.reduce_precision(values, 8, 7)
    second = lax.reduce_precision(values - first, 8, 7)
    third = lax.reduce_precision(values - first - second, 8, 7)
    return first, second, third


def one_hot(index, size):
    return (index[:, None] == jnp.arange(size, dtype=index.dtype)[None, :]).astype(jnp.bfloat16)


def dot_f32(left, right):
    return jnp.dot(left, right, preferred_element_type=jnp.float32)


def dot_first(left, right):
    return lax.dot_general(
        left, right, (((0,), (0,)), ((), ())), preferred_element_type=jnp.float32
    )


def dot_last(left, right):
    return lax.dot_general(
        left, right, (((1,), (1,)), ((), ())), preferred_element_type=jnp.float32
    )


def swap_cores(values):
    return lax.ppermute(values, "mp", [(0, 1), (1, 0)])


def exchange(values):
    return lax.all_to_all(values, "dp", split_axis=0, concat_axis=0, tiled=True)


def plan_requests(ids, devices, rows, capacity):
    owner = ids // rows
    owners = one_hot(owner, devices)
    local = one_hot(ids % rows, rows)
    wanted = dot_first(owners, local) > 0.5
    order = jnp.arange(rows)
    before = (order[:, None] < order[None, :]).astype(jnp.bfloat16)
    position = dot_f32(wanted.astype(jnp.bfloat16), before)
    longest = jnp.max(jnp.sum(wanted.astype(jnp.float32), axis=1))
    spots = jnp.sum(
        owners.astype(jnp.float32) * dot_last(local, position.astype(jnp.bfloat16)), axis=1
    )
    slot = owner * capacity + spots.astype(jnp.int32)
    keyed = jnp.where(wanted, position, -1.0)
    match = keyed[:, None, :] == jnp.arange(capacity, dtype=jnp.float32)[None, :, None]
    listed = jnp.sum(jnp.where(match, order.astype(jnp.float32) + 1.0, 0.0), axis=2) - 1.0
    return listed.astype(jnp.int32), slot, longest


def plan_negatives(negatives, devices, rows, capacity, device):
    blocks, negs = negatives.shape
    chunk = math.gcd(negs, 128)
    owner = negatives // rows
    mine = (owner == device).astype(jnp.float32)
    grouped = mine.reshape(blocks * (negs // chunk), chunk)
    order = jnp.arange(chunk)
    before = (order[:, None] < order[None, :]).astype(jnp.bfloat16)
    inner = dot_f32(grouped.astype(jnp.bfloat16), before).reshape(blocks, negs // chunk, chunk)
    totals = jnp.sum(grouped, axis=1).reshape(blocks, negs // chunk)
    group = jnp.arange(negs // chunk)
    outer = jnp.sum(
        jnp.where(group[None, :, None] > group[None, None, :], totals[:, None, :], 0.0), axis=2
    )
    position = (inner + outer[:, :, None]).reshape(blocks, negs)
    keyed = jnp.where(mine > 0.5, position, -1.0)
    match = keyed[:, None, :] == jnp.arange(capacity, dtype=jnp.float32)[None, :, None]
    local = (negatives % rows).astype(jnp.float32) + 1.0
    listed = jnp.sum(jnp.where(match, local[:, None, :], 0.0), axis=2) - 1.0
    return listed.astype(jnp.int32)


def most_negatives(negatives, devices, rows):
    owner = negatives // rows
    counts = jnp.sum(
        (owner[:, None, :] == jnp.arange(devices)[None, :, None]).astype(jnp.float32), axis=2
    )
    return jnp.max(counts)


def cost(microseconds):
    return pl.CostEstimate(
        flops=0, bytes_accessed=int(microseconds * 3.6e6), transcendentals=0
    )


def widen(code, width):
    return jnp.concatenate([code] * (width // code.shape[1]), axis=1)


def forward_kernel(half, mp_ref, own_ref, oth_ref, code_ref, start_ref, wi_own, wi_oth, wr_own,
                   wr_oth, outs_ref, outo_ref, ent_ref, upd_ref, rst_ref, cand_ref, rec_ref, pri_ref, end_ref,
                   sq_ref, wi, wr, pre, state, sems):
    me = mp_ref[0]
    other = 1 - me
    copies = [
        pltpu.make_async_copy(wi_own, wi.at[me], sems.at[0]),
        pltpu.make_async_copy(wi_oth, wi.at[other], sems.at[1]),
        pltpu.make_async_copy(wr_own, wr.at[me], sems.at[2]),
        pltpu.make_async_copy(wr_oth, wr.at[other], sems.at[3]),
    ]
    for copy in copies:
        copy.start()
    steps, slots, _ = code_ref.shape
    width = own_ref.shape[1]
    lane = lax.broadcasted_iota(jnp.int32, (slots, width), 1)
    real = lane < half
    ones = (lane >= half) & (lane < half + 3)
    own = own_ref[...]
    oth = oth_ref[...]
    state[...] = start_ref[...]
    copies[0].wait()
    copies[1].wait()
    for side in range(2):
        for gate in range(3):
            value = dot_f32(own, wi[side, gate, me]) + dot_f32(oth, wi[side, gate, other])
            pre[side, gate] = value.reshape(steps, slots, width)
    copies[2].wait()
    copies[3].wait()

    def step(t, sums):
        in_sum, out_sum = sums
        code = code_ref[t]
        keep = widen((code == 1.0).astype(jnp.float32), width)
        live = widen((code > 0.0).astype(jnp.float32), width)
        rows = pl.ds(pl.multiple_of(t * slots, slots), slots)
        for ref in (own_ref, oth_ref):
            entry = jnp.where(real, ref[rows, :].astype(jnp.float32), 0.0)
            in_sum = in_sum + live * entry * entry
        entering = []
        for side in range(2):
            value = keep * state[side].astype(jnp.bfloat16).astype(jnp.float32)
            if side == 0:
                value = jnp.where(ones, 1.0, value)
            value = value.astype(jnp.bfloat16)
            ent_ref[t, :, side * width : (side + 1) * width] = value
            entering.append(value)
        lows = []
        for side in range(2):
            recurrent = [
                dot_f32(entering[0], wr[side, gate, 0]) + dot_f32(entering[1], wr[side, gate, 1])
                for gate in range(3)
            ]
            update = jax.nn.sigmoid(pre[side, 0, t] + recurrent[0])
            reset = jax.nn.sigmoid(pre[side, 1, t] + recurrent[1])
            candidate = jnp.tanh(pre[side, 2, t] + reset * recurrent[2])
            prior = keep * state[side]
            fresh = live * ((1.0 - update) * candidate + update * prior)
            fresh = jnp.where(real, fresh, 0.0)
            upd_ref[side, t] = update
            rst_ref[side, t] = reset
            cand_ref[side, t] = candidate
            rec_ref[side, t] = recurrent[2]
            pri_ref[side, t] = prior
            state[side] = fresh
            low = fresh.astype(jnp.bfloat16)
            out_sum = out_sum + low.astype(jnp.float32) * low.astype(jnp.float32)
            if side == 0:
                low = jnp.where(ones, 1.0, low.astype(jnp.float32)).astype(jnp.bfloat16)
            lows.append(low)
        outs_ref[t] = jnp.where(me == 0, lows[0], lows[1])
        outo_ref[t] = jnp.where(me == 0, lows[1], lows[0])
        return in_sum, out_sum

    zero = jnp.zeros((slots, width), jnp.float32)
    in_sum, out_sum = lax.fori_loop(0, steps, step, (zero, zero))
    end_ref[...] = state[...]
    sq_ref[0] = in_sum
    sq_ref[1] = out_sum


def run_forward(half, block, me, own, oth, codes, start, weights):
    _, blocks, events, width = own.shape
    _, steps, slots, lanes = codes.shape
    f32, low = jnp.float32, jnp.bfloat16
    whole = lambda shape: pl.BlockSpec(shape, lambda i, s: (0,) * len(shape))
    saved = (2, steps, slots, width)
    hidden = (2, slots, width)
    return pl.pallas_call(
        functools.partial(forward_kernel, half),
        grid_spec=pltpu.PrefetchScalarGridSpec(
            num_scalar_prefetch=1,
            grid=(1,),
            in_specs=[
                pl.BlockSpec((None, None, events, width), lambda i, s: (0, block, 0, 0)),
                pl.BlockSpec((None, None, events, width), lambda i, s: (1, block, 0, 0)),
                pl.BlockSpec((None, steps, slots, lanes), lambda i, s: (block, 0, 0, 0)),
                whole(hidden),
            ]
            + [pl.BlockSpec(memory_space=pl.ANY)] * 4,
            out_specs=[whole(saved[1:])] * 2
            + [whole((steps, slots, 2 * width))]
            + [whole(saved)] * 5
            + [whole(hidden)] * 2,
            scratch_shapes=[
                pltpu.VMEM((2, 3, 2, width, width), low),
                pltpu.VMEM((2, 3, 2, width, width), low),
                pltpu.VMEM((2, 3, steps, slots, width), f32),
                pltpu.VMEM(hidden, f32),
                pltpu.SemaphoreType.DMA((4,)),
            ],
        ),
        out_shape=[jax.ShapeDtypeStruct(saved[1:], low)] * 2
        + [jax.ShapeDtypeStruct((steps, slots, 2 * width), low)]
        + [jax.ShapeDtypeStruct(saved, f32)] * 5
        + [jax.ShapeDtypeStruct(hidden, f32)] * 2,
        compiler_params=pltpu.CompilerParams(vmem_limit_bytes=VMEM_LIMIT),
        cost_estimate=cost(18),
        name="forward",
    )(me, own, oth, codes, start, *weights)


def backward_kernel(half, mp_ref, code_ref, from_own, from_oth, upd_ref, rst_ref, cand_ref, rec_ref, pri_ref,
                    last_ref, wi_own, wi_oth, wr_own, wr_oth, gate_own, gate_oth, emb_own, emb_oth,
                    first_ref, wi, wr, gate_ref, state, sems):
    me = mp_ref[0]
    other = 1 - me
    copies = [
        pltpu.make_async_copy(wr_own, wr.at[me], sems.at[0]),
        pltpu.make_async_copy(wr_oth, wr.at[other], sems.at[1]),
        pltpu.make_async_copy(wi_own, wi.at[me], sems.at[2]),
        pltpu.make_async_copy(wi_oth, wi.at[other], sems.at[3]),
    ]
    for copy in copies:
        copy.start()
    steps, slots, _ = code_ref.shape
    width = from_own.shape[-1]
    real = lax.broadcasted_iota(jnp.int32, (slots, width), 1) < half
    state[...] = last_ref[...]
    copies[0].wait()
    copies[1].wait()

    def step(i, carry):
        t = steps - 1 - i
        code = code_ref[t]
        keep = widen((code == 1.0).astype(jnp.float32), width)
        live = widen((code > 0.0).astype(jnp.float32), width)
        gates = []
        direct = []
        for side in range(2):
            toward = jnp.where(me == side, from_own[t], from_oth[t])
            grad = live * (state[side] + toward)
            update, reset = upd_ref[side, t], rst_ref[side, t]
            candidate = cand_ref[side, t]
            grad_update = grad * (pri_ref[side, t] - candidate)
            grad_cand = grad * (1.0 - update) * (1.0 - candidate * candidate)
            grad_reset = grad_cand * rec_ref[side, t]
            values = [
                grad_update * update * (1.0 - update),
                grad_reset * reset * (1.0 - reset),
                grad_cand * reset,
                grad_cand,
            ]
            values = [value.astype(jnp.bfloat16) for value in values]
            for gate in range(4):
                gate_ref[gate, side, t] = values[gate]
            gates.append(values)
            direct.append(grad * update)
        for gate in range(4):
            gate_own[gate, t] = jnp.where(me == 0, gates[0][gate], gates[1][gate])
            gate_oth[gate, t] = jnp.where(me == 0, gates[1][gate], gates[0][gate])
        for into in range(2):
            total = direct[into]
            for side in range(2):
                for gate in range(3):
                    total = total + dot_last(gates[side][gate], wr[side, gate, into])
            state[into] = jnp.where(real, keep * total, 0.0)
        return carry

    lax.fori_loop(0, steps, step, 0)
    first_ref[...] = state[...]
    copies[2].wait()
    copies[3].wait()
    events = steps * slots
    results = []
    for into in range(2):
        total = jnp.zeros((events, width), jnp.float32)
        for side in range(2):
            for gate in range(3):
                grads = gate_ref[3 if gate == 2 else gate, side].reshape(events, width)
                total = total + dot_last(grads, wi[side, gate, into])
        results.append(total.astype(jnp.bfloat16))
    emb_own[...] = jnp.where(me == 0, results[0], results[1])
    emb_oth[...] = jnp.where(me == 0, results[1], results[0])


def run_backward(half, block, me, codes, from_own, from_oth, saved_values, last, weights):
    _, steps, slots, lanes = codes.shape
    width = last.shape[-1]
    f32, low = jnp.float32, jnp.bfloat16
    whole = lambda shape: pl.BlockSpec(shape, lambda i, s: (0,) * len(shape))
    saved = (2, steps, slots, width)
    hidden = (2, slots, width)
    return pl.pallas_call(
        functools.partial(backward_kernel, half),
        grid_spec=pltpu.PrefetchScalarGridSpec(
            num_scalar_prefetch=1,
            grid=(1,),
            in_specs=[pl.BlockSpec((None, steps, slots, lanes), lambda i, s: (block, 0, 0, 0))]
            + [whole(saved[1:])] * 2
            + [whole(saved)] * 5
            + [whole(hidden)]
            + [pl.BlockSpec(memory_space=pl.ANY)] * 4,
            out_specs=[
                whole((4,) + saved[1:]),
                whole((4,) + saved[1:]),
                whole((steps * slots, width)),
                whole((steps * slots, width)),
                whole(hidden),
            ],
            scratch_shapes=[
                pltpu.VMEM((2, 3, 2, width, width), low),
                pltpu.VMEM((2, 3, 2, width, width), low),
                pltpu.VMEM((4,) + saved, low),
                pltpu.VMEM(hidden, f32),
                pltpu.SemaphoreType.DMA((4,)),
            ],
        ),
        out_shape=[
            jax.ShapeDtypeStruct((4,) + saved[1:], low),
            jax.ShapeDtypeStruct((4,) + saved[1:], low),
            jax.ShapeDtypeStruct((steps * slots, width), low),
            jax.ShapeDtypeStruct((steps * slots, width), low),
            jax.ShapeDtypeStruct(hidden, f32),
        ],
        compiler_params=pltpu.CompilerParams(vmem_limit_bytes=VMEM_LIMIT),
        cost_estimate=cost(23),
        name="backward",
    )(me, codes, from_own, from_oth, *saved_values, last, *weights)


def score_kernel(half, mp_ref, inv_ref, out_own, out_oth, want_ref, live_ref, use_ref, tgt_own, tgt_oth,
                 neg_own, neg_oth, grad_ref, to_own, to_oth, stat_ref, scores):
    me = mp_ref[0]
    events, width = out_own.shape
    batch = tgt_own.shape[0]
    devices, capacity, _ = neg_own.shape
    negs = devices * capacity
    cols = batch + negs
    lane = lax.broadcasted_iota(jnp.int32, (16, width), 1)
    row = lax.broadcasted_iota(jnp.int32, (16, width), 0)
    pick = jnp.where(
        row == 0,
        jnp.where(lane == half + 3, 256.0, jnp.where(lane == half + 4, 1.0, 0.0)),
        jnp.where((row == 1) & (lane == half + 5), 1.0, 0.0),
    ).astype(jnp.bfloat16)
    left_own = jnp.concatenate([out_own[...], pick], axis=0)
    left_oth = jnp.concatenate([out_oth[...], pick], axis=0)
    nown = neg_own[...].reshape(negs, width)
    noth = neg_oth[...].reshape(negs, width)
    scores[:, :batch] = dot_last(left_own, tgt_own[...]) + dot_last(left_oth, tgt_oth[...])
    scores[:, batch:] = dot_last(left_own, nown) + dot_last(left_oth, noth)
    ids = scores[events : events + 1, :]
    usable = jnp.concatenate([use_ref[:1, :], scores[events + 1 : events + 2, batch:]], axis=1)
    ids = jnp.where(usable > 0.5, ids, -1.0)
    group = 16
    inv = inv_ref[0]
    base = me * events

    def rows_step(i, stats):
        loss_sum, square_sum = stats
        rows = pl.ds(pl.multiple_of(i * group, group), group)
        s = scores[rows, :]
        want = want_ref[rows, :1]
        live = live_ref[rows, :1]
        allowed = (ids != want) & (usable > 0.5)
        head = s[:, :batch]
        column = lax.broadcasted_iota(jnp.int32, (group, batch), 1)
        place = lax.broadcasted_iota(jnp.int32, (group, batch), 0) + (base + i * group)
        diagonal = column == place
        positive = jnp.sum(jnp.where(diagonal, head, 0.0), axis=1, keepdims=True)
        masked = jnp.where(allowed, s, NEGATIVE_FLOOR)
        top = jnp.max(masked, axis=1, keepdims=True)
        weight = jnp.exp(masked - top)
        normal = jnp.sum(weight, axis=1, keepdims=True)
        gap = positive - s
        tail = jnp.exp(-jnp.abs(gap))
        lift = 1.0 + tail
        joined = jnp.where(allowed, jnp.minimum(s, positive) - jnp.log(lift), NEGATIVE_FLOOR)
        top_joined = jnp.max(joined, axis=1, keepdims=True)
        mass = jnp.exp(joined - top_joined)
        joined_sum = jnp.sum(mass, axis=1, keepdims=True)
        shared = mass / lift
        below = gap >= 0.0
        to_score = shared * jnp.where(below, 1.0, tail)
        to_positive = jnp.sum(shared * jnp.where(below, tail, 1.0), axis=1, keepdims=True)
        square = s * s
        penalty = jnp.sum(weight * square, axis=1, keepdims=True) / normal
        loss = top + jnp.log(normal) - top_joined - jnp.log(joined_sum) + REGULAR * penalty
        scale = live * inv
        grad = (scale / normal) * weight * (
            1.0 + REGULAR * (square + 2.0 * s - penalty)
        ) - (scale / joined_sum) * to_score
        drop = jnp.where(diagonal, scale * to_positive / joined_sum, 0.0)
        grad_ref[rows, :batch] = (grad[:, :batch] - drop).astype(jnp.bfloat16)
        grad_ref[rows, batch:] = grad[:, batch:].astype(jnp.bfloat16)
        loss_sum = loss_sum + live * loss
        square_sum = square_sum + live * jnp.sum(square, axis=1, keepdims=True)
        return loss_sum, square_sum

    zero = jnp.zeros((group, 1), jnp.float32)
    loss_sum, square_sum = lax.fori_loop(0, events // group, rows_step, (zero, zero))
    stat_ref[0] = jnp.broadcast_to(loss_sum[:8] + loss_sum[8:], (8, 128))
    stat_ref[1] = jnp.broadcast_to(square_sum[:8] + square_sum[8:], (8, 128))
    grad_tgt = grad_ref[:, :batch]
    grad_neg = grad_ref[:, batch:]
    real = lax.broadcasted_iota(jnp.int32, (events, width), 1) < half
    total = dot_f32(grad_tgt, tgt_own[...]) + dot_f32(grad_neg, nown)
    to_own[...] = jnp.where(real, total, 0.0)
    total = dot_f32(grad_tgt, tgt_oth[...]) + dot_f32(grad_neg, noth)
    to_oth[...] = jnp.where(real, total, 0.0)


def run_scores(half, block, me, inv, out_own, out_oth, want, live, use, tgt_own, tgt_oth, neg_own,
               neg_oth):
    events, width = out_own.shape
    batch = tgt_own.shape[1]
    devices, _, capacity, _ = neg_own.shape
    cols = batch + devices * capacity
    low, f32 = jnp.bfloat16, jnp.float32
    whole = lambda shape: pl.BlockSpec(shape, lambda i, s: (0,) * len(shape))
    ofblock = lambda shape: pl.BlockSpec((None,) + shape, lambda i, s: (block,) + (0,) * len(shape))
    once = pl.Buffered(1)
    neg = pl.BlockSpec(
        (devices, None, capacity, width), lambda i, s: (0, block, 0, 0), pipeline_mode=once
    )
    return pl.pallas_call(
        functools.partial(score_kernel, half),
        grid_spec=pltpu.PrefetchScalarGridSpec(
            num_scalar_prefetch=1,
            grid=(1,),
            in_specs=[
                pl.BlockSpec(memory_space=pltpu.SMEM),
                whole((events, width)),
                whole((events, width)),
                ofblock((events, 128)),
                ofblock((events, 128)),
                ofblock((8, batch)),
                ofblock((batch, width)),
                ofblock((batch, width)),
                neg,
                neg,
            ],
            out_specs=[
                whole((events, cols)),
                whole((events, width)),
                whole((events, width)),
                whole((2, 8, 128)),
            ],
            scratch_shapes=[pltpu.VMEM((events + 16, cols), f32)],
        ),
        out_shape=[
            jax.ShapeDtypeStruct((events, cols), low),
            jax.ShapeDtypeStruct((events, width), f32),
            jax.ShapeDtypeStruct((events, width), f32),
            jax.ShapeDtypeStruct((2, 8, 128), f32),
        ],
        compiler_params=pltpu.CompilerParams(vmem_limit_bytes=VMEM_LIMIT),
        cost_estimate=cost(22),
        name="scores",
    )(me, inv, out_own, out_oth, want, live, use, tgt_own, tgt_oth, neg_own, neg_oth)


def after(values, *others):
    return lax.optimization_barrier((values, others))[0]


AR_GROUPS = ((0, 2), (1, 3), (4,), (5,))


def unpad_kernel(half, sides_ref, *refs):
    halves, outs = refs[:-2], refs[-2:]
    width = halves[0].shape[0]

    def one_chunk(i, k, chunk):
        kept, came = halves[2 * i], halves[2 * i + 1]
        lanes = slice(k * width, (k + 1) * width)
        for side in range(2):
            value = jnp.where(sides_ref[chunk] == side, kept[:, lanes], came[:, lanes])
            rows = slice(side * half, (side + 1) * half)
            outs[chunk // 3][rows, :] = value.astype(jnp.float32)[:half, :half]

    for i, group in enumerate(AR_GROUPS):
        for k, chunk in enumerate(group):
            pl.when(pl.program_id(0) == chunk % 3)(functools.partial(one_chunk, i, k, chunk))


def unpad(half, sides, halves):
    shape = jax.ShapeDtypeStruct((3, 2 * half, half), jnp.float32)
    vmem = pl.BlockSpec(memory_space=pltpu.VMEM)
    out = pl.BlockSpec((None, 2 * half, half), lambda gate: (gate, 0, 0))
    return pl.pallas_call(
        functools.partial(unpad_kernel, half),
        grid=(3,),
        in_specs=[pl.BlockSpec(memory_space=pltpu.SMEM)] + [vmem] * len(halves),
        out_specs=[out, out],
        out_shape=[shape, shape],
        compiler_params=pltpu.CompilerParams(vmem_limit_bytes=VMEM_LIMIT),
        cost_estimate=cost(8),
        name="unpad",
    )(sides, *halves)


def pair(index, own, oth):
    return jnp.where(index == 0, jnp.stack([own, oth]), jnp.stack([oth, own]))


def reduce_orders(devices):
    bits = devices.bit_length() - 1
    if devices != 1 << bits or bits < 3:
        return None
    rest = list(range(3, bits))
    along, across = [0, 1, 2, *rest], [1, 0, 2, *rest]
    return [along, across] * 3


def flip(values, bit):
    devices = lax.axis_size("dp")
    return lax.ppermute(values, "dp", [(i, i ^ (1 << bit)) for i in range(devices)])


def halve(values, bit):
    place = (lax.axis_index("dp") >> bit) & 1
    size = values.shape[0] // 2
    send = lax.dynamic_slice_in_dim(values, (1 - place) * size, size)
    keep = lax.dynamic_slice_in_dim(values, place * size, size)
    return send, keep


def add_low(left, right):
    return (left.astype(jnp.float32) + right.astype(jnp.float32)).astype(left.dtype)


def scatter_sum(chunks, orders, owner_sums):
    parts = list(chunks)
    for level in range(len(orders[0])):
        if level >= 2:
            arrived = [value.came for value in owner_sums]
            parts = [after(part, arrived) for part in parts]
        sends = []
        for i, order in enumerate(orders):
            send, keep = halve(parts[i], order[level])
            parts[i] = add_low(keep, flip(send, order[level]))
            sends.append(send)
        if level != 1:
            for value in owner_sums:
                value.finish(sends)
                if value.order:
                    value.start()
    while owner_sums and owner_sums[0].order:
        for value in owner_sums:
            value.start()
            value.finish()
    return parts


def gather_sum(parts, orders, sent):
    device = lax.axis_index("dp")
    parts = [jnp.concatenate([parts[i] for i in group], axis=1) for group in AR_GROUPS]
    orders = [orders[group[0]] for group in AR_GROUPS]
    halves = []
    for level in reversed(range(len(orders[0]))):
        if level == 1:
            came_rows = exchange(after(sent, parts))
        for i, order in enumerate(orders):
            bit = (device >> order[level]) & 1
            came = flip(parts[i], order[level])
            if level == 0:
                halves += [parts[i], came]
            else:
                parts[i] = jnp.where(
                    bit == 0,
                    jnp.concatenate([parts[i], came]),
                    jnp.concatenate([came, parts[i]]),
                )
    return halves, came_rows


class OwnerSum:
    def __init__(self, values, order):
        bits = len(order)
        self.order = list(order)
        self.axes = list(reversed(range(bits)))
        self.values = values.reshape((2,) * bits + values.shape[1:])

    def start(self):
        bit = self.order.pop(0)
        axis = self.axes.index(bit)
        place = (lax.axis_index("dp") >> bit) & 1
        send = lax.dynamic_index_in_dim(self.values, 1 - place, axis, keepdims=False)
        self.keep = lax.dynamic_index_in_dim(self.values, place, axis, keepdims=False)
        self.axes.remove(bit)
        self.came = flip(send, bit)
        return send

    def finish(self, *others):
        self.values = add_low(self.keep, after(self.came, *others) if others else self.came)

    def join(self, other):
        self.values = jnp.concatenate([self.values, other.values], axis=-2)


def routed(items, targets, masks, plan, negatives, h_init, emb, w_in, w_rec, b_in, b_rec_n,
           out_table, out_bias, item_list, target_list, item_slot, target_slot, neg_capacity, over):
    f32, low = jnp.float32, jnp.bfloat16
    blocks, steps, all_slots = items.shape
    slots = all_slots // 2
    events = steps * slots
    batch = 2 * events
    half = h_init.shape[1]
    width = roundup(half + 6, 128)
    rows = emb.shape[0]
    devices = lax.axis_size("dp")
    device = lax.axis_index("dp")
    core = lax.axis_index("mp")
    me = core.astype(jnp.int32).reshape(1)
    first_half = (core == 0).astype(f32)
    capacity = item_list.shape[1]
    breadth = 2 * half
    spare = width - half

    def mine(values):
        return lax.dynamic_index_in_dim(values, core, 0, keepdims=False)

    def theirs(values):
        return lax.dynamic_index_in_dim(values, 1 - core, 0, keepdims=False)

    def core_major(values):
        return values.reshape(blocks, steps, 2, slots).transpose(2, 0, 1, 3)

    row_lanes = jnp.concatenate(
        [jnp.ones((rows, 3), f32), jnp.zeros((rows, spare - 3), f32)], axis=1
    )
    emb_wide = jnp.concatenate([emb, (row_lanes * first_half).astype(low)], axis=1)
    ids = device * rows + jnp.arange(rows)
    parts = bf16_parts(out_bias)
    out_lanes = jnp.stack(
        [*parts, (ids // 256).astype(f32), (ids % 256).astype(f32), jnp.ones((rows,), f32)]
        + [jnp.zeros((rows,), f32)] * (spare - 6),
        axis=1,
    )
    out_wide = jnp.concatenate([out_table, (out_lanes * first_half).astype(low)], axis=1)

    own_negatives = plan_negatives(negatives, devices, rows, neg_capacity, device)
    negative_pick = one_hot(own_negatives.reshape(blocks * neg_capacity), rows)
    neg_own = lax.all_gather(
        dot_f32(negative_pick, out_wide).astype(low), "dp", axis=0, tiled=True
    )
    alive = jnp.sum((masks > 0).astype(jnp.int32))
    told = jnp.broadcast_to(jnp.stack([alive, over])[None, :], (devices, 2))
    asking = jnp.concatenate([item_list, target_list, told], axis=1)
    asked = exchange(asking)
    wanted_rows = asked[:, : 2 * capacity]
    count = jnp.sum(asked[:, 2 * capacity]).astype(f32)
    overs = jnp.sum(asked[:, 2 * capacity + 1])
    item_pick = one_hot(wanted_rows[:, :capacity].reshape(devices * capacity), rows)
    target_pick = one_hot(wanted_rows[:, capacity:].reshape(devices * capacity), rows)
    item_send = dot_f32(item_pick, emb_wide).astype(low).reshape(devices, capacity, width)
    w_in, w_rec = after((w_in, w_rec), item_send)
    item_rows = exchange(item_send).reshape(devices * capacity, width)
    target_send = dot_f32(target_pick, out_wide).astype(low).reshape(devices, capacity, width)

    def widened(weight, bias, gate):
        matrix = weight[:, gate, :].reshape(2, half, half)
        matrix = jnp.pad(matrix, ((0, 0), (0, 0), (0, spare)))
        if bias is None:
            extra = jnp.zeros((2, spare, width), low)
        else:
            line = jnp.stack([*bf16_parts(bias)]).astype(low)
            extra = jnp.pad(line[None], ((0, 1), (0, spare - 3), (0, spare)))
        return jnp.concatenate([matrix, extra], axis=1)

    wi_own = jnp.stack([widened(w_in, b_in[gate], gate) for gate in range(3)])
    wr_own = jnp.stack([widened(w_rec, b_rec_n if gate == 2 else None, gate) for gate in range(3)])
    weights = (wi_own, swap_cores(wi_own), wr_own, swap_cores(wr_own))

    start_all = jnp.pad(h_init, ((0, 0), (0, spare))).reshape(2, slots, width)
    start_own = mine(start_all)
    start_oth = swap_cores(lax.dynamic_index_in_dim(start_all, 1 - core, 0, keepdims=False))
    state = pair(core, start_own, start_oth)

    codes_all = core_major(masks)
    codes = mine(codes_all).astype(f32)
    codes_wide = jnp.broadcast_to(codes[..., None], (blocks, steps, slots, 128))
    target_all = core_major(targets).reshape(2, blocks, events)
    want = jnp.broadcast_to(mine(target_all).astype(f32)[..., None], (blocks, events, 128))
    live = (codes_wide > 0.0).astype(f32).reshape(blocks, events, 128)
    use = (codes_all > 0).astype(f32).reshape(2, blocks, events).transpose(1, 0, 2)
    use = jnp.broadcast_to(use.reshape(blocks, 1, batch), (blocks, 8, batch))

    slots_first = item_slot.reshape(2, blocks * events)
    slots_first = jnp.concatenate([mine(slots_first), theirs(slots_first)])
    item_hot = one_hot(slots_first, devices * capacity)
    emb_own = dot_f32(item_hot, item_rows).astype(low)
    emb_oth = swap_cores(emb_own)
    emb_own = emb_own.reshape(2, blocks, events, width)
    emb_oth = emb_oth.reshape(2, blocks, events, width)
    inputs = jnp.concatenate(
        [
            emb_own.reshape(blocks * batch, width),
            jnp.concatenate([emb_oth[1], emb_oth[0]]).reshape(blocks * batch, width),
        ],
        axis=1,
    )

    hop = -(-slots // devices)
    saves = []
    outs = []
    entries = []
    routes = []
    squares = []
    lane_real = (jnp.arange(2 * width) % width < half).astype(f32)
    for block in range(blocks):
        result = run_forward(half, block, me, emb_own, emb_oth, codes_wide, state, weights)
        outs.append([value.reshape(events, width) for value in result[:2]])
        entries.append(result[2].reshape(events, 2 * width))
        saves.append(result[3:8])
        state = result[8]
        squares.append(result[9])
        if block + 1 < blocks:
            going = lax.dynamic_slice_in_dim(plan[block], core * slots, slots, 0)
            aim = going // all_slots
            place = going % all_slots
            order = jnp.arange(slots)
            earlier = (aim[:, None] == aim[None, :]) & (order[:, None] > order[None, :])
            position = aim * hop + jnp.sum(earlier.astype(jnp.int32), axis=1)
            lanes = jnp.arange(2 * width)[None, :]
            flat = state.transpose(1, 0, 2).reshape(slots, 2 * width)
            flat = jnp.where(lanes == half, place.astype(f32)[:, None], flat)
            flat = jnp.where(lanes == half + 1, 1.0, flat).astype(low)
            put = (jnp.arange(devices * hop)[:, None] == position[None, :]).astype(low)
            sent = dot_f32(put, flat).astype(low).reshape(devices, hop, 2 * width)
            came = exchange(sent).reshape(devices * hop, 2 * width)
            both = jnp.concatenate([came, swap_cores(came)], axis=0)
            label = jnp.where(both[:, half + 1] > 0.5, both[:, half].astype(f32), -1.0)
            here = (core * slots + order).astype(f32)
            take = (here[:, None] == label[None, :]).astype(low)
            moved = dot_f32(take, both) * lane_real
            state = moved.reshape(slots, 2, width).transpose(1, 0, 2)
            if block == 0:
                target_send = after(target_send, state)
                state = after(state, target_send)
                target_rows = exchange(target_send)
                target_rows = target_rows.reshape(devices * capacity, width)
                neg_own = after(neg_own, state)
            routes.append((label[: devices * hop], put))

    target_slot_blocks = target_slot.reshape(2, blocks, events).transpose(1, 0, 2)
    target_hot = one_hot(target_slot_blocks.reshape(blocks * batch), devices * capacity)
    neg_oth = swap_cores(neg_own)
    outs[-1] = after(outs[-1], neg_oth)
    outs[:-1] = after(outs[:-1], outs[-1])
    target_rows = after(target_rows, outs[-1])
    tgt_own = dot_f32(target_hot, target_rows).astype(low)
    tgt_oth = swap_cores(tgt_own).reshape(blocks, batch, width)
    neg_oth = neg_oth.reshape(devices, blocks, neg_capacity, width)
    neg_own = neg_own.reshape(devices, blocks, neg_capacity, width)
    tgt_own = tgt_own.reshape(blocks, batch, width)
    inv = (1.0 / count).reshape(1)
    from_scores = [None] * blocks
    orders = reduce_orders(devices)
    stats = []
    row_grads = [None] * blocks
    gate_own = [None] * blocks
    gate_oth = [None] * blocks
    emb_grads = [None] * blocks
    emb_grads_oth = [None] * blocks
    grad_state = jnp.zeros((2, slots, width), f32)
    grad_pairs = []
    for block in reversed(range(blocks)):
        grad_own, *from_scores[block], stat = run_scores(
            half, block, me, inv, *outs[block], want, live, use, tgt_own, tgt_oth, neg_own, neg_oth
        )
        stats.append(stat)
        grad_pairs.insert(0, (grad_own, swap_cores(grad_own), swap_cores(outs[block][1])))
    negative_grads = [None] * blocks

    for block in range(blocks):
        grad_own, grad_oth, outs_oth = grad_pairs[block]
        value = dot_first(grad_own, outs[block][0]) + dot_first(grad_oth, outs_oth)
        row_grads[block] = value.astype(low)
    negative_grads = jnp.stack(
        [value[batch:].reshape(devices, neg_capacity, width) for value in row_grads], axis=1
    )
    cut = roundup(neg_capacity // 2, 16)
    owner_sums = []
    if orders is not None:
        owner_sums = [
            OwnerSum(negative_grads[:, :, :cut], orders[0]),
            OwnerSum(negative_grads[:, :, cut:], orders[1]),
        ]
        from_scores[-1] = after(from_scores[-1], [value.start() for value in owner_sums])
    target_grads = jnp.concatenate([value[:batch] for value in row_grads], axis=0)
    target_send = dot_first(target_hot, target_grads).astype(low)
    target_came = exchange(target_send.reshape(devices, capacity, width))
    entering = jnp.concatenate(entries, axis=0)
    entering = jnp.concatenate([entering, swap_cores(entering)], axis=0)
    for block in reversed(range(blocks)):
        own, oth, emb_grads[block], emb_oth_grad, grad_state = run_backward(
            half,
            block,
            me,
            codes_wide,
            *[value.reshape(steps, slots, width) for value in from_scores[block]],
            saves[block],
            grad_state,
            weights,
        )
        gate_own[block] = own.reshape(4, events, width)
        gate_oth[block] = swap_cores(oth).reshape(4, events, width)
        emb_grads_oth[block] = swap_cores(emb_oth_grad)
        if block > 0:
            label, put = routes[block - 1]
            flat = grad_state.transpose(1, 0, 2).reshape(slots, 2 * width).astype(low)
            both = jnp.concatenate([flat, swap_cores(flat)], axis=0)
            order = jnp.arange(slots)
            names = jnp.concatenate([core * slots + order, (1 - core) * slots + order]).astype(f32)
            fetch = (label[:, None] == names[None, :]).astype(low)
            home = dot_f32(fetch, both).astype(low).reshape(devices, hop, 2 * width)
            back = exchange(home)
            flat = dot_first(put, back.reshape(devices * hop, 2 * width)) * lane_real
            grad_state = flat.reshape(slots, 2, width).transpose(1, 0, 2)
            if block == 1 and orders is not None:
                for value in owner_sums:
                    value.finish(home)
                grad_state = after(grad_state, [value.start() for value in owner_sums], target_send)

    gates = jnp.concatenate([*gate_own, *gate_oth], axis=1)
    gates = after(gates, target_came)
    chunks = [dot_first(entering, gates[gate]).astype(low) for gate in (0, 1, 2)]
    chunks += [dot_first(inputs, gates[gate]).astype(low) for gate in (0, 1, 3)]
    marker = chunks[-1]
    target_came = after(target_came, marker)
    own_stats = [
        sum(jnp.sum(value[0, :, 0]) for value in stats),
        sum(jnp.sum(value[0]) for value in squares),
        sum(jnp.sum(value[1]) for value in squares),
        sum(jnp.sum(value[1, :, 0]) for value in stats),
    ]
    own_stats = jnp.stack(bf16_parts(jnp.stack(own_stats)))
    own_stats = jnp.pad(own_stats, ((0, capacity - 3), (width - 4, 0)))

    def row_sums():
        item_grads = jnp.concatenate([*emb_grads, *emb_grads_oth], axis=0)
        item_sums = dot_first(item_hot, after(item_grads, marker))
        item_sums = item_sums.reshape(devices, capacity, width) + own_stats
        return item_sums.astype(low)

    if orders is None:
        item_came = exchange(row_sums())
        sums = [lax.psum(chunk, "dp") for chunk in chunks]
        sums = [jnp.concatenate([sums[i] for i in group], axis=1) for group in AR_GROUPS]
        halves = [value for chunk in sums for value in (chunk[:width], chunk[width:])]
        sides = [jnp.zeros((), jnp.int32)] * 6
        negative_sum = lax.psum_scatter(
            negative_grads, "dp", scatter_dimension=0, tiled=True
        ).reshape(blocks * neg_capacity, width)
    else:

        parts = scatter_sum(chunks, orders, owner_sums)
        first, second = [value.values for value in owner_sums]
        negative_sum = jnp.concatenate(
            [first.reshape(blocks, cut, width), second.reshape(blocks, neg_capacity - cut, width)],
            axis=1,
        ).reshape(blocks * neg_capacity, width)
        halves, item_came = gather_sum(parts, orders, row_sums())
        sides = [(device >> order[0]) & 1 for order in orders]
    all_stats = jnp.sum(item_came[:, :3, width - 4 :].astype(f32), axis=(0, 1))
    all_stats = all_stats + swap_cores(all_stats)
    sides = [side.astype(jnp.int32) for side in sides]
    sides = jnp.stack(sides[:3] + [side ^ core.astype(jnp.int32) for side in sides[3:]])

    def first_row(chunk):
        for i, group in enumerate(AR_GROUPS):
            if chunk in group:
                lanes = slice(group.index(chunk) * width, group.index(chunk) * width + half)
                kept, came = halves[2 * i][half, lanes], halves[2 * i + 1][half, lanes]
        return jnp.where(sides[chunk] == 0, kept, came).astype(f32)

    grad_b_in = jnp.stack([first_row(chunk) for chunk in (3, 4, 5)])
    grad_b_rec = first_row(2)
    grad_emb = dot_first(item_pick, item_came.reshape(devices * capacity, width))[:, :half]
    grad_out = dot_first(
        target_pick, target_came.reshape(devices * capacity, width)
    ) + dot_first(negative_pick, negative_sum)
    bias_own = grad_out[:, half]
    grad_out_bias = jnp.where(core == 0, bias_own, swap_cores(bias_own))

    def slots_of(values):
        own = mine(values)
        oth = swap_cores(theirs(values))
        return pair(core, own, oth).reshape(all_slots, width)[:, :half]

    columns = batch + negatives.shape[1]
    return overs, halves, sides, (
        all_stats[0] / count,
        jnp.sqrt(all_stats[1] / (count * breadth)),
        jnp.sqrt(all_stats[2] / (count * breadth)),
        jnp.sqrt(all_stats[3] / (count * columns)),
        slots_of(after(state, marker)),
        slots_of(after(grad_state, marker)),
        grad_emb,
        grad_b_in,
        grad_b_rec,
        grad_out[:, :half],
        grad_out_bias,
    )


def shards(items, targets, masks, plan, negatives, h_init, emb, w_in, w_rec, b_in, b_rec_n,
           out_table, out_bias):
    blocks, steps, all_slots = items.shape
    devices = lax.axis_size("dp")
    rows = emb.shape[0]
    requests = blocks * steps * all_slots
    capacity = max(32, roundup(-(-requests // devices), 16))
    mean = -(-negatives.shape[1] // devices)
    neg_capacity = min(roundup(mean + 4 * math.isqrt(mean), 16), roundup(rows, 16))

    def core_major(values):
        split = values.reshape(blocks, steps, 2, all_slots // 2)
        return split.transpose(2, 0, 1, 3).reshape(requests)

    item_rows, item_slot, item_most = plan_requests(core_major(items), devices, rows, capacity)
    target_rows, target_slot, target_most = plan_requests(
        core_major(targets), devices, rows, capacity
    )
    negative_most = most_negatives(negatives, devices, rows)
    over = (
        (item_most > capacity) | (target_most > capacity) | (negative_most > neg_capacity)
    ).astype(jnp.int32)
    given = (items, targets, masks, plan, negatives, h_init, emb, w_in, w_rec, b_in, b_rec_n,
             out_table, out_bias)
    overs, halves, sides, ready = routed(
        *given, item_rows, target_rows, item_slot, target_slot, neg_capacity, over
    )

    halves, sides, ready = lax.optimization_barrier((halves, sides, ready))

    def finish(halves, sides, ready):
        grad_w_rec, grad_w_in = unpad(h_init.shape[1], sides, halves)
        return (
            *ready[:7],
            grad_w_in.transpose(1, 0, 2),
            grad_w_rec.transpose(1, 0, 2),
            *ready[7:],
        )

    return lax.cond(overs == 0, finish, lambda *unused: general(*given), halves, sides, ready)


def solution(mesh):
    return jax.shard_map(
        shards,
        mesh=mesh,
        in_specs=(
            P(None, None, "dp"),
            P(None, None, "dp"),
            P(None, None, "dp"),
            P(None, "dp"),
            P(),
            P("dp", "mp"),
            P("dp", "mp"),
            P(None, None, "mp"),
            P(None, None, "mp"),
            P(None, "mp"),
            P("mp"),
            P("dp", "mp"),
            P("dp"),
        ),
        out_specs=(
            P(),
            P(),
            P(),
            P(),
            P("dp", "mp"),
            P("dp", "mp"),
            P("dp", "mp"),
            P(None, None, "mp"),
            P(None, None, "mp"),
            P(None, "mp"),
            P("mp"),
            P("dp", "mp"),
            P("dp"),
        ),
        check_vma=False,
    )
```

```python
import functools
import math

import jax
import jax.numpy as jnp
from jax import lax
from jax.experimental import pallas as pl
from jax.experimental.pallas import tpu as pltpu
from jax.sharding import PartitionSpec as P

REGULAR = 1.0
NEGATIVE_FLOOR = -1e30
VMEM_LIMIT = 56 * 1024 * 1024


def bpr_rows(scores, wanted, chosen, usable):
    session_events = scores.shape[0]
    allowed = usable[None, :] & (chosen[None, :] != wanted[:, None])
    positive = jnp.diagonal(scores[:, :session_events])
    top_score = jnp.max(jnp.where(allowed, scores, NEGATIVE_FLOOR), axis=1, keepdims=True)
    weights = jnp.exp(jnp.where(allowed, scores - top_score, NEGATIVE_FLOOR))
    normal = jnp.sum(weights, axis=1, keepdims=True)
    joined = scores + jax.nn.log_sigmoid(positive[:, None] - scores)
    top_joined = jnp.max(jnp.where(allowed, joined, NEGATIVE_FLOOR), axis=1, keepdims=True)
    joined_sum = jnp.sum(
        jnp.exp(jnp.where(allowed, joined - top_joined, NEGATIVE_FLOOR)), axis=1, keepdims=True
    )
    ranking = top_score + jnp.log(normal) - top_joined - jnp.log(joined_sum)
    penalty = jnp.sum(weights / normal * scores * scores, axis=1)
    return ranking[:, 0] + REGULAR * penalty


def gru_cell(gates_in, recurrent, prior, bias_cand, active_sessions):
    update = jax.nn.sigmoid(gates_in[:, 0] + recurrent[:, 0])
    reset = jax.nn.sigmoid(gates_in[:, 1] + recurrent[:, 1])
    candidate = jnp.tanh(gates_in[:, 2] + reset * (recurrent[:, 2] + bias_cand))
    return active_sessions * ((1.0 - update) * candidate + update * prior)


def block_rows(total, row_count):
    return math.gcd(total, 2 ** max(8, 22 - row_count.bit_length()))


def lookup_rows(index, table, row_count):
    total = index.shape[0]
    size = block_rows(total, row_count)

    def one_block(index_block):
        indicator = index_block[:, None] == jnp.arange(row_count, dtype=jnp.int32)[None, :]
        return jnp.dot(indicator.astype(jnp.bfloat16), table, preferred_element_type=jnp.float32)

    picked = lax.map(one_block, index.reshape(total // size, size))
    return picked.reshape(total, table.shape[1])


def sum_rows(index, values, row_count):
    total = index.shape[0]
    breadth = values.shape[1]
    size = block_rows(total, row_count)

    def add_block(accum, pair):
        index_block, value_block = pair
        indicator = index_block[:, None] == jnp.arange(row_count, dtype=jnp.int32)[None, :]
        term = lax.dot_general(
            indicator.astype(jnp.bfloat16),
            value_block,
            (((0,), (0,)), ((), ())),
            preferred_element_type=jnp.float32,
        )
        return (accum + term, None)

    accum, _ = lax.scan(
        add_block,
        jnp.zeros((row_count, breadth), jnp.float32),
        (index.reshape(total // size, size), values.reshape(total // size, size, breadth)),
    )
    return accum


def spread(own_low):
    return lax.all_gather(own_low, "mp", axis=1, tiled=True)


def move_state(state, destination, devices, slots):
    capacity = (slots + devices - 1) // devices
    target_device = destination // slots
    target_slot = destination % slots
    order = jnp.arange(slots)
    earlier = (target_device[:, None] == target_device[None, :]) & (order[:, None] > order[None, :])
    position = target_device * capacity + jnp.sum(earlier.astype(jnp.int32), axis=1)
    outgoing = jnp.zeros((devices * capacity, state.shape[1]), jnp.float32).at[position].set(state)
    labels = jnp.full((devices * capacity,), slots, jnp.int32).at[position].set(target_slot)
    arrived, arrived_labels = (
        lax.all_to_all(
            outgoing.astype(jnp.bfloat16), "dp", split_axis=0, concat_axis=0, tiled=True
        ).astype(outgoing.dtype),
        lax.all_to_all(labels, "dp", split_axis=0, concat_axis=0, tiled=True),
    )
    moved = jnp.zeros_like(state).at[arrived_labels].set(arrived, mode="drop")
    return (moved, arrived_labels, position)


def return_state(grad_start, labels, position, slots):
    inside = labels < slots
    spot = jnp.where(inside, labels, 0)
    returning = jnp.where(inside[:, None], jnp.take(grad_start, spot, axis=0), 0.0)
    back = lax.all_to_all(
        returning.astype(jnp.bfloat16), "dp", split_axis=0, concat_axis=0, tiled=True
    ).astype(returning.dtype)
    return jnp.take(back, position, axis=0)


def general(
    items,
    targets,
    masks,
    plan,
    negatives,
    h_init,
    emb,
    w_in,
    w_rec,
    b_in,
    b_rec_n,
    out_table,
    out_bias,
):
    blocks, steps, slots = items.shape
    halfwidth = h_init.shape[1]
    breadth = w_in.shape[0]
    vocab_rows = emb.shape[0]
    devices = lax.axis_size("dp")
    negs = negatives.shape[1]
    session_events = steps * slots
    columns = session_events + negs
    token_ids = blocks * session_events
    item_ids = items.reshape(token_ids)
    cand_ids = jnp.concatenate([targets.reshape(blocks, session_events), negatives], axis=1)
    flat_cands = cand_ids.reshape(blocks * columns)
    alive_flags = (masks > 0).astype(jnp.float32)
    w_in_flat = w_in.reshape(breadth, 3 * halfwidth)
    w_rec_flat = w_rec.reshape(breadth, 3 * halfwidth)
    cand_rows = jnp.zeros((blocks * columns, halfwidth), jnp.bfloat16)
    cand_bias = jnp.zeros((blocks * columns,), jnp.float32)
    emb_piece = lax.all_gather(emb, "dp", axis=0, tiled=True)
    out_piece = lax.all_gather(out_table, "dp", axis=0, tiled=True)
    bias_piece = lax.all_gather(out_bias.astype(jnp.bfloat16), "dp", axis=0, tiled=True).astype(
        jnp.float32
    )
    row_count = emb_piece.shape[0]
    embedded = lookup_rows(item_ids, emb_piece, row_count)
    shifted = flat_cands
    inside = (shifted >= 0) & (shifted < row_count)
    take_position = jnp.clip(shifted, 0, row_count - 1)
    cand_rows = jnp.where(inside[:, None], jnp.take(out_piece, take_position, axis=0), cand_rows)
    cand_bias = jnp.where(inside, jnp.take(bias_piece, take_position), cand_bias)
    embedded, cand_rows, cand_bias = (embedded, cand_rows, cand_bias)
    inputs_full, cand_full = (
        lax.all_gather(embedded.astype(jnp.bfloat16), "mp", axis=1, tiled=True),
        lax.all_gather(cand_rows, "mp", axis=1, tiled=True),
    )
    preacts = jnp.dot(inputs_full, w_in_flat, preferred_element_type=jnp.float32)
    preacts = preacts.reshape(blocks, steps, slots, 3, halfwidth) + b_in

    def advance(carry_pair, step_inputs):
        prior, prior_low = carry_pair
        gates_in, codes = step_inputs
        keeping = (codes == 1).astype(jnp.float32)[:, None]
        active_sessions = (codes > 0).astype(jnp.float32)[:, None]
        entering = prior_low * keeping.astype(jnp.bfloat16)
        recurrent = jnp.dot(entering, w_rec_flat, preferred_element_type=jnp.float32).reshape(
            slots, 3, halfwidth
        )
        fresh = gru_cell(gates_in, recurrent, prior * keeping, b_rec_n, active_sessions)
        fresh_own = fresh.astype(jnp.bfloat16)
        fresh_low = spread(fresh_own)
        return ((fresh, fresh_low), (prior, prior_low, recurrent, fresh_low, fresh_own))

    state = h_init
    state_low = spread(h_init.astype(jnp.bfloat16))
    records = []
    routes = []
    for event_block in range(blocks):
        (state, state_low), record = lax.scan(
            advance, (state, state_low), (preacts[event_block], masks[event_block])
        )
        records.append(record)
        if event_block + 1 < blocks:
            state, labels, position = move_state(state, plan[event_block], devices, slots)
            routes.append((labels, position))
            state_low = spread(state.astype(jnp.bfloat16))
    loss_total_sum = jnp.zeros((), jnp.float32)
    score_squared = jnp.zeros((), jnp.float32)
    hidden_squared = jnp.zeros((), jnp.float32)
    score_list = []
    for event_block in range(blocks):
        outputs = records[event_block][3].reshape(session_events, breadth)
        candidates = cand_full[event_block * columns : (event_block + 1) * columns]
        scores = lax.dot_general(
            outputs, candidates, (((1,), (1,)), ((), ())), preferred_element_type=jnp.float32
        )
        scores = scores + cand_bias[event_block * columns : (event_block + 1) * columns]
        active_sessions = alive_flags[event_block].reshape(session_events)
        usable = jnp.concatenate([active_sessions > 0, jnp.ones((negs,), dtype=bool)])
        losses = bpr_rows(
            scores, targets[event_block].reshape(session_events), cand_ids[event_block], usable
        )
        loss_total_sum = loss_total_sum + jnp.sum(active_sessions * losses)
        score_squared = score_squared + jnp.sum(active_sessions * jnp.sum(scores * scores, axis=1))
        output_values = outputs.astype(jnp.float32)
        hidden_squared = hidden_squared + jnp.sum(
            active_sessions[:, None] * output_values * output_values
        )
        score_list.append(scores)
    input_entries = inputs_full.astype(jnp.float32)
    input_squared = jnp.sum(alive_flags.reshape(token_ids)[:, None] * input_entries * input_entries)
    count_all, loss_all, input_all, hidden_all, score_all = lax.psum(
        (jnp.sum(alive_flags), loss_total_sum, input_squared, hidden_squared, score_squared), "dp"
    )
    loss = loss_all / count_all
    rms_inputs = jnp.sqrt(input_all / (count_all * breadth))
    rms_hidden = jnp.sqrt(hidden_all / (count_all * breadth))
    rms_scores = jnp.sqrt(score_all / (count_all * columns))
    from_scores = []
    row_grads = []
    bias_grads = []
    for event_block in range(blocks):
        active_sessions = alive_flags[event_block].reshape(session_events)
        usable = jnp.concatenate([active_sessions > 0, jnp.ones((negs,), dtype=bool)])
        wanted = targets[event_block].reshape(session_events)
        chosen = cand_ids[event_block]

        def block_loss(scores_arg):
            return jnp.sum(active_sessions * bpr_rows(scores_arg, wanted, chosen, usable))

        _, pullback = jax.vjp(block_loss, score_list[event_block])
        (grad_scores,) = pullback(jnp.ones((), jnp.float32) / count_all)
        bias_grads.append(jnp.sum(grad_scores, axis=0))
        scores_low = grad_scores.astype(jnp.bfloat16)
        own_rows = cand_rows[event_block * columns : (event_block + 1) * columns]
        to_outputs = jnp.dot(scores_low, own_rows, preferred_element_type=jnp.float32)
        from_scores.append(to_outputs.reshape(steps, slots, halfwidth))
        own_outputs = records[event_block][4].reshape(session_events, halfwidth)
        row_grads.append(
            lax.dot_general(
                scores_low,
                own_outputs,
                (((0,), (0,)), ((), ())),
                preferred_element_type=jnp.float32,
            )
        )
    cand_row_grads = jnp.concatenate(row_grads, axis=0)
    cand_bias_grads = jnp.concatenate(bias_grads, axis=0)

    def retreat(carry_triple, saved):
        grad_state, grad_rec_w, grad_bias_cand = carry_triple
        prior, prior_low, recurrent, gates_in, codes, from_output = saved
        grad_state = grad_state + from_output
        keeping = (codes == 1).astype(jnp.float32)[:, None]
        active_sessions = (codes > 0).astype(jnp.float32)[:, None]
        _, cell_pull = jax.vjp(
            lambda gate_arg, rec_arg, prior_arg, bias_arg: gru_cell(
                gate_arg, rec_arg, prior_arg, bias_arg, active_sessions
            ),
            gates_in,
            recurrent,
            prior * keeping,
            b_rec_n,
        )
        grad_gates, grad_rec, grad_prior, grad_bias = cell_pull(grad_state)
        rec_low = grad_rec.reshape(slots, 3 * halfwidth).astype(jnp.bfloat16)
        partial_sum = lax.dot_general(
            rec_low, w_rec_flat, (((1,), (1,)), ((), ())), preferred_element_type=jnp.float32
        )
        through_rec = lax.psum_scatter(
            partial_sum.astype(jnp.bfloat16), "mp", scatter_dimension=1, tiled=True
        ).astype(jnp.float32)
        entering = prior_low * keeping.astype(jnp.bfloat16)
        grad_rec_w = grad_rec_w + lax.dot_general(
            entering, rec_low, (((0,), (0,)), ((), ())), preferred_element_type=jnp.float32
        )
        previous = keeping * (grad_prior + through_rec)
        return ((previous, grad_rec_w, grad_bias_cand + grad_bias), grad_gates)

    grad_state = jnp.zeros((slots, halfwidth), jnp.float32)
    grad_rec_w = jnp.zeros((breadth, 3 * halfwidth), jnp.float32)
    grad_bias_cand = jnp.zeros((halfwidth,), jnp.float32)
    pre_grads = [None] * blocks
    for event_block in reversed(range(blocks)):
        prior_all, prior_low_all, recurrent_all, _, _ = records[event_block]
        (grad_state, grad_rec_w, grad_bias_cand), grad_pre = lax.scan(
            retreat,
            (grad_state, grad_rec_w, grad_bias_cand),
            (
                prior_all,
                prior_low_all,
                recurrent_all,
                preacts[event_block],
                masks[event_block],
                from_scores[event_block],
            ),
            reverse=True,
        )
        pre_grads[event_block] = grad_pre
        if event_block > 0:
            grad_state = return_state(
                grad_state, routes[event_block - 1][0], routes[event_block - 1][1], slots
            )
    pre_all = jnp.stack(pre_grads)
    grad_bias_in = jnp.sum(pre_all, axis=(0, 1, 2))
    pre_low = pre_all.reshape(token_ids, 3 * halfwidth).astype(jnp.bfloat16)
    grad_w_in = lax.dot_general(
        inputs_full, pre_low, (((0,), (0,)), ((), ())), preferred_element_type=jnp.float32
    )
    input_part = lax.dot_general(
        pre_low, w_in_flat, (((1,), (1,)), ((), ())), preferred_element_type=jnp.float32
    )
    grad_inputs = lax.psum_scatter(
        input_part.astype(jnp.bfloat16), "mp", scatter_dimension=1, tiled=True
    )
    bias_term = jnp.zeros((vocab_rows * devices,), jnp.float32).at[flat_cands].add(cand_bias_grads)
    weight_count = breadth * 3 * halfwidth
    packed_grads = jnp.concatenate(
        [
            grad_w_in.reshape(weight_count),
            grad_rec_w.reshape(weight_count),
            grad_bias_in.reshape(3 * halfwidth),
            grad_bias_cand,
        ]
    )
    packed_length = packed_grads.shape[0]
    padded_length = -(-packed_length // devices) * devices
    packed_grads = jnp.pad(packed_grads, (0, padded_length - packed_length))
    own_share, grad_out_bias = (
        lax.psum_scatter(packed_grads, "dp", scatter_dimension=0, tiled=True),
        lax.psum_scatter(bias_term, "dp", scatter_dimension=0, tiled=True),
    )
    summed_all = lax.all_gather(own_share.astype(jnp.bfloat16), "dp", axis=0, tiled=True).astype(
        own_share.dtype
    )
    summed_w_in = summed_all[:weight_count]
    summed_w_rec = summed_all[weight_count : 2 * weight_count]
    summed_b_in = summed_all[2 * weight_count : 2 * weight_count + 3 * halfwidth].reshape(
        3, halfwidth
    )
    summed_b_cand = summed_all[2 * weight_count + 3 * halfwidth : 2 * weight_count + 4 * halfwidth]
    shifted = flat_cands
    inside = (shifted >= 0) & (shifted < lax.axis_size("dp") * vocab_rows)
    position = jnp.where(inside, shifted, lax.axis_size("dp") * vocab_rows)
    both = lax.psum_scatter(
        jnp.concatenate(
            [
                sum_rows(item_ids, grad_inputs, lax.axis_size("dp") * vocab_rows),
                jnp.zeros((lax.axis_size("dp") * vocab_rows, halfwidth), jnp.float32)
                .at[position]
                .add(cand_row_grads, mode="drop"),
            ],
            axis=1,
        ),
        "dp",
        scatter_dimension=0,
        tiled=True,
    )
    grad_emb = both[:, :halfwidth]
    grad_out_table = both[:, halfwidth:]
    return (
        loss,
        rms_inputs,
        rms_hidden,
        rms_scores,
        state,
        grad_state,
        grad_emb,
        summed_w_in.reshape(breadth, 3, halfwidth),
        summed_w_rec.reshape(breadth, 3, halfwidth),
        summed_b_in,
        summed_b_cand,
        grad_out_table,
        grad_out_bias,
    )


def roundup(value, unit):
    return -(-value // unit) * unit


def bf16_parts(values):
    first = lax.reduce_precision(values, 8, 7)
    second = lax.reduce_precision(values - first, 8, 7)
    third = lax.reduce_precision(values - first - second, 8, 7)
    return first, second, third


def one_hot(index, size):
    return (index[:, None] == jnp.arange(size, dtype=index.dtype)[None, :]).astype(jnp.bfloat16)


def dot_f32(left, right):
    return jnp.dot(left, right, preferred_element_type=jnp.float32)


def dot_first(left, right):
    return lax.dot_general(
        left, right, (((0,), (0,)), ((), ())), preferred_element_type=jnp.float32
    )


def dot_last(left, right):
    return lax.dot_general(
        left, right, (((1,), (1,)), ((), ())), preferred_element_type=jnp.float32
    )


def swap_cores(values):
    return lax.ppermute(values, "mp", [(0, 1), (1, 0)])


def exchange(values):
    return lax.all_to_all(values, "dp", split_axis=0, concat_axis=0, tiled=True)


def plan_requests(ids, devices, rows, capacity):
    owner = ids // rows
    owners = one_hot(owner, devices)
    local = one_hot(ids % rows, rows)
    wanted = dot_first(owners, local) > 0.5
    order = jnp.arange(rows)
    before = (order[:, None] < order[None, :]).astype(jnp.bfloat16)
    position = dot_f32(wanted.astype(jnp.bfloat16), before)
    longest = jnp.max(jnp.sum(wanted.astype(jnp.float32), axis=1))
    spots = jnp.sum(
        owners.astype(jnp.float32) * dot_last(local, position.astype(jnp.bfloat16)), axis=1
    )
    slot = owner * capacity + spots.astype(jnp.int32)
    keyed = jnp.where(wanted, position, -1.0)
    match = keyed[:, None, :] == jnp.arange(capacity, dtype=jnp.float32)[None, :, None]
    listed = jnp.sum(jnp.where(match, order.astype(jnp.float32) + 1.0, 0.0), axis=2) - 1.0
    return listed.astype(jnp.int32), slot, longest


def plan_negatives(negatives, devices, rows, capacity, device):
    blocks, negs = negatives.shape
    chunk = math.gcd(negs, 128)
    owner = negatives // rows
    mine = (owner == device).astype(jnp.float32)
    grouped = mine.reshape(blocks * (negs // chunk), chunk)
    order = jnp.arange(chunk)
    before = (order[:, None] < order[None, :]).astype(jnp.bfloat16)
    inner = dot_f32(grouped.astype(jnp.bfloat16), before).reshape(blocks, negs // chunk, chunk)
    totals = jnp.sum(grouped, axis=1).reshape(blocks, negs // chunk)
    group = jnp.arange(negs // chunk)
    outer = jnp.sum(
        jnp.where(group[None, :, None] > group[None, None, :], totals[:, None, :], 0.0), axis=2
    )
    position = (inner + outer[:, :, None]).reshape(blocks, negs)
    keyed = jnp.where(mine > 0.5, position, -1.0)
    match = keyed[:, None, :] == jnp.arange(capacity, dtype=jnp.float32)[None, :, None]
    local = (negatives % rows).astype(jnp.float32) + 1.0
    listed = jnp.sum(jnp.where(match, local[:, None, :], 0.0), axis=2) - 1.0
    return listed.astype(jnp.int32)


def most_negatives(negatives, devices, rows):
    owner = negatives // rows
    counts = jnp.sum(
        (owner[:, None, :] == jnp.arange(devices)[None, :, None]).astype(jnp.float32), axis=2
    )
    return jnp.max(counts)


def cost(microseconds):
    return pl.CostEstimate(
        flops=0, bytes_accessed=int(microseconds * 3.6e6), transcendentals=0
    )


def widen(code, width):
    return jnp.concatenate([code] * (width // code.shape[1]), axis=1)


def forward_kernel(half, mp_ref, own_ref, oth_ref, code_ref, start_ref, wi_own, wi_oth, wr_own,
                   wr_oth, outs_ref, outo_ref, ent_ref, upd_ref, rst_ref, cand_ref, rec_ref, pri_ref, end_ref,
                   sq_ref, wi, wr, pre, state, sems):
    me = mp_ref[0]
    other = 1 - me
    copies = [
        pltpu.make_async_copy(wi_own, wi.at[me], sems.at[0]),
        pltpu.make_async_copy(wi_oth, wi.at[other], sems.at[1]),
        pltpu.make_async_copy(wr_own, wr.at[me], sems.at[2]),
        pltpu.make_async_copy(wr_oth, wr.at[other], sems.at[3]),
    ]
    for copy in copies:
        copy.start()
    steps, slots, _ = code_ref.shape
    width = own_ref.shape[1]
    lane = lax.broadcasted_iota(jnp.int32, (slots, width), 1)
    real = lane < half
    ones = (lane >= half) & (lane < half + 3)
    own = own_ref[...]
    oth = oth_ref[...]
    state[...] = start_ref[...]
    for side, copy in ((me, copies[0]), (other, copies[1])):
        copy.wait()
        for gate in range(3):
            value = dot_f32(own, wi[side, gate, me]) + dot_f32(oth, wi[side, gate, other])
            pre[side, gate] = value.reshape(steps, slots, width)
    copies[2].wait()
    copies[3].wait()

    def step(t, sums):
        in_sum, out_sum = sums
        code = code_ref[t]
        keep = widen((code == 1.0).astype(jnp.float32), width)
        live = widen((code > 0.0).astype(jnp.float32), width)
        rows = pl.ds(pl.multiple_of(t * slots, slots), slots)
        for ref in (own_ref, oth_ref):
            entry = jnp.where(real, ref[rows, :].astype(jnp.float32), 0.0)
            in_sum = in_sum + live * entry * entry
        entering = []
        for side in range(2):
            value = keep * state[side].astype(jnp.bfloat16).astype(jnp.float32)
            if side == 0:
                value = jnp.where(ones, 1.0, value)
            value = value.astype(jnp.bfloat16)
            ent_ref[t, :, side * width : (side + 1) * width] = value
            entering.append(value)
        lows = []
        for side in range(2):
            recurrent = [
                dot_f32(entering[0], wr[side, gate, 0]) + dot_f32(entering[1], wr[side, gate, 1])
                for gate in range(3)
            ]
            update = jax.nn.sigmoid(pre[side, 0, t] + recurrent[0])
            reset = jax.nn.sigmoid(pre[side, 1, t] + recurrent[1])
            candidate = jnp.tanh(pre[side, 2, t] + reset * recurrent[2])
            prior = keep * state[side]
            fresh = live * ((1.0 - update) * candidate + update * prior)
            fresh = jnp.where(real, fresh, 0.0)
            upd_ref[side, t] = update
            rst_ref[side, t] = reset
            cand_ref[side, t] = candidate
            rec_ref[side, t] = recurrent[2]
            pri_ref[side, t] = prior
            state[side] = fresh
            low = fresh.astype(jnp.bfloat16)
            out_sum = out_sum + low.astype(jnp.float32) * low.astype(jnp.float32)
            if side == 0:
                low = jnp.where(ones, 1.0, low.astype(jnp.float32)).astype(jnp.bfloat16)
            lows.append(low)
        outs_ref[t] = jnp.where(me == 0, lows[0], lows[1])
        outo_ref[t] = jnp.where(me == 0, lows[1], lows[0])
        return in_sum, out_sum

    zero = jnp.zeros((slots, width), jnp.float32)
    in_sum, out_sum = lax.fori_loop(0, steps, step, (zero, zero))
    end_ref[...] = state[...]
    sq_ref[0] = in_sum
    sq_ref[1] = out_sum


def run_forward(half, block, me, own, oth, codes, start, weights):
    _, blocks, events, width = own.shape
    _, steps, slots, lanes = codes.shape
    f32, low = jnp.float32, jnp.bfloat16
    whole = lambda shape: pl.BlockSpec(shape, lambda i, s: (0,) * len(shape))
    saved = (2, steps, slots, width)
    hidden = (2, slots, width)
    return pl.pallas_call(
        functools.partial(forward_kernel, half),
        grid_spec=pltpu.PrefetchScalarGridSpec(
            num_scalar_prefetch=1,
            grid=(1,),
            in_specs=[
                pl.BlockSpec((None, None, events, width), lambda i, s: (0, block, 0, 0)),
                pl.BlockSpec((None, None, events, width), lambda i, s: (1, block, 0, 0)),
                pl.BlockSpec((None, steps, slots, lanes), lambda i, s: (block, 0, 0, 0)),
                whole(hidden),
            ]
            + [pl.BlockSpec(memory_space=pl.ANY)] * 4,
            out_specs=[whole(saved[1:])] * 2
            + [whole((steps, slots, 2 * width))]
            + [whole(saved)] * 5
            + [whole(hidden)] * 2,
            scratch_shapes=[
                pltpu.VMEM((2, 3, 2, width, width), low),
                pltpu.VMEM((2, 3, 2, width, width), low),
                pltpu.VMEM((2, 3, steps, slots, width), f32),
                pltpu.VMEM(hidden, f32),
                pltpu.SemaphoreType.DMA((4,)),
            ],
        ),
        out_shape=[jax.ShapeDtypeStruct(saved[1:], low)] * 2
        + [jax.ShapeDtypeStruct((steps, slots, 2 * width), low)]
        + [jax.ShapeDtypeStruct(saved, f32)] * 5
        + [jax.ShapeDtypeStruct(hidden, f32)] * 2,
        compiler_params=pltpu.CompilerParams(vmem_limit_bytes=VMEM_LIMIT),
        cost_estimate=cost(18),
        name="forward",
    )(me, own, oth, codes, start, *weights)


def backward_kernel(half, mp_ref, code_ref, from_own, from_oth, upd_ref, rst_ref, cand_ref, rec_ref, pri_ref,
                    last_ref, wi_own, wi_oth, wr_own, wr_oth, gate_own, gate_oth, emb_own, emb_oth,
                    first_ref, wi, wr, gate_ref, state, sems):
    me = mp_ref[0]
    other = 1 - me
    copies = [
        pltpu.make_async_copy(wr_own, wr.at[me], sems.at[0]),
        pltpu.make_async_copy(wr_oth, wr.at[other], sems.at[1]),
        pltpu.make_async_copy(wi_own, wi.at[me], sems.at[2]),
        pltpu.make_async_copy(wi_oth, wi.at[other], sems.at[3]),
    ]
    for copy in copies:
        copy.start()
    steps, slots, _ = code_ref.shape
    width = from_own.shape[-1]
    real = lax.broadcasted_iota(jnp.int32, (slots, width), 1) < half
    state[...] = last_ref[...]
    copies[0].wait()
    copies[1].wait()

    def step(i, carry):
        t = steps - 1 - i
        code = code_ref[t]
        keep = widen((code == 1.0).astype(jnp.float32), width)
        live = widen((code > 0.0).astype(jnp.float32), width)
        gates = []
        direct = []
        for side in range(2):
            toward = jnp.where(me == side, from_own[t], from_oth[t])
            grad = live * (state[side] + toward)
            update, reset = upd_ref[side, t], rst_ref[side, t]
            candidate = cand_ref[side, t]
            grad_update = grad * (pri_ref[side, t] - candidate)
            grad_cand = grad * (1.0 - update) * (1.0 - candidate * candidate)
            grad_reset = grad_cand * rec_ref[side, t]
            values = [
                grad_update * update * (1.0 - update),
                grad_reset * reset * (1.0 - reset),
                grad_cand * reset,
                grad_cand,
            ]
            values = [value.astype(jnp.bfloat16) for value in values]
            for gate in range(4):
                gate_ref[gate, side, t] = values[gate]
            gates.append(values)
            direct.append(grad * update)
        for gate in range(4):
            gate_own[gate, t] = jnp.where(me == 0, gates[0][gate], gates[1][gate])
            gate_oth[gate, t] = jnp.where(me == 0, gates[1][gate], gates[0][gate])
        for into in range(2):
            total = direct[into]
            for side in range(2):
                for gate in range(3):
                    total = total + dot_last(gates[side][gate], wr[side, gate, into])
            state[into] = jnp.where(real, keep * total, 0.0)
        return carry

    lax.fori_loop(0, steps, step, 0)
    first_ref[...] = state[...]
    copies[2].wait()
    copies[3].wait()
    events = steps * slots
    results = []
    for into in range(2):
        total = jnp.zeros((events, width), jnp.float32)
        for side in range(2):
            for gate in range(3):
                grads = gate_ref[3 if gate == 2 else gate, side].reshape(events, width)
                total = total + dot_last(grads, wi[side, gate, into])
        results.append(total.astype(jnp.bfloat16))
    emb_own[...] = jnp.where(me == 0, results[0], results[1])
    emb_oth[...] = jnp.where(me == 0, results[1], results[0])


def run_backward(half, block, me, codes, from_own, from_oth, saved_values, last, weights):
    _, steps, slots, lanes = codes.shape
    width = last.shape[-1]
    f32, low = jnp.float32, jnp.bfloat16
    whole = lambda shape: pl.BlockSpec(shape, lambda i, s: (0,) * len(shape))
    saved = (2, steps, slots, width)
    hidden = (2, slots, width)
    return pl.pallas_call(
        functools.partial(backward_kernel, half),
        grid_spec=pltpu.PrefetchScalarGridSpec(
            num_scalar_prefetch=1,
            grid=(1,),
            in_specs=[pl.BlockSpec((None, steps, slots, lanes), lambda i, s: (block, 0, 0, 0))]
            + [whole(saved[1:])] * 2
            + [whole(saved)] * 5
            + [whole(hidden)]
            + [pl.BlockSpec(memory_space=pl.ANY)] * 4,
            out_specs=[
                whole((4,) + saved[1:]),
                whole((4,) + saved[1:]),
                whole((steps * slots, width)),
                whole((steps * slots, width)),
                whole(hidden),
            ],
            scratch_shapes=[
                pltpu.VMEM((2, 3, 2, width, width), low),
                pltpu.VMEM((2, 3, 2, width, width), low),
                pltpu.VMEM((4,) + saved, low),
                pltpu.VMEM(hidden, f32),
                pltpu.SemaphoreType.DMA((4,)),
            ],
        ),
        out_shape=[
            jax.ShapeDtypeStruct((4,) + saved[1:], low),
            jax.ShapeDtypeStruct((4,) + saved[1:], low),
            jax.ShapeDtypeStruct((steps * slots, width), low),
            jax.ShapeDtypeStruct((steps * slots, width), low),
            jax.ShapeDtypeStruct(hidden, f32),
        ],
        compiler_params=pltpu.CompilerParams(vmem_limit_bytes=VMEM_LIMIT),
        cost_estimate=cost(23),
        name="backward",
    )(me, codes, from_own, from_oth, *saved_values, last, *weights)


def score_kernel(half, mp_ref, inv_ref, out_own, out_oth, want_ref, live_ref, use_ref, tgt_own, tgt_oth,
                 neg_own, neg_oth, grad_ref, to_own, to_oth, stat_ref, scores):
    me = mp_ref[0]
    events, width = out_own.shape
    batch = tgt_own.shape[0]
    devices, capacity, _ = neg_own.shape
    negs = devices * capacity
    cols = batch + negs
    lane = lax.broadcasted_iota(jnp.int32, (16, width), 1)
    row = lax.broadcasted_iota(jnp.int32, (16, width), 0)
    pick = jnp.where(
        row == 0,
        jnp.where(lane == half + 3, 256.0, jnp.where(lane == half + 4, 1.0, 0.0)),
        jnp.where((row == 1) & (lane == half + 5), 1.0, 0.0),
    ).astype(jnp.bfloat16)
    left_own = jnp.concatenate([out_own[...], pick], axis=0)
    left_oth = jnp.concatenate([out_oth[...], pick], axis=0)
    nown = neg_own[...].reshape(negs, width)
    noth = neg_oth[...].reshape(negs, width)
    scores[:, :batch] = dot_last(left_own, tgt_own[...]) + dot_last(left_oth, tgt_oth[...])
    scores[:, batch:] = dot_last(left_own, nown) + dot_last(left_oth, noth)
    ids = scores[events : events + 1, :]
    usable = jnp.concatenate([use_ref[:1, :], scores[events + 1 : events + 2, batch:]], axis=1)
    ids = jnp.where(usable > 0.5, ids, -1.0)
    group = 64
    inv = inv_ref[0]
    base = me * events

    def rows_step(i, stats):
        loss_sum, square_sum = stats
        rows = pl.ds(pl.multiple_of(i * group, group), group)
        s = scores[rows, :]
        want = want_ref[rows, :1]
        live = live_ref[rows, :1]
        allowed = (ids != want) & (usable > 0.5)
        head = s[:, :batch]
        column = lax.broadcasted_iota(jnp.int32, (group, batch), 1)
        place = lax.broadcasted_iota(jnp.int32, (group, batch), 0) + (base + i * group)
        diagonal = column == place
        positive = jnp.sum(jnp.where(diagonal, head, 0.0), axis=1, keepdims=True)
        masked = jnp.where(allowed, s, NEGATIVE_FLOOR)
        top = jnp.max(masked, axis=1, keepdims=True)
        weight = jnp.exp(masked - top)
        normal = jnp.sum(weight, axis=1, keepdims=True)
        gap = positive - s
        tail = jnp.exp(-jnp.abs(gap))
        lift = 1.0 + tail
        joined = jnp.where(allowed, jnp.minimum(s, positive) - jnp.log(lift), NEGATIVE_FLOOR)
        top_joined = jnp.max(joined, axis=1, keepdims=True)
        mass = jnp.exp(joined - top_joined)
        joined_sum = jnp.sum(mass, axis=1, keepdims=True)
        shared = mass / lift
        below = gap >= 0.0
        to_score = shared * jnp.where(below, 1.0, tail)
        to_positive = jnp.sum(shared * jnp.where(below, tail, 1.0), axis=1, keepdims=True)
        square = s * s
        penalty = jnp.sum(weight * square, axis=1, keepdims=True) / normal
        loss = top + jnp.log(normal) - top_joined - jnp.log(joined_sum) + REGULAR * penalty
        scale = live * inv
        grad = (scale / normal) * weight * (
            1.0 + REGULAR * (square + 2.0 * s - penalty)
        ) - (scale / joined_sum) * to_score
        drop = jnp.where(diagonal, scale * to_positive / joined_sum, 0.0)
        grad_ref[rows, :batch] = (grad[:, :batch] - drop).astype(jnp.bfloat16)
        grad_ref[rows, batch:] = grad[:, batch:].astype(jnp.bfloat16)
        loss_sum = loss_sum + live * loss
        square_sum = square_sum + live * jnp.sum(square, axis=1, keepdims=True)
        return loss_sum, square_sum

    zero = jnp.zeros((group, 1), jnp.float32)
    loss_sum, square_sum = lax.fori_loop(0, events // group, rows_step, (zero, zero))
    stat_ref[0] = jnp.broadcast_to(sum(loss_sum[i : i + 8] for i in range(0, group, 8)), (8, 128))
    stat_ref[1] = jnp.broadcast_to(sum(square_sum[i : i + 8] for i in range(0, group, 8)), (8, 128))
    grad_tgt = grad_ref[:, :batch]
    grad_neg = grad_ref[:, batch:]
    real = lax.broadcasted_iota(jnp.int32, (events, width), 1) < half
    total = dot_f32(grad_tgt, tgt_own[...]) + dot_f32(grad_neg, nown)
    to_own[...] = jnp.where(real, total, 0.0)
    total = dot_f32(grad_tgt, tgt_oth[...]) + dot_f32(grad_neg, noth)
    to_oth[...] = jnp.where(real, total, 0.0)


def run_scores(half, block, me, inv, out_own, out_oth, want, live, use, tgt_own, tgt_oth, neg_own,
               neg_oth):
    events, width = out_own.shape
    batch = tgt_own.shape[1]
    devices, _, capacity, _ = neg_own.shape
    cols = batch + devices * capacity
    low, f32 = jnp.bfloat16, jnp.float32
    whole = lambda shape: pl.BlockSpec(shape, lambda i, s: (0,) * len(shape))
    ofblock = lambda shape: pl.BlockSpec((None,) + shape, lambda i, s: (block,) + (0,) * len(shape))
    once = pl.Buffered(1)
    neg = pl.BlockSpec(
        (devices, None, capacity, width), lambda i, s: (0, block, 0, 0), pipeline_mode=once
    )
    return pl.pallas_call(
        functools.partial(score_kernel, half),
        grid_spec=pltpu.PrefetchScalarGridSpec(
            num_scalar_prefetch=1,
            grid=(1,),
            in_specs=[
                pl.BlockSpec(memory_space=pltpu.SMEM),
                whole((events, width)),
                whole((events, width)),
                ofblock((events, 128)),
                ofblock((events, 128)),
                ofblock((8, batch)),
                ofblock((batch, width)),
                ofblock((batch, width)),
                neg,
                neg,
            ],
            out_specs=[
                whole((events, cols)),
                whole((events, width)),
                whole((events, width)),
                whole((2, 8, 128)),
            ],
            scratch_shapes=[pltpu.VMEM((events + 16, cols), f32)],
        ),
        out_shape=[
            jax.ShapeDtypeStruct((events, cols), low),
            jax.ShapeDtypeStruct((events, width), f32),
            jax.ShapeDtypeStruct((events, width), f32),
            jax.ShapeDtypeStruct((2, 8, 128), f32),
        ],
        compiler_params=pltpu.CompilerParams(vmem_limit_bytes=VMEM_LIMIT),
        cost_estimate=cost(22),
        name="scores",
    )(me, inv, out_own, out_oth, want, live, use, tgt_own, tgt_oth, neg_own, neg_oth)


def after(values, *others):
    return lax.optimization_barrier((values, others))[0]


AR_GROUPS = ((0, 2), (1, 3), (4,), (5,))


def unpad_kernel(half, sides_ref, *refs):
    halves, outs = refs[:-2], refs[-2:]
    width = halves[0].shape[0]

    def one_chunk(i, k, chunk):
        kept, came = halves[2 * i], halves[2 * i + 1]
        lanes = slice(k * width, (k + 1) * width)
        for side in range(2):
            value = jnp.where(sides_ref[chunk] == side, kept[:, lanes], came[:, lanes])
            rows = slice(side * half, (side + 1) * half)
            outs[chunk // 3][rows, :] = value.astype(jnp.float32)[:half, :half]

    for i, group in enumerate(AR_GROUPS):
        for k, chunk in enumerate(group):
            pl.when(pl.program_id(0) == chunk % 3)(functools.partial(one_chunk, i, k, chunk))


def unpad(half, sides, halves):
    shape = jax.ShapeDtypeStruct((3, 2 * half, half), jnp.float32)
    vmem = pl.BlockSpec(memory_space=pltpu.VMEM)
    out = pl.BlockSpec((None, 2 * half, half), lambda gate: (gate, 0, 0))
    return pl.pallas_call(
        functools.partial(unpad_kernel, half),
        grid=(3,),
        in_specs=[pl.BlockSpec(memory_space=pltpu.SMEM)] + [vmem] * len(halves),
        out_specs=[out, out],
        out_shape=[shape, shape],
        compiler_params=pltpu.CompilerParams(vmem_limit_bytes=VMEM_LIMIT),
        cost_estimate=cost(8),
        name="unpad",
    )(sides, *halves)


def pair(index, own, oth):
    return jnp.where(index == 0, jnp.stack([own, oth]), jnp.stack([oth, own]))


def reduce_orders(devices):
    bits = devices.bit_length() - 1
    if devices != 1 << bits or bits < 3:
        return None
    rest = list(range(3, bits))
    along, across = [0, 1, 2, *rest], [1, 0, 2, *rest]
    return [along, across] * 3


def flip(values, bit):
    devices = lax.axis_size("dp")
    return lax.ppermute(values, "dp", [(i, i ^ (1 << bit)) for i in range(devices)])


def halve(values, bit):
    place = (lax.axis_index("dp") >> bit) & 1
    size = values.shape[0] // 2
    send = lax.dynamic_slice_in_dim(values, (1 - place) * size, size)
    keep = lax.dynamic_slice_in_dim(values, place * size, size)
    return send, keep


def add_low(left, right):
    return (left.astype(jnp.float32) + right.astype(jnp.float32)).astype(left.dtype)


def scatter_sum(chunks, orders, owner_sums):
    parts = list(chunks)
    for level in range(len(orders[0])):
        if level == 2:
            arrived = [value.came for value in owner_sums]
            parts = [after(part, arrived) for part in parts]
        sends = []
        for i, order in enumerate(orders):
            send, keep = halve(parts[i], order[level])
            parts[i] = add_low(keep, flip(send, order[level]))
            sends.append(send)
        if level != 1:
            for value in owner_sums:
                value.finish(sends)
                if value.order:
                    value.start()
    while owner_sums and owner_sums[0].order:
        for value in owner_sums:
            value.start()
            value.finish()
    return parts


def gather_sum(parts, orders, sent):
    device = lax.axis_index("dp")
    parts = [jnp.concatenate([parts[i] for i in group], axis=1) for group in AR_GROUPS]
    orders = [orders[group[0]] for group in AR_GROUPS]
    halves = []
    for level in reversed(range(len(orders[0]))):
        if level == 1:
            came_rows = exchange(after(sent, parts))
        for i, order in enumerate(orders):
            bit = (device >> order[level]) & 1
            came = flip(parts[i], order[level])
            if level == 0:
                halves += [parts[i], came]
            else:
                parts[i] = jnp.where(
                    bit == 0,
                    jnp.concatenate([parts[i], came]),
                    jnp.concatenate([came, parts[i]]),
                )
    return halves, came_rows


class OwnerSum:
    def __init__(self, values, order):
        bits = len(order)
        self.order = list(order)
        self.axes = list(reversed(range(bits)))
        self.values = values.reshape((2,) * bits + values.shape[1:])

    def start(self):
        bit = self.order.pop(0)
        axis = self.axes.index(bit)
        place = (lax.axis_index("dp") >> bit) & 1
        send = lax.dynamic_index_in_dim(self.values, 1 - place, axis, keepdims=False)
        self.keep = lax.dynamic_index_in_dim(self.values, place, axis, keepdims=False)
        self.axes.remove(bit)
        self.came = flip(send, bit)
        return send

    def finish(self, *others):
        self.values = add_low(self.keep, after(self.came, *others) if others else self.came)

    def join(self, other):
        self.values = jnp.concatenate([self.values, other.values], axis=-2)


def routed(items, targets, masks, plan, negatives, h_init, emb, w_in, w_rec, b_in, b_rec_n,
           out_table, out_bias, item_list, target_list, item_slot, target_slot, neg_capacity, over):
    f32, low = jnp.float32, jnp.bfloat16
    blocks, steps, all_slots = items.shape
    slots = all_slots // 2
    events = steps * slots
    batch = 2 * events
    half = h_init.shape[1]
    width = roundup(half + 6, 128)
    rows = emb.shape[0]
    devices = lax.axis_size("dp")
    device = lax.axis_index("dp")
    core = lax.axis_index("mp")
    me = core.astype(jnp.int32).reshape(1)
    first_half = (core == 0).astype(f32)
    capacity = item_list.shape[1]
    breadth = 2 * half
    spare = width - half

    def mine(values):
        return lax.dynamic_index_in_dim(values, core, 0, keepdims=False)

    def theirs(values):
        return lax.dynamic_index_in_dim(values, 1 - core, 0, keepdims=False)

    def core_major(values):
        return values.reshape(blocks, steps, 2, slots).transpose(2, 0, 1, 3)

    row_lanes = jnp.concatenate(
        [jnp.ones((rows, 3), f32), jnp.zeros((rows, spare - 3), f32)], axis=1
    )
    emb_wide = jnp.concatenate([emb, (row_lanes * first_half).astype(low)], axis=1)
    ids = device * rows + jnp.arange(rows)
    parts = bf16_parts(out_bias)
    out_lanes = jnp.stack(
        [*parts, (ids // 256).astype(f32), (ids % 256).astype(f32), jnp.ones((rows,), f32)]
        + [jnp.zeros((rows,), f32)] * (spare - 6),
        axis=1,
    )
    out_wide = jnp.concatenate([out_table, (out_lanes * first_half).astype(low)], axis=1)

    own_negatives = plan_negatives(negatives, devices, rows, neg_capacity, device)
    negative_pick = one_hot(own_negatives.reshape(blocks * neg_capacity), rows)
    neg_own = lax.all_gather(
        dot_f32(negative_pick, out_wide).astype(low), "dp", axis=0, tiled=True
    )
    alive = jnp.sum((masks > 0).astype(jnp.int32))
    told = jnp.broadcast_to(jnp.stack([alive, over])[None, :], (devices, 2))
    asking = jnp.concatenate([item_list, target_list, told], axis=1)
    asked = exchange(asking)
    wanted_rows = asked[:, : 2 * capacity]
    count = jnp.sum(asked[:, 2 * capacity]).astype(f32)
    overs = jnp.sum(asked[:, 2 * capacity + 1])
    item_pick = one_hot(wanted_rows[:, :capacity].reshape(devices * capacity), rows)
    target_pick = one_hot(wanted_rows[:, capacity:].reshape(devices * capacity), rows)
    item_send = dot_f32(item_pick, emb_wide).astype(low).reshape(devices, capacity, width)
    w_in, w_rec = after((w_in, w_rec), item_send)
    item_rows = exchange(item_send).reshape(devices * capacity, width)
    target_send = dot_f32(target_pick, out_wide).astype(low).reshape(devices, capacity, width)

    def widened(weight, bias, gate):
        matrix = weight[:, gate, :].reshape(2, half, half)
        matrix = jnp.pad(matrix, ((0, 0), (0, 0), (0, spare)))
        if bias is None:
            extra = jnp.zeros((2, spare, width), low)
        else:
            line = jnp.stack([*bf16_parts(bias)]).astype(low)
            extra = jnp.pad(line[None], ((0, 1), (0, spare - 3), (0, spare)))
        return jnp.concatenate([matrix, extra], axis=1)

    wi_own = jnp.stack([widened(w_in, b_in[gate], gate) for gate in range(3)])
    wr_own = jnp.stack([widened(w_rec, b_rec_n if gate == 2 else None, gate) for gate in range(3)])
    weights = (wi_own, swap_cores(wi_own), wr_own, swap_cores(wr_own))

    start_all = jnp.pad(h_init, ((0, 0), (0, spare))).reshape(2, slots, width)
    start_own = mine(start_all)
    start_oth = swap_cores(lax.dynamic_index_in_dim(start_all, 1 - core, 0, keepdims=False))
    state = pair(core, start_own, start_oth)

    codes_all = core_major(masks)
    codes = mine(codes_all).astype(f32)
    codes_wide = jnp.broadcast_to(codes[..., None], (blocks, steps, slots, 128))
    target_all = core_major(targets).reshape(2, blocks, events)
    want = jnp.broadcast_to(mine(target_all).astype(f32)[..., None], (blocks, events, 128))
    live = (codes_wide > 0.0).astype(f32).reshape(blocks, events, 128)
    use = (codes_all > 0).astype(f32).reshape(2, blocks, events).transpose(1, 0, 2)
    use = jnp.broadcast_to(use.reshape(blocks, 1, batch), (blocks, 8, batch))

    slots_first = item_slot.reshape(2, blocks * events)
    slots_first = jnp.concatenate([mine(slots_first), theirs(slots_first)])
    item_hot = one_hot(slots_first, devices * capacity)
    emb_own = dot_f32(item_hot, item_rows).astype(low)
    emb_oth = swap_cores(emb_own)
    emb_own = emb_own.reshape(2, blocks, events, width)
    emb_oth = emb_oth.reshape(2, blocks, events, width)
    inputs = jnp.concatenate(
        [
            emb_own.reshape(blocks * batch, width),
            jnp.concatenate([emb_oth[1], emb_oth[0]]).reshape(blocks * batch, width),
        ],
        axis=1,
    )

    hop = -(-slots // devices)
    saves = []
    outs = []
    entries = []
    routes = []
    squares = []
    lane_real = (jnp.arange(2 * width) % width < half).astype(f32)
    for block in range(blocks):
        result = run_forward(half, block, me, emb_own, emb_oth, codes_wide, state, weights)
        outs.append([value.reshape(events, width) for value in result[:2]])
        entries.append(result[2].reshape(events, 2 * width))
        saves.append(result[3:8])
        state = result[8]
        squares.append(result[9])
        if block + 1 < blocks:
            going = lax.dynamic_slice_in_dim(plan[block], core * slots, slots, 0)
            aim = going // all_slots
            place = going % all_slots
            order = jnp.arange(slots)
            earlier = (aim[:, None] == aim[None, :]) & (order[:, None] > order[None, :])
            position = aim * hop + jnp.sum(earlier.astype(jnp.int32), axis=1)
            lanes = jnp.arange(2 * width)[None, :]
            flat = state.transpose(1, 0, 2).reshape(slots, 2 * width)
            flat = jnp.where(lanes == half, place.astype(f32)[:, None], flat)
            flat = jnp.where(lanes == half + 1, 1.0, flat).astype(low)
            put = (jnp.arange(devices * hop)[:, None] == position[None, :]).astype(low)
            sent = dot_f32(put, flat).astype(low).reshape(devices, hop, 2 * width)
            came = exchange(sent).reshape(devices * hop, 2 * width)
            both = jnp.concatenate([came, swap_cores(came)], axis=0)
            label = jnp.where(both[:, half + 1] > 0.5, both[:, half].astype(f32), -1.0)
            here = (core * slots + order).astype(f32)
            take = (here[:, None] == label[None, :]).astype(low)
            moved = dot_f32(take, both) * lane_real
            state = moved.reshape(slots, 2, width).transpose(1, 0, 2)
            if block == 0:
                target_send = after(target_send, state)
                state = after(state, target_send)
                target_rows = exchange(target_send)
                target_rows = target_rows.reshape(devices * capacity, width)
                neg_own = after(neg_own, state)
            routes.append((label[: devices * hop], put))

    target_slot_blocks = target_slot.reshape(2, blocks, events).transpose(1, 0, 2)
    target_hot = one_hot(target_slot_blocks.reshape(blocks * batch), devices * capacity)
    neg_oth = swap_cores(neg_own)
    outs[-1] = after(outs[-1], neg_oth)
    outs[:-1] = after(outs[:-1], outs[-1])
    target_rows = after(target_rows, outs[-1])
    tgt_own = dot_f32(target_hot, target_rows).astype(low)
    tgt_oth = swap_cores(tgt_own).reshape(blocks, batch, width)
    neg_oth = neg_oth.reshape(devices, blocks, neg_capacity, width)
    neg_own = neg_own.reshape(devices, blocks, neg_capacity, width)
    tgt_own = tgt_own.reshape(blocks, batch, width)
    inv = (1.0 / count).reshape(1)
    from_scores = [None] * blocks
    orders = reduce_orders(devices)
    stats = []
    row_grads = [None] * blocks
    gate_own = [None] * blocks
    gate_oth = [None] * blocks
    emb_grads = [None] * blocks
    emb_grads_oth = [None] * blocks
    grad_state = jnp.zeros((2, slots, width), f32)
    grad_pairs = []
    for block in reversed(range(blocks)):
        grad_own, *from_scores[block], stat = run_scores(
            half, block, me, inv, *outs[block], want, live, use, tgt_own, tgt_oth, neg_own, neg_oth
        )
        stats.append(stat)
        grad_pairs.insert(0, (grad_own, swap_cores(grad_own), swap_cores(outs[block][1])))
    negative_grads = [None] * blocks

    for block in range(blocks):
        grad_own, grad_oth, outs_oth = grad_pairs[block]
        value = dot_first(grad_own, outs[block][0]) + dot_first(grad_oth, outs_oth)
        row_grads[block] = value.astype(low)
    negative_grads = jnp.stack(
        [value[batch:].reshape(devices, neg_capacity, width) for value in row_grads], axis=1
    )
    cut = roundup(neg_capacity // 2, 16)
    owner_sums = []
    if orders is not None:
        owner_sums = [
            OwnerSum(negative_grads[:, :, :cut], orders[0]),
            OwnerSum(negative_grads[:, :, cut:], orders[1]),
        ]
        from_scores[-1] = after(from_scores[-1], [value.start() for value in owner_sums])
    target_grads = jnp.concatenate([value[:batch] for value in row_grads], axis=0)
    target_send = dot_first(target_hot, target_grads).astype(low)
    target_came = exchange(target_send.reshape(devices, capacity, width))
    entering = jnp.concatenate(entries, axis=0)
    entering = jnp.concatenate([entering, swap_cores(entering)], axis=0)
    for block in reversed(range(blocks)):
        own, oth, emb_grads[block], emb_oth_grad, grad_state = run_backward(
            half,
            block,
            me,
            codes_wide,
            *[value.reshape(steps, slots, width) for value in from_scores[block]],
            saves[block],
            grad_state,
            weights,
        )
        gate_own[block] = own.reshape(4, events, width)
        gate_oth[block] = swap_cores(oth).reshape(4, events, width)
        emb_grads_oth[block] = swap_cores(emb_oth_grad)
        if block > 0:
            label, put = routes[block - 1]
            flat = grad_state.transpose(1, 0, 2).reshape(slots, 2 * width).astype(low)
            both = jnp.concatenate([flat, swap_cores(flat)], axis=0)
            order = jnp.arange(slots)
            names = jnp.concatenate([core * slots + order, (1 - core) * slots + order]).astype(f32)
            fetch = (label[:, None] == names[None, :]).astype(low)
            home = dot_f32(fetch, both).astype(low).reshape(devices, hop, 2 * width)
            back = exchange(home)
            flat = dot_first(put, back.reshape(devices * hop, 2 * width)) * lane_real
            grad_state = flat.reshape(slots, 2, width).transpose(1, 0, 2)
            if block == 1 and orders is not None:
                for value in owner_sums:
                    value.finish(home)
                grad_state = after(grad_state, [value.start() for value in owner_sums], target_send)

    gates = jnp.concatenate([*gate_own, *gate_oth], axis=1)
    gates = after(gates, target_came)
    chunks = [dot_first(entering, gates[gate]).astype(low) for gate in (0, 1, 2)]
    chunks += [dot_first(inputs, gates[gate]).astype(low) for gate in (0, 1, 3)]
    marker = chunks[-1]
    target_came = after(target_came, marker)
    own_stats = [
        sum(jnp.sum(value[0, :, 0]) for value in stats),
        sum(jnp.sum(value[0]) for value in squares),
        sum(jnp.sum(value[1]) for value in squares),
        sum(jnp.sum(value[1, :, 0]) for value in stats),
    ]
    own_stats = jnp.stack(bf16_parts(jnp.stack(own_stats)))
    own_stats = jnp.pad(own_stats, ((0, capacity - 3), (width - 4, 0)))

    def row_sums():
        item_grads = jnp.concatenate([*emb_grads, *emb_grads_oth], axis=0)
        item_sums = dot_first(item_hot, after(item_grads, marker))
        item_sums = item_sums.reshape(devices, capacity, width) + own_stats
        return item_sums.astype(low)

    if orders is None:
        item_came = exchange(row_sums())
        sums = [lax.psum(chunk, "dp") for chunk in chunks]
        sums = [jnp.concatenate([sums[i] for i in group], axis=1) for group in AR_GROUPS]
        halves = [value for chunk in sums for value in (chunk[:width], chunk[width:])]
        sides = [jnp.zeros((), jnp.int32)] * 6
        negative_sum = lax.psum_scatter(
            negative_grads, "dp", scatter_dimension=0, tiled=True
        ).reshape(blocks * neg_capacity, width)
    else:

        parts = scatter_sum(chunks, orders, owner_sums)
        first, second = [value.values for value in owner_sums]
        negative_sum = jnp.concatenate(
            [first.reshape(blocks, cut, width), second.reshape(blocks, neg_capacity - cut, width)],
            axis=1,
        ).reshape(blocks * neg_capacity, width)
        halves, item_came = gather_sum(parts, orders, row_sums())
        sides = [(device >> order[0]) & 1 for order in orders]
    all_stats = jnp.sum(item_came[:, :3, width - 4 :].astype(f32), axis=(0, 1))
    all_stats = all_stats + swap_cores(all_stats)
    sides = [side.astype(jnp.int32) for side in sides]
    sides = jnp.stack(sides[:3] + [side ^ core.astype(jnp.int32) for side in sides[3:]])

    def first_row(chunk):
        for i, group in enumerate(AR_GROUPS):
            if chunk in group:
                lanes = slice(group.index(chunk) * width, group.index(chunk) * width + half)
                kept, came = halves[2 * i][half, lanes], halves[2 * i + 1][half, lanes]
        return jnp.where(sides[chunk] == 0, kept, came).astype(f32)

    grad_b_in = jnp.stack([first_row(chunk) for chunk in (3, 4, 5)])
    grad_b_rec = first_row(2)
    grad_emb = dot_first(item_pick, item_came.reshape(devices * capacity, width))[:, :half]
    grad_out = dot_first(
        target_pick, target_came.reshape(devices * capacity, width)
    ) + dot_first(negative_pick, negative_sum)
    bias_own = grad_out[:, half]
    grad_out_bias = jnp.where(core == 0, bias_own, swap_cores(bias_own))

    def slots_of(values):
        own = mine(values)
        oth = swap_cores(theirs(values))
        return pair(core, own, oth).reshape(all_slots, width)[:, :half]

    columns = batch + negatives.shape[1]
    return overs, halves, sides, (
        all_stats[0] / count,
        jnp.sqrt(all_stats[1] / (count * breadth)),
        jnp.sqrt(all_stats[2] / (count * breadth)),
        jnp.sqrt(all_stats[3] / (count * columns)),
        slots_of(after(state, marker)),
        slots_of(after(grad_state, marker)),
        grad_emb,
        grad_b_in,
        grad_b_rec,
        grad_out[:, :half],
        grad_out_bias,
    )


def shards(items, targets, masks, plan, negatives, h_init, emb, w_in, w_rec, b_in, b_rec_n,
           out_table, out_bias):
    blocks, steps, all_slots = items.shape
    devices = lax.axis_size("dp")
    rows = emb.shape[0]
    requests = blocks * steps * all_slots
    capacity = max(32, roundup(-(-requests // devices), 16))
    mean = -(-negatives.shape[1] // devices)
    neg_capacity = min(roundup(mean + 4 * math.isqrt(mean), 16), roundup(rows, 16))

    def core_major(values):
        split = values.reshape(blocks, steps, 2, all_slots // 2)
        return split.transpose(2, 0, 1, 3).reshape(requests)

    item_rows, item_slot, item_most = plan_requests(core_major(items), devices, rows, capacity)
    target_rows, target_slot, target_most = plan_requests(
        core_major(targets), devices, rows, capacity
    )
    negative_most = most_negatives(negatives, devices, rows)
    over = (
        (item_most > capacity) | (target_most > capacity) | (negative_most > neg_capacity)
    ).astype(jnp.int32)
    given = (items, targets, masks, plan, negatives, h_init, emb, w_in, w_rec, b_in, b_rec_n,
             out_table, out_bias)
    overs, halves, sides, ready = routed(
        *given, item_rows, target_rows, item_slot, target_slot, neg_capacity, over
    )

    halves, sides, ready = lax.optimization_barrier((halves, sides, ready))

    def finish(halves, sides, ready):
        grad_w_rec, grad_w_in = unpad(h_init.shape[1], sides, halves)
        return (
            *ready[:7],
            grad_w_in.transpose(1, 0, 2),
            grad_w_rec.transpose(1, 0, 2),
            *ready[7:],
        )

    return lax.cond(overs == 0, finish, lambda *unused: general(*given), halves, sides, ready)


def solution(mesh):
    return jax.shard_map(
        shards,
        mesh=mesh,
        in_specs=(
            P(None, None, "dp"),
            P(None, None, "dp"),
            P(None, None, "dp"),
            P(None, "dp"),
            P(),
            P("dp", "mp"),
            P("dp", "mp"),
            P(None, None, "mp"),
            P(None, None, "mp"),
            P(None, "mp"),
            P("mp"),
            P("dp", "mp"),
            P("dp"),
        ),
        out_specs=(
            P(),
            P(),
            P(),
            P(),
            P("dp", "mp"),
            P("dp", "mp"),
            P("dp", "mp"),
            P(None, None, "mp"),
            P(None, None, "mp"),
            P(None, "mp"),
            P("mp"),
            P("dp", "mp"),
            P("dp"),
        ),
        check_vma=False,
    )
```
